32 devices in a mesh: ew: 8 (over z, x), ns: 4 (over y, core).
Axes of the slice: x: 2, y: 2, z: 4, core: 2. Of those that a mesh axis runs over, the one named last changes fastest.
Arguments:
- temp: float32 [32, 64, 1024], P(None, 'ns', 'ew'), may hold values from -6 to 6
- salt: float32 [32, 64, 1024], P(None, 'ns', 'ew'), may hold values from -6 to 6
- u_east: float32 [32, 64, 1024], P(None, 'ns', 'ew'), may hold values from -0.25 to 0.25
- v_north: float32 [32, 64, 1024], P(None, 'ns', 'ew'), may hold values from -0.25 to 0.25
- wet: int32 [32, 64, 1024], P(None, 'ns', 'ew'), may hold values 0 or 1
- cot_temp: float32 [32, 64, 1024], P(None, 'ns', 'ew'), may hold values from -6 to 6
- cot_salt: float32 [32, 64, 1024], P(None, 'ns', 'ew'), may hold values from -6 to 6
Outputs:
- temp_final: float32 [32, 64, 1024], P(None, 'ns', 'ew')
- salt_final: float32 [32, 64, 1024], P(None, 'ns', 'ew')
- grad_temp: float32 [32, 64, 1024], P(None, 'ns', 'ew')
- grad_salt: float32 [32, 64, 1024], P(None, 'ns', 'ew')
The draws below stay inside these ranges and needn't reach their ends.
All inputs are finite; a program needn't handle non-finite values. No bound on the sum of `wet` on one device may be relied on, other than what follows from the above.
Results may differ from the reference program's by a relative error of at most 0.00002.
Values sent between devices are 32-bit elements; how exact they have to be, the bound alone decides.
No kernel may reach another device: no remote copies, remote signals or barrier semaphores. Data moves between devices by JAX's collectives and lax.ppermute only.
A program may use at most 64 MiB of HBM per device.

```python
import jax
import jax.numpy as jnp
from jax import lax

LEVELS = 32
NY = 64
NX = 1024


def place_ends(entries, rng, least, top_value):
    longest = entries.shape.index(max(entries.shape))
    spots = []
    for shift in (0, 1):
        where = [jax.random.randint(jax.random.fold_in(rng, axis), (), 0, length) for axis, length in enumerate(entries.shape)]
        where[longest] = (where[longest] + shift) % entries.shape[longest]
        spots.append(tuple(where))
    return entries.at[spots[0]].set(least).at[spots[1]].set(top_value)


def shard_levels(own_key, dims, shards, low, largest):
    level = 1.0
    for position, blocks in shards:
        heights = jax.random.uniform(jax.random.fold_in(jax.random.fold_in(own_key, 6), position), (blocks,), jnp.float32, low / len(shards), largest / len(shards))
        level = level * jnp.repeat(jnp.exp(heights), dims[position] // blocks).reshape((-1,) + (1,) * (len(dims) - 1 - position))
    return level


def bell_draw(stream_key, extent, deviation, limit, pieces=(), kind=jnp.bfloat16):
    entries = deviation * jax.random.normal(stream_key, extent, jnp.float32)
    if pieces:
        entries = entries * shard_levels(stream_key, extent, pieces, -0.22, 0.18)
    return jnp.clip(entries, -limit, limit).astype(kind)


def setup_inputs(seed: int = 0) -> dict:
    keys = jax.random.split(jax.random.key(seed), 8)
    temp = bell_draw(keys[0], (LEVELS, NY, NX), 1.0, 6.0, ((1, 4), (2, 8)), jnp.float32)
    salt = bell_draw(keys[1], (LEVELS, NY, NX), 1.0, 6.0, ((1, 4), (2, 8)), jnp.float32)
    u_east = jnp.clip(jax.random.uniform(keys[2], (LEVELS, NY, NX), jnp.float32, -0.25, 0.25) * shard_levels(keys[2], (LEVELS, NY, NX), ((1, 4), (2, 8)), -0.4, 0.0), -0.25, 0.25)
    v_north = jnp.clip(jax.random.uniform(keys[3], (LEVELS, NY, NX), jnp.float32, -0.25, 0.25) * shard_levels(keys[3], (LEVELS, NY, NX), ((1, 4), (2, 8)), -0.4, 0.0), -0.25, 0.25)
    wet = place_ends((jax.random.randint(keys[4], (LEVELS, NY, NX), 0, 4) < 3).astype(jnp.int32), jax.random.fold_in(keys[4], 1), 0, 1)
    cot_temp = bell_draw(keys[5], (LEVELS, NY, NX), 1.0, 6.0, ((1, 4), (2, 8)), jnp.float32)
    cot_salt = bell_draw(keys[6], (LEVELS, NY, NX), 1.0, 6.0, ((1, 4), (2, 8)), jnp.float32)
    return dict(temp=temp, salt=salt, u_east=u_east, v_north=v_north, wet=wet, cot_temp=cot_temp, cot_salt=cot_salt)


horizontal_mix = 0.05
vertical_mix = 0.2

def window_of(array, start, stop, axis):
    return lax.slice_in_dim(array, start, array.shape[axis] + stop, 1, axis)

def coefficients(speed):
    magnitude = jnp.abs(speed)
    return ((-speed - magnitude) / 12.0, (7.0 * speed + 3.0 * magnitude) / 12.0 + horizontal_mix, (7.0 * speed - 3.0 * magnitude) / 12.0 - horizontal_mix, (-speed + magnitude) / 12.0)

def face_change(field, speed, wetness, axis):
    far_left = window_of(field, 0, -3, axis)
    left = window_of(field, 1, -2, axis)
    right = window_of(field, 2, -1, axis)
    far_right = window_of(field, 3, 0, axis)
    weights = coefficients(window_of(speed, 1, -2, axis))
    open_face = window_of(wetness, 1, -2, axis) * window_of(wetness, 2, -1, axis)
    flux = open_face * (weights[0] * far_left + weights[1] * left + weights[2] * right + weights[3] * far_right)
    return window_of(flux, 0, -1, axis) - window_of(flux, 1, 0, axis)

def vertical_change(field, wetness):
    open_face = wetness[:, :-1] * wetness[:, 1:]
    flux = vertical_mix * open_face * (field[:, :-1] - field[:, 1:])
    return jnp.pad(flux, ((0, 0), (1, 0), (0, 0), (0, 0))) - jnp.pad(flux, ((0, 0), (0, 1), (0, 0), (0, 0)))

def advance(padded, flow_wide):
    margin = (flow_wide.shape[2] - padded.shape[2]) // 2
    flow_wide = flow_wide[:, :, margin:flow_wide.shape[2] - margin, margin:flow_wide.shape[3] - margin]
    east_speed = flow_wide[0:1]
    north_speed = flow_wide[1:2]
    wetness = flow_wide[2:3]
    change_x = face_change(window_of(padded, 2, -2, 2), window_of(east_speed, 2, -2, 2), window_of(wetness, 2, -2, 2), 3)
    change_y = face_change(window_of(padded, 2, -2, 3), window_of(north_speed, 2, -2, 3), window_of(wetness, 2, -2, 3), 2)
    inner = window_of(window_of(padded, 2, -2, 2), 2, -2, 3)
    inner_wet = window_of(window_of(wetness, 2, -2, 2), 2, -2, 3)
    change_z = vertical_change(inner, inner_wet)
    return inner + inner_wet * (change_x + change_y + change_z)

def pad_grid(field, width):
    wrapped = jnp.concatenate([field[..., -width:], field, field[..., :width]], axis=-1)
    return jnp.pad(wrapped, ((0, 0), (0, 0), (width, width), (0, 0)))

def reference(temp, salt, u_east, v_north, wet, cot_temp, cot_salt):
    flow_wide = pad_grid(jnp.stack([u_east, v_north, wet.astype(jnp.float32)]), 2)

    def forward(state):
        for turn in range(2):
            state = advance(pad_grid(state, 2), flow_wide)
        return state
    results = []
    gradients = []
    for tracer, sensitivity in ((temp, cot_temp), (salt, cot_salt)):
        final, pullback = jax.vjp(forward, tracer[None])
        gradient, = pullback(sensitivity[None])
        results.append(final[0])
        gradients.append(gradient[0])
    return (results[0], results[1], gradients[0], gradients[1])
```

```python
import jax
import jax.numpy as jnp
from jax import lax
from jax.experimental import pallas as pl
from jax.experimental.pallas import tpu as pltpu
from jax.sharding import PartitionSpec as P

horizontal_mix = 0.05
vertical_mix = 0.2

F32 = jnp.float32
K = 32
R = 16
W = 128
HALO = 4
E = R + 2 * HALO
FIELDS = 7
U, V, M = 4, 5, 6
EDGE_BLOCKS = 4
SIDE_BLOCKS = 28
ROWS_AT = (0, 4, 8, 12, 24, 16, 20)
CORNERS_AT = 26
MIB = 1 << 20


def lanes():
    return lax.broadcasted_iota(jnp.int32, (K, W), 1)


def turn(x, amount):
    return pltpu.roll(x, amount % W, 1)


def row_of(ref, j):
    return ref[pl.ds(j, K, stride=R), :].astype(F32)


def pack_edges(*refs):
    fields, (east, west) = refs[:FIELDS], refs[FIELDS:]
    lane = lanes()
    for block in range(EDGE_BLOCKS):
        to_east = to_west = jnp.zeros((K, W), F32)
        for f in range(2 * block, min(2 * block + 2, FIELDS)):
            for r in range(R):
                start = 64 * (f % 2) + 4 * r
                turned = turn(row_of(fields[f], r), start + 4)
                group = lane // 4
                to_east = jnp.where(group == start // 4, turned, to_east)
                to_west = jnp.where(group == (start // 4 + 1) % (W // 4), turned, to_west)
        east[block] = to_east
        west[block] = to_west


def pack_sides(*refs):
    fields, (from_west, from_east, first, second) = refs[:FIELDS], refs[FIELDS:]
    odd = lax.axis_index("ns") % 2
    lane = lanes()
    for out, north in ((first, 1 - odd), (second, odd)):
        start = (R - HALO) * north
        for f in range(FIELDS):
            for r in range(2 if f == U else HALO):
                shift = 2 * north if f == U else 0
                out[ROWS_AT[f] + r] = row_of(fields[f], start + shift + r)
        left = right = jnp.zeros((K, W), F32)
        for f in range(FIELDS):
            amount = lax.rem(16 * f + 2 * W - 64 * (f % 2) - 4 * start, W)
            a = pltpu.roll(from_west[f // 2], amount, 1)
            b = pltpu.roll(from_east[f // 2], amount, 1)
            left = jnp.where((lane >= 16 * f) & (lane < 16 * f + 16), a, left)
            right = jnp.where((lane >= 16 * f + 4) & (lane < 16 * f + 20), b, right)
        out[CORNERS_AT] = left
        out[CORNERS_AT + 1] = right


def shifted(c, h, d, lane):
    if d > 0:
        return turn(jnp.where(lane < d, h, c), -d)
    return turn(jnp.where(lane >= W + d, h, c), -d)


def face_weights(speed, open_face):
    magnitude = jnp.abs(speed)
    forth = (-speed - magnitude) / 12.0
    back = (-speed + magnitude) / 12.0
    near = (7.0 * speed + 3.0 * magnitude) / 12.0 + horizontal_mix
    far = (7.0 * speed - 3.0 * magnitude) / 12.0 - horizontal_mix
    return forth * open_face, near * open_face, far * open_face, back * open_face


def compute(*refs):
    fields = refs[:FIELDS]
    from_west, from_east, first, second = refs[FIELDS : FIELDS + 4]
    outs = refs[FIELDS + 4 : FIELDS + 8]
    c_ref, h_ref, c1_ref, h1_ref, y_ref, yh_ref, x_ref, xh_ref = refs[FIELDS + 8 :]
    lane = lanes()
    place = lax.axis_index("ns")
    last = lax.axis_size("ns") - 1
    odd = place % 2

    def fill(r, carry):
        for f in range(FIELDS):
            c_ref[f, r + HALO] = row_of(fields[f], r)
            start = 64 * (f % 2) + 4 * r
            a = from_west[f // 2]
            b = from_east[f // 2]
            h = jnp.where((lane >= start) & (lane < start + 4), a, b)
            h_ref[f, r + HALO] = pltpu.roll(h, lax.rem(2 * W - 4 - start, W), 1)
        return carry

    lax.fori_loop(0, R, fill, 0)

    def halo(ref, base, keep, north):
        for f in range(FIELDS):
            rows = range(2) if f == U else range(HALO)
            for r in rows:
                at = base + r + (2 if f == U and not north else 0)
                c_ref[f, at] = jnp.where(keep, ref[ROWS_AT[f] + r], 0.0)
            for r in (range(0, 2) if north else range(2, 4)):
                start = 16 * f + 4 * r
                h = jnp.where(
                    (lane >= start) & (lane < start + 4), ref[CORNERS_AT], ref[CORNERS_AT + 1]
                )
                h_ref[f, base + r] = jnp.where(keep, turn(h, W - 4 - start), 0.0)

    @pl.when(odd == 0)
    def _():
        halo(first, HALO + R, place < last, True)
        halo(second, 0, place > 0, False)

    @pl.when(odd == 1)
    def _():
        halo(second, HALO + R, place < last, True)
        halo(first, 0, place > 0, False)

    def y_faces(source, target):
        def body(e, carry):
            speed = source[V, e]
            open_face = source[M, e] * source[M, e + 1]
            w = face_weights(speed, open_face)
            for k in range(4):
                target[k, e] = w[k]
            return carry

        return body

    lax.fori_loop(0, E - 1, y_faces(c_ref, y_ref), 0)
    lax.fori_loop(2, E - 3, y_faces(h_ref, yh_ref), 0)

    def x_coefficients(e, carry):
        m, mh = c_ref[M, e], h_ref[M, e]
        u, uh = c_ref[U, e], h_ref[U, e]
        w = face_weights(u, m * shifted(m, mh, 1, lane))
        wh = face_weights(uh, mh * shifted(mh, m, 1, lane))
        vertical = lax.broadcasted_iota(jnp.int32, (K, W), 0) < K - 1
        for own, other, mask, target, y in ((w, wh, m, x_ref, y_ref), (wh, w, mh, xh_ref, yh_ref)):
            back = [shifted(own[k], other[k], -1, lane) for k in range(4)]
            q0 = shifted(own[0], other[0], 1, lane)
            b2 = back[3] - own[2]
            up = jnp.where(vertical, vertical_mix * mask * pltpu.roll(mask, K - 1, 0), 0.0)
            down = pltpu.roll(up, 1, 0)
            w3back2 = shifted(own[3], other[3], -2, lane)
            target[0, e] = back[0]
            target[1, e] = back[1] - own[0]
            target[2, e] = b2
            target[3, e] = -own[3]
            target[4, e] = -w3back2
            target[5, e] = w3back2 - back[2]
            target[6, e] = own[1] - q0
            target[7, e] = q0
            target[8, e] = up
            target[9, e] = down
            target[10, e] = 1.0 + (back[2] - own[1]) - up - down + (y[2, e - 1] - y[1, e])
        return carry

    lax.fori_loop(2, E - 2, x_coefficients, 0)

    def stencil(source, h_source, x, y, e, forward, swap, fields_here):
        if forward:
            xs = [x[k, e] for k in (0, 1, 2, 3)]
            ys = [
                y[0, e - 1],
                y[1, e - 1] - y[0, e],
                y[3, e - 1] - y[2, e],
                -y[3, e],
            ]
        else:
            xs = [x[k, e] for k in (4, 5, 6, 7)]
            ys = [
                -y[3, e - 2],
                y[3, e - 2] - y[2, e - 1],
                y[1, e] - y[0, e + 1],
                y[0, e + 1],
            ]
        up, down, centre = x[8, e], x[9, e], x[10, e]
        results = []
        for f in fields_here:
            own, other = (h_source, source) if swap else (source, h_source)
            c, h = own[f, e], other[f, e]
            total = centre * c
            total += up * pltpu.roll(c, K - 1, 0) + down * pltpu.roll(c, 1, 0)
            for coefficient, d in zip(xs, (-2, -1, 1, 2)):
                total += coefficient * shifted(c, h, d, lane)
            for coefficient, d in zip(ys, (-2, -1, 1, 2)):
                total += coefficient * own[f, e + d]
            results.append(total)
        return results

    def first_step(e, carry):
        inside = ((place > 0) | (e >= HALO)) & ((place < last) | (e < HALO + R))
        for forward, here in ((True, (0, 1)), (False, (2, 3))):
            got = stencil(c_ref, h_ref, x_ref, y_ref, e, forward, False, here)
            for f, value in zip(here, got):
                c1_ref[f, e] = value if forward else jnp.where(inside, value, 0.0)
        return carry

    lax.fori_loop(2, E - 2, first_step, 0)

    def first_step_halo(e, carry):
        for forward, here in ((True, (0, 1)), (False, (2, 3))):
            got = stencil(c_ref, h_ref, xh_ref, yh_ref, e, forward, True, here)
            for f, value in zip(here, got):
                h1_ref[f, e] = value
        return carry

    lax.fori_loop(HALO, HALO + R, first_step_halo, 0)

    def second_step(e, carry):
        for forward, here in ((True, (0, 1)), (False, (2, 3))):
            got = stencil(c1_ref, h1_ref, x_ref, y_ref, e, forward, False, here)
            for f, value in zip(here, got):
                outs[f][pl.ds(e - HALO, K, stride=R), :] = value
        return carry

    lax.fori_loop(HALO, HALO + R, second_step, 0)


def vmem():
    return pl.BlockSpec(memory_space=pltpu.VMEM)


def call(kernel, n_in, out_shapes, scratch=(), limit=24 * MIB):
    return pl.pallas_call(
        kernel,
        out_shape=[jax.ShapeDtypeStruct(shape, F32) for shape in out_shapes],
        in_specs=[vmem()] * n_in,
        out_specs=[vmem()] * len(out_shapes),
        scratch_shapes=list(scratch),
        compiler_params=pltpu.CompilerParams(vmem_limit_bytes=limit),
    )


def local(temp, salt, u_east, v_north, wet, cot_temp, cot_salt):
    flat = [a.reshape(K * R, W) for a in (temp, salt, cot_temp, cot_salt, u_east, v_north, wet)]

    n = lax.axis_size("ew")
    edge = (EDGE_BLOCKS, K, W)
    to_east, to_west = call(pack_edges, FIELDS, [edge, edge])(*flat)
    from_west = lax.ppermute(to_east, "ew", [(i, (i + 1) % n) for i in range(n)])
    from_east = lax.ppermute(to_west, "ew", [((i + 1) % n, i) for i in range(n)])

    n = lax.axis_size("ns")
    side = (SIDE_BLOCKS, K, W)
    first, second = call(pack_sides, FIELDS + 2, [side, side])(*flat, from_west, from_east)

    def partners(odd):
        pairs = [(i, i + 1) for i in range(odd, n - 1, 2)]
        met = {i for pair in pairs for i in pair}
        return pairs + [(b, a) for a, b in pairs] + [(i, i) for i in range(n) if i not in met]

    second = lax.ppermute(second, "ns", partners(1))
    first = lax.ppermute(first, "ns", partners(0))

    outs = call(
        compute,
        FIELDS + 4,
        [(K * R, W)] * 4,
        [
            pltpu.VMEM((FIELDS, E, K, W), F32),
            pltpu.VMEM((FIELDS, E, K, W), F32),
            pltpu.VMEM((4, E, K, W), F32),
            pltpu.VMEM((4, E, K, W), F32),
            pltpu.VMEM((4, E, K, W), F32),
            pltpu.VMEM((4, E, K, W), F32),
            pltpu.VMEM((11, E, K, W), F32),
            pltpu.VMEM((11, E, K, W), F32),
        ],
        limit=40 * MIB,
    )(*flat, from_west, from_east, first, second)
    return tuple(a.reshape(K, R, W) for a in outs)


def solution(mesh):
    spec = P(None, "ns", "ew")
    return jax.shard_map(
        local, mesh=mesh, in_specs=(spec,) * 7, out_specs=(spec,) * 4, check_vma=False
    )
```

```python
import jax
import jax.numpy as jnp
from jax import lax
from jax.experimental import pallas as pl
from jax.experimental.pallas import tpu as pltpu
from jax.sharding import PartitionSpec as P

horizontal_mix = 0.05
vertical_mix = 0.2

F32 = jnp.float32
K = 32
R = 16
W = 128
G = W // R
HALO = 4
FIELDS = 7
U, V, M = 4, 5, 6
PAIRS = 4
SIDE_BLOCKS = 28
ROWS_AT = (0, 4, 8, 12, 24, 16, 20)
CORNERS_AT = 26
SOUTH, NORTH = 0, 1
MIB = 1 << 20


def lanes():
    return lax.broadcasted_iota(jnp.int32, (K, W), 1)


def turn(x, amount):
    return pltpu.roll(x, amount % W, 1)


def pack_edges(*refs):
    sources = refs[:FIELDS]
    rows, own, to_east, to_west, raw, raw_wet, arrived = refs[FIELDS:]
    copies = []
    for f in range(FIELDS):
        target = raw_wet if f == M else raw.at[f]
        copies.append(pltpu.make_async_copy(sources[f], target, arrived.at[f]))
        copies[-1].start()
    lane = lanes()
    group = lane // G
    packed = []
    for f in range(FIELDS):
        copies[f].wait()
        source = raw_wet if f == M else raw.at[f]
        edges = jnp.zeros((K, W), F32)
        for r in range(R):
            x = source[pl.ds(r, K, stride=R), :].astype(F32)
            rows[f, r] = x
            edges = jnp.where(group == r, turn(x, G * r + HALO), edges)
        own[f] = edges
        packed.append(edges)
    west_half = lane % G < HALO
    packed.append(jnp.zeros((K, W), F32))
    for p in range(PAIRS):
        a, b = packed[2 * p], packed[2 * p + 1]
        to_east[p] = jnp.where(west_half, a, turn(b, HALO))
        to_west[p] = jnp.where(west_half, turn(b, -HALO), a)


def pack_sides(rows, own, from_west, from_east, _, left, right, merged, first, second):
    odd = lax.axis_index("ns") % 2
    lane = lanes()
    column = lane % G
    west_half = column < HALO
    for f in range(FIELDS):
        a, b = from_west[f // 2], from_east[f // 2]
        if f % 2:
            a, b = turn(a, -HALO), turn(b, HALO)
        left_f = jnp.where(west_half, a, own[f])
        right_f = jnp.where(west_half, own[f], b)
        left[f] = left_f
        right[f] = right_f
        merged[f] = jnp.where(west_half, left_f, right_f)
    for out, north in ((first, 1 - odd), (second, odd)):
        for f in range(FIELDS):
            count = 2 if f == U else HALO
            start = (R - count) * north
            for r in range(count):
                out[ROWS_AT[f] + r] = rows[f, start + r]
        for side, edges in enumerate((left, right)):
            block = jnp.zeros((K, W), F32)
            for f in range(FIELDS):
                amount = lax.rem(2 * G * f + W - (W - 2 * G) * north, W)
                moved = pltpu.roll(edges[f], amount, 1)
                block = jnp.where(lane // (2 * G) == f, moved, block)
            out[CORNERS_AT + side] = block


def coefficients(speed, mask):
    opened = {d: mask[d] * mask[d + 1] for d in (-2, -1, 0, 1)}
    s = {d: speed[d] * opened[d] * (1.0 / 12.0) for d in opened}
    a = {d: jnp.abs(s[d]) for d in s}
    w0 = {d: -(s[d] + a[d]) for d in (-1, 0, 1)}
    w3 = {d: a[d] - s[d] for d in (-2, -1, 0)}
    w1, w2 = {}, {}
    for d in (-1, 0):
        even, odd = 7.0 * s[d], 3.0 * a[d] + horizontal_mix * opened[d]
        w1[d], w2[d] = even + odd, even - odd
    forward = [w0[-1], w1[-1] - w0[0], w3[-1] - w2[0], -w3[0]]
    transposed = [-w3[-2], w3[-2] - w2[-1], w1[0] - w0[1], w0[1]]
    return forward + transposed + [w2[-1] - w1[0]]


def shifted(c, h, d, lane, step=1):
    if d == 0:
        return c
    if d > 0:
        return turn(jnp.where(lane < step * d, h, c), -step * d)
    return turn(jnp.where(lane >= W + step * d, h, c), -step * d)


def x_coefficients(u, uh, m, mh, lane):
    return coefficients(
        {d: shifted(u, uh, d, lane) for d in (-2, -1, 0, 1)},
        {d: shifted(m, mh, d, lane) for d in (-2, -1, 0, 1, 2)},
    )


def vertical_coefficient(m):
    inner = lax.broadcasted_iota(jnp.int32, (K, W), 0) < K - 1
    return jnp.where(inner, vertical_mix * m * pltpu.roll(m, K - 1, 0), 0.0)


def step_row(cell, halo, x_of, y_of, vertical, store, lane):
    for direction in (0, 1):
        here = (2 * direction, 2 * direction + 1)
        halos, verticals = [], []
        for f in here:
            c = cell(f, 0)[...]
            flux = vertical * (c - pltpu.roll(c, K - 1, 0))
            verticals.append(pltpu.roll(flux, 1, 0) - flux)
            halos.append(halo(f))
        for q in range(0, K, 8):
            part = pl.ds(q, 8)
            lane_q = lane[:8]
            xs = [x_of.at[4 * direction + k][part] for k in range(4)]
            ys = [y_of.at[4 * direction + k][part] for k in range(4)]
            centre = 1.0 + x_of.at[8][part] + y_of.at[8][part]
            for f, h, z in zip(here, halos, verticals):
                c = cell(f, 0)[part]
                total = centre * c + z[q : q + 8]
                for coefficient, d in zip(xs, (-2, -1, 1, 2)):
                    total += coefficient * shifted(c, h[q : q + 8], d, lane_q)
                for coefficient, d in zip(ys, (-2, -1, 1, 2)):
                    total += coefficient * cell(f, d)[part]
                store(f, part, total)


def halo_columns(merged, j):
    return pltpu.roll(merged, lax.rem(2 * W - HALO - G * j, W), 1)


def edge_step(left, right, left_rows, right_rows, store):
    lane = lanes()
    column = lane % G
    west_half = column < HALO
    sides = []
    for side, rows in ((left, left_rows), (right, right_rows)):
        u, v, m = side[U], side[V], side[M]
        xs = coefficients(
            {d: turn(u, -d) for d in (-2, -1, 0, 1)},
            {d: turn(m, -d) for d in (-2, -1, 0, 1, 2)},
        )
        vh, mh = rows(V), rows(M)
        ys = coefficients(
            {d: shifted(v, vh, d, lane, G) for d in (-2, -1, 0, 1)},
            {d: shifted(m, mh, d, lane, G) for d in (-2, -1, 0, 1, 2)},
        )
        centre = 1.0 + xs[8] + ys[8]
        vertical = vertical_coefficient(m)
        results = []
        for f in range(4):
            c, ch = side[f], rows(f)
            at = 4 * (f // 2)
            flux = vertical * (c - pltpu.roll(c, K - 1, 0))
            total = centre * c + (pltpu.roll(flux, 1, 0) - flux)
            for coefficient, d in zip(xs[at : at + 4], (-2, -1, 1, 2)):
                total += coefficient * turn(c, -d)
            for coefficient, d in zip(ys[at : at + 4], (-2, -1, 1, 2)):
                total += coefficient * shifted(c, ch, d, lane, G)
            results.append(total)
        sides.append(results)
    for f in range(4):
        store(f, jnp.where(west_half, sides[0][f], sides[1][f]))


def y_coefficients_at(row, j):
    return coefficients(
        {d: row(V, j + d)[...] for d in (-2, -1, 0, 1)},
        {d: row(M, j + d)[...] for d in (-2, -1, 0, 1, 2)},
    )


def prepare(rows, y_out, vertical_out):
    def body(j, carry):
        got = y_coefficients_at(lambda f, r: rows.at[f, r], j)
        for k in range(9):
            y_out[j - 2, k] = got[k]
        return carry

    lax.fori_loop(2, R - 2, body, 0)

    def levels(j, carry):
        vertical_out[j] = vertical_coefficient(rows[M, j])
        return carry

    lax.fori_loop(0, R, levels, 0)


def interior(rows, left, right, merged, y_in, vertical_in, x_out, c1_out, c2_out, merged1):
    lane = lanes()

    def x_body(j, carry):
        got = x_coefficients(
            rows[U, j], halo_columns(merged[U], j), rows[M, j], halo_columns(merged[M], j), lane
        )
        for k in range(9):
            x_out[j, k] = got[k]
        return carry

    lax.fori_loop(0, R, x_body, 0)

    def keep(f, value):
        merged1[f] = value

    edge_step(left, right, lambda f: left[f], lambda f: right[f], keep)

    def first(j, carry):
        def store(f, part, value):
            c1_out.at[f, j - 2][part] = value

        step_row(
            lambda f, d: rows.at[f, j + d],
            lambda f: halo_columns(merged[f], j),
            x_out.at[j],
            y_in.at[j - 2],
            vertical_in[j],
            store,
            lane,
        )
        return carry

    lax.fori_loop(2, R - 2, first, 0)

    def second(j, carry):
        def store(f, part, value):
            c2_out.at[f, j - 4][part] = value

        step_row(
            lambda f, d: c1_out.at[f, j - 2 + d],
            lambda f: halo_columns(merged1[f], j),
            x_out.at[j],
            y_in.at[j - 2],
            vertical_in[j],
            store,
            lane,
        )
        return carry

    lax.fori_loop(4, R - 4, second, 0)


def boundary(*refs):
    rows, left, right, merged, y_in, vertical_in, x_in, c1_in, c2_in, first, second = refs[:11]
    outs = refs[11:15]
    sides, x_new, y_new, vertical_new, c1_new, merged1, rows_halo = refs[15:]
    lane = lanes()
    place = lax.axis_index("ns")
    last = lax.axis_size("ns") - 1
    odd = place % 2
    there = (place > 0, place < last)

    def unpack(b, carry):
        for source, side in ((first, 1 - odd), (second, odd)):
            here = jnp.where(side == NORTH, place < last, place > 0)
            sides[side, b] = jnp.where(here, source[b], 0.0)
        return carry

    lax.fori_loop(0, SIDE_BLOCKS, unpack, 0)

    def row(f, j):
        if j < 0:
            return sides.at[SOUTH, ROWS_AT[f] + j + (2 if f == U else HALO)]
        if j >= R:
            return sides.at[NORTH, ROWS_AT[f] + j - R]
        return rows.at[f, j]

    for s in range(2):
        for f in range(FIELDS):
            south = turn(sides[SOUTH, CORNERS_AT + s], W - 2 * G - 2 * G * f)
            north = turn(sides[NORTH, CORNERS_AT + s], -2 * G * f)
            rows_halo[s, f] = jnp.where(lane >= W // 2, south, north)

    def keep(f, value):
        merged1[f] = value

    edge_step(
        left, right, lambda f: rows_halo[0, f], lambda f: rows_halo[1, f], keep
    )

    west_half = lane % G < HALO

    def halo(f, j):
        if 0 <= j < R:
            return halo_columns(merged[f], j)
        corner = jnp.where(west_half, rows_halo[0, f], rows_halo[1, f])
        return halo_columns(corner, j % R)

    edge_rows = (-2, -1, 0, 1, R - 2, R - 1, R, R + 1)
    new_at = {j: i for i, j in enumerate(edge_rows)}
    for j in edge_rows:
        got = y_coefficients_at(row, j)
        for k in range(9):
            y_new[new_at[j], k] = got[k]
        if not 0 <= j < R:
            got = x_coefficients(row(U, j)[...], halo(U, j), row(M, j)[...], halo(M, j), lane)
            for k in range(9):
                x_new[new_at[j], k] = got[k]
            vertical_new[new_at[j]] = vertical_coefficient(row(M, j)[...])

    def x_of(j):
        return x_in.at[j] if 0 <= j < R else x_new.at[new_at[j]]

    def y_of(j):
        return y_new.at[new_at[j]] if j in new_at else y_in.at[j - 2]

    def vertical_of(j):
        return vertical_in[j] if 0 <= j < R else vertical_new[new_at[j]]

    for j in edge_rows:
        def store(f, part, value, j=j):
            if f >= 2 and not 0 <= j < R:
                value = jnp.where(there[0 if j < 0 else 1], value, 0.0)
            c1_new.at[f, new_at[j]][part] = value

        step_row(
            lambda f, d: row(f, j + d),
            lambda f: halo(f, j),
            x_of(j),
            y_of(j),
            vertical_of(j),
            store,
            lane,
        )

    def row1(f, j):
        return c1_new.at[f, new_at[j]] if j in new_at else c1_in.at[f, j - 2]

    for j in (0, 1, 2, 3, R - 4, R - 3, R - 2, R - 1):
        def store(f, part, value, j=j):
            outs[f][pl.ds(part.start * R + j, 8, stride=R), :] = value

        step_row(
            lambda f, d: row1(f, j + d),
            lambda f: halo_columns(merged1[f], j),
            x_of(j),
            y_of(j),
            vertical_of(j),
            store,
            lane,
        )

    def copy(j, carry):
        for f in range(4):
            outs[f][pl.ds(j, K, stride=R), :] = c2_in[f, j - 4]
        return carry

    lax.fori_loop(4, R - 4, copy, 0)


def vmem():
    return pl.BlockSpec(memory_space=pltpu.VMEM)


def call(kernel, in_specs, out_shapes, scratch=(), limit=16 * MIB, cost=0):
    return pl.pallas_call(
        kernel,
        out_shape=[jax.ShapeDtypeStruct(shape, F32) for shape in out_shapes],
        in_specs=in_specs,
        out_specs=[vmem()] * len(out_shapes),
        scratch_shapes=list(scratch),
        compiler_params=pltpu.CompilerParams(vmem_limit_bytes=limit),
        cost_estimate=pl.CostEstimate(flops=cost, bytes_accessed=MIB, transcendentals=0),
    )


def local(temp, salt, u_east, v_north, wet, cot_temp, cot_salt):
    flat = [a.reshape(K * R, W) for a in (temp, salt, cot_temp, cot_salt, u_east, v_north, wet)]

    rows, own, to_east, to_west = call(
        pack_edges,
        [pl.BlockSpec(memory_space=pltpu.HBM)] * FIELDS,
        [(FIELDS, R, K, W), (FIELDS, K, W), (PAIRS, K, W), (PAIRS, K, W)],
        [
            pltpu.VMEM((FIELDS - 1, K * R, W), F32),
            pltpu.VMEM((K * R, W), jnp.int32),
            pltpu.SemaphoreType.DMA((FIELDS,)),
        ],
    )(*[pltpu.with_memory_space_constraint(a, pltpu.HBM) for a in flat])

    n = lax.axis_size("ew")
    from_west = lax.ppermute(to_east, "ew", [(i, (i + 1) % n) for i in range(n)])
    from_east = lax.ppermute(to_west, "ew", [((i + 1) % n, i) for i in range(n)])

    y_in, vertical = call(
        prepare, [vmem()], [(R - 4, 9, K, W), (R, K, W)], cost=10_000_000
    )(rows)

    left, right, merged, first, second = call(
        pack_sides,
        [vmem()] * 4 + [pl.BlockSpec(memory_space=pl.ANY)],
        [(FIELDS, K, W)] * 3 + [(SIDE_BLOCKS, K, W)] * 2,
    )(rows, own, from_west, from_east, vertical)

    n = lax.axis_size("ns")

    def partners(odd):
        pairs = [(i, i + 1) for i in range(odd, n - 1, 2)]
        met = {i for pair in pairs for i in pair}
        return pairs + [(b, a) for a, b in pairs] + [(i, i) for i in range(n) if i not in met]

    second = lax.ppermute(second, "ns", partners(1))
    first = lax.ppermute(first, "ns", partners(0))

    x_in, c1, c2 = call(
        interior,
        [vmem()] * 6,
        [(R, 9, K, W), (4, R - 4, K, W), (4, R - 8, K, W)],
        [pltpu.VMEM((4, K, W), F32)],
        cost=10_000_000,
    )(rows, left, right, merged, y_in, vertical)

    outs = call(
        boundary,
        [vmem()] * 11,
        [(K * R, W)] * 4,
        [
            pltpu.VMEM((2, SIDE_BLOCKS, K, W), F32),
            pltpu.VMEM((8, 9, K, W), F32),
            pltpu.VMEM((8, 9, K, W), F32),
            pltpu.VMEM((8, K, W), F32),
            pltpu.VMEM((4, 8, K, W), F32),
            pltpu.VMEM((4, K, W), F32),
            pltpu.VMEM((2, FIELDS, K, W), F32),
        ],
        cost=10_000_000,
    )(rows, left, right, merged, y_in, vertical, x_in, c1, c2, first, second)
    return tuple(a.reshape(K, R, W) for a in outs)


def solution(mesh):
    spec = P(None, "ns", "ew")
    return jax.shard_map(
        local, mesh=mesh, in_specs=(spec,) * 7, out_specs=(spec,) * 4, check_vma=False
    )
```

```python
import jax
import jax.numpy as jnp
from jax import lax
from jax.experimental import pallas as pl
from jax.experimental.pallas import tpu as pltpu
from jax.sharding import PartitionSpec as P

horizontal_mix = 0.05
vertical_mix = 0.2

F32 = jnp.float32
K = 32
R = 16
W = 128
G = W // R
HALO = 4
FIELDS = 7
U, V, M = 4, 5, 6
PAIRS = 4
SIDE_BLOCKS = 28
ROWS_AT = (0, 4, 8, 12, 24, 16, 20)
CORNERS_AT = 26
SOUTH, NORTH = 0, 1
MIB = 1 << 20


def lanes():
    return lax.broadcasted_iota(jnp.int32, (K, W), 1)


def turn(x, amount):
    return pltpu.roll(x, amount % W, 1)


def pack_edges(*refs):
    sources = refs[:FIELDS]
    rows, own, to_east, to_west, raw, raw_wet, arrived = refs[FIELDS:]
    copies = []
    for f in range(FIELDS):
        target = raw_wet if f == M else raw.at[f]
        copies.append(pltpu.make_async_copy(sources[f], target, arrived.at[f]))
        copies[-1].start()
    lane = lanes()
    group = lane // G
    packed = []
    for f in range(FIELDS):
        copies[f].wait()
        source = raw_wet if f == M else raw.at[f]
        edges = jnp.zeros((K, W), F32)
        for r in range(R):
            x = source[pl.ds(r, K, stride=R), :].astype(F32)
            rows[f, r] = x
            edges = jnp.where(group == r, turn(x, G * r + HALO), edges)
        own[f] = edges
        packed.append(edges)
    west_half = lane % G < HALO
    packed.append(jnp.zeros((K, W), F32))
    for p in range(PAIRS):
        a, b = packed[2 * p], packed[2 * p + 1]
        to_east[p] = jnp.where(west_half, a, turn(b, HALO))
        to_west[p] = jnp.where(west_half, turn(b, -HALO), a)


def pack_sides(rows, own, from_west, from_east, _, left, right, merged, first, second):
    odd = lax.axis_index("ns") % 2
    lane = lanes()
    column = lane % G
    west_half = column < HALO
    for f in range(FIELDS):
        a, b = from_west[f // 2], from_east[f // 2]
        if f % 2:
            a, b = turn(a, -HALO), turn(b, HALO)
        left_f = jnp.where(west_half, a, own[f])
        right_f = jnp.where(west_half, own[f], b)
        left[f] = left_f
        right[f] = right_f
        merged[f] = jnp.where(west_half, left_f, right_f)
    for out, north in ((first, 1 - odd), (second, odd)):
        for f in range(FIELDS):
            count = 2 if f == U else HALO
            start = (R - count) * north
            for r in range(count):
                out[ROWS_AT[f] + r] = rows[f, start + r]
        for side, edges in enumerate((left, right)):
            block = jnp.zeros((K, W), F32)
            for f in range(FIELDS):
                amount = lax.rem(2 * G * f + W - (W - 2 * G) * north, W)
                moved = pltpu.roll(edges[f], amount, 1)
                block = jnp.where(lane // (2 * G) == f, moved, block)
            out[CORNERS_AT + side] = block


def coefficients(speed, mask):
    opened = {d: mask[d] * mask[d + 1] for d in (-2, -1, 0, 1)}
    s = {d: speed[d] * opened[d] * (1.0 / 12.0) for d in opened}
    a = {d: jnp.abs(s[d]) for d in s}
    w0 = {d: -(s[d] + a[d]) for d in (-1, 0, 1)}
    w3 = {d: a[d] - s[d] for d in (-2, -1, 0)}
    w1, w2 = {}, {}
    for d in (-1, 0):
        even, odd = 7.0 * s[d], 3.0 * a[d] + horizontal_mix * opened[d]
        w1[d], w2[d] = even + odd, even - odd
    forward = [w0[-1], w1[-1] - w0[0], w3[-1] - w2[0], -w3[0]]
    transposed = [-w3[-2], w3[-2] - w2[-1], w1[0] - w0[1], w0[1]]
    return forward + transposed + [w2[-1] - w1[0]]


def shifted(c, h, d, lane, step=1):
    if d == 0:
        return c
    if d > 0:
        return turn(jnp.where(lane < step * d, h, c), -step * d)
    return turn(jnp.where(lane >= W + step * d, h, c), -step * d)


def x_coefficients(u, uh, m, mh, lane):
    return coefficients(
        {d: shifted(u, uh, d, lane) for d in (-2, -1, 0, 1)},
        {d: shifted(m, mh, d, lane) for d in (-2, -1, 0, 1, 2)},
    )


def vertical_coefficient(m):
    inner = lax.broadcasted_iota(jnp.int32, (K, W), 0) < K - 1
    return jnp.where(inner, vertical_mix * m * pltpu.roll(m, K - 1, 0), 0.0)


def step_row(cell, halo, x_of, y_of, vertical, store, lane):
    results = []
    for direction in (0, 1):
        here = (2 * direction, 2 * direction + 1)
        halos, verticals = [], []
        for f in here:
            c = cell(f, 0)[...]
            flux = vertical * (c - pltpu.roll(c, K - 1, 0))
            verticals.append(pltpu.roll(flux, 1, 0) - flux)
            halos.append(halo(f))
        for q in range(0, K, 8):
            part = pl.ds(q, 8)
            lane_q = lane[:8]
            xs = [x_of.at[4 * direction + k][part] for k in range(4)]
            ys = [y_of.at[4 * direction + k][part] for k in range(4)]
            centre = 1.0 + x_of.at[8][part] + y_of.at[8][part]
            for f, h, z in zip(here, halos, verticals):
                c = cell(f, 0)[part]
                total = centre * c + z[q : q + 8]
                for coefficient, d in zip(xs, (-2, -1, 1, 2)):
                    total += coefficient * shifted(c, h[q : q + 8], d, lane_q)
                for coefficient, d in zip(ys, (-2, -1, 1, 2)):
                    total += coefficient * cell(f, d)[part]
                results.append((f, part, total))
    for result in results:
        store(*result)


def halo_columns(merged, j):
    return pltpu.roll(merged, lax.rem(2 * W - HALO - G * j, W), 1)


def edge_step(left, right, left_rows, right_rows, store):
    lane = lanes()
    column = lane % G
    west_half = column < HALO
    sides = []
    for side, rows in ((left, left_rows), (right, right_rows)):
        u, v, m = side[U], side[V], side[M]
        xs = coefficients(
            {d: turn(u, -d) for d in (-2, -1, 0, 1)},
            {d: turn(m, -d) for d in (-2, -1, 0, 1, 2)},
        )
        vh, mh = rows(V), rows(M)
        ys = coefficients(
            {d: shifted(v, vh, d, lane, G) for d in (-2, -1, 0, 1)},
            {d: shifted(m, mh, d, lane, G) for d in (-2, -1, 0, 1, 2)},
        )
        centre = 1.0 + xs[8] + ys[8]
        vertical = vertical_coefficient(m)
        results = []
        for f in range(4):
            c, ch = side[f], rows(f)
            at = 4 * (f // 2)
            flux = vertical * (c - pltpu.roll(c, K - 1, 0))
            total = centre * c + (pltpu.roll(flux, 1, 0) - flux)
            for coefficient, d in zip(xs[at : at + 4], (-2, -1, 1, 2)):
                total += coefficient * turn(c, -d)
            for coefficient, d in zip(ys[at : at + 4], (-2, -1, 1, 2)):
                total += coefficient * shifted(c, ch, d, lane, G)
            results.append(total)
        sides.append(results)
    for f in range(4):
        store(f, jnp.where(west_half, sides[0][f], sides[1][f]))


def y_coefficients_at(row, j):
    return coefficients(
        {d: row(V, j + d)[...] for d in (-2, -1, 0, 1)},
        {d: row(M, j + d)[...] for d in (-2, -1, 0, 1, 2)},
    )


def prepare(rows, y_out, vertical_out):
    def body(j, carry):
        got = y_coefficients_at(lambda f, r: rows.at[f, r], j)
        for k in range(9):
            y_out[j - 2, k] = got[k]
        return carry

    lax.fori_loop(2, R - 2, body, 0)

    def levels(j, carry):
        vertical_out[j] = vertical_coefficient(rows[M, j])
        return carry

    lax.fori_loop(0, R, levels, 0)


def interior(rows, left, right, merged, y_in, vertical_in, x_out, c1_out, c2_out, merged1):
    lane = lanes()

    def x_body(j, carry):
        got = x_coefficients(
            rows[U, j], halo_columns(merged[U], j), rows[M, j], halo_columns(merged[M], j), lane
        )
        for k in range(9):
            x_out[j, k] = got[k]
        return carry

    lax.fori_loop(0, R, x_body, 0)

    def keep(f, value):
        merged1[f] = value

    edge_step(left, right, lambda f: left[f], lambda f: right[f], keep)

    def first(j, carry):
        def store(f, part, value):
            c1_out.at[f, j - 2][part] = value

        step_row(
            lambda f, d: rows.at[f, j + d],
            lambda f: halo_columns(merged[f], j),
            x_out.at[j],
            y_in.at[j - 2],
            vertical_in[j],
            store,
            lane,
        )
        return carry

    lax.fori_loop(2, R - 2, first, 0)

    def second(j, carry):
        def store(f, part, value):
            c2_out.at[f, j - 4][part] = value

        step_row(
            lambda f, d: c1_out.at[f, j - 2 + d],
            lambda f: halo_columns(merged1[f], j),
            x_out.at[j],
            y_in.at[j - 2],
            vertical_in[j],
            store,
            lane,
        )
        return carry

    lax.fori_loop(4, R - 4, second, 0)


def boundary(*refs):
    rows, left, right, merged, y_in, vertical_in, x_in, c1_in, c2_in, second, first = refs[:11]
    outs = refs[11:15]
    sides, x_new, y_new, vertical_new, c1_new, merged1, rows_halo = refs[15:]
    lane = lanes()
    place = lax.axis_index("ns")
    last = lax.axis_size("ns") - 1
    odd = place % 2
    there = (place > 0, place < last)

    def unpack(b, carry):
        for source, side in ((first, 1 - odd), (second, odd)):
            here = jnp.where(side == NORTH, place < last, place > 0)
            sides[side, b] = jnp.where(here, source[b], 0.0)
        return carry

    lax.fori_loop(0, SIDE_BLOCKS, unpack, 0)

    def row(f, j):
        if j < 0:
            return sides.at[SOUTH, ROWS_AT[f] + j + (2 if f == U else HALO)]
        if j >= R:
            return sides.at[NORTH, ROWS_AT[f] + j - R]
        return rows.at[f, j]

    for s in range(2):
        for f in range(FIELDS):
            south = turn(sides[SOUTH, CORNERS_AT + s], W - 2 * G - 2 * G * f)
            north = turn(sides[NORTH, CORNERS_AT + s], -2 * G * f)
            rows_halo[s, f] = jnp.where(lane >= W // 2, south, north)

    def keep(f, value):
        merged1[f] = value

    edge_step(
        left, right, lambda f: rows_halo[0, f], lambda f: rows_halo[1, f], keep
    )

    west_half = lane % G < HALO

    def halo(f, j):
        if 0 <= j < R:
            return halo_columns(merged[f], j)
        corner = jnp.where(west_half, rows_halo[0, f], rows_halo[1, f])
        return halo_columns(corner, j % R)

    edge_rows = (-2, -1, 0, 1, R - 2, R - 1, R, R + 1)
    new_at = {j: i for i, j in enumerate(edge_rows)}
    for j in edge_rows:
        got = y_coefficients_at(row, j)
        for k in range(9):
            y_new[new_at[j], k] = got[k]
        if not 0 <= j < R:
            got = x_coefficients(row(U, j)[...], halo(U, j), row(M, j)[...], halo(M, j), lane)
            for k in range(9):
                x_new[new_at[j], k] = got[k]
            vertical_new[new_at[j]] = vertical_coefficient(row(M, j)[...])

    def x_of(j):
        return x_in.at[j] if 0 <= j < R else x_new.at[new_at[j]]

    def y_of(j):
        return y_new.at[new_at[j]] if j in new_at else y_in.at[j - 2]

    def vertical_of(j):
        return vertical_in[j] if 0 <= j < R else vertical_new[new_at[j]]

    for j in edge_rows:
        def store(f, part, value, j=j):
            if f >= 2 and not 0 <= j < R:
                value = jnp.where(there[0 if j < 0 else 1], value, 0.0)
            c1_new.at[f, new_at[j]][part] = value

        step_row(
            lambda f, d: row(f, j + d),
            lambda f: halo(f, j),
            x_of(j),
            y_of(j),
            vertical_of(j),
            store,
            lane,
        )

    def row1(f, j):
        return c1_new.at[f, new_at[j]] if j in new_at else c1_in.at[f, j - 2]

    for j in (0, 1, 2, 3, R - 4, R - 3, R - 2, R - 1):
        def store(f, part, value, j=j):
            outs[f][pl.ds(part.start * R + j, 8, stride=R), :] = value

        step_row(
            lambda f, d: row1(f, j + d),
            lambda f: halo_columns(merged1[f], j),
            x_of(j),
            y_of(j),
            vertical_of(j),
            store,
            lane,
        )

    def copy(j, carry):
        for f in range(4):
            outs[f][pl.ds(j, K, stride=R), :] = c2_in[f, j - 4]
        return carry

    lax.fori_loop(4, R - 4, copy, 0)


def vmem():
    return pl.BlockSpec(memory_space=pltpu.VMEM)


def call(kernel, in_specs, out_shapes, scratch=(), limit=16 * MIB, cost=0):
    return pl.pallas_call(
        kernel,
        out_shape=[jax.ShapeDtypeStruct(shape, F32) for shape in out_shapes],
        in_specs=in_specs,
        out_specs=[vmem()] * len(out_shapes),
        scratch_shapes=list(scratch),
        compiler_params=pltpu.CompilerParams(vmem_limit_bytes=limit),
        cost_estimate=pl.CostEstimate(flops=cost, bytes_accessed=MIB, transcendentals=0),
    )


def local(temp, salt, u_east, v_north, wet, cot_temp, cot_salt):
    flat = [a.reshape(K * R, W) for a in (temp, salt, cot_temp, cot_salt, u_east, v_north, wet)]

    rows, own, to_east, to_west = call(
        pack_edges,
        [pl.BlockSpec(memory_space=pltpu.HBM)] * FIELDS,
        [(FIELDS, R, K, W), (FIELDS, K, W), (PAIRS, K, W), (PAIRS, K, W)],
        [
            pltpu.VMEM((FIELDS - 1, K * R, W), F32),
            pltpu.VMEM((K * R, W), jnp.int32),
            pltpu.SemaphoreType.DMA((FIELDS,)),
        ],
    )(*[pltpu.with_memory_space_constraint(a, pltpu.HBM) for a in flat])

    n = lax.axis_size("ew")
    from_west = lax.ppermute(to_east, "ew", [(i, (i + 1) % n) for i in range(n)])
    from_east = lax.ppermute(to_west, "ew", [((i + 1) % n, i) for i in range(n)])

    y_in, vertical = call(
        prepare, [vmem()], [(R - 4, 9, K, W), (R, K, W)], cost=10_000_000
    )(rows)

    left, right, merged, first, second = call(
        pack_sides,
        [vmem()] * 4 + [pl.BlockSpec(memory_space=pl.ANY)],
        [(FIELDS, K, W)] * 3 + [(SIDE_BLOCKS, K, W)] * 2,
    )(rows, own, from_west, from_east, vertical)

    n = lax.axis_size("ns")

    def partners(odd):
        pairs = [(i, i + 1) for i in range(odd, n - 1, 2)]
        met = {i for pair in pairs for i in pair}
        return pairs + [(b, a) for a, b in pairs] + [(i, i) for i in range(n) if i not in met]

    second = lax.ppermute(second, "ns", partners(1))
    first = lax.ppermute(first, "ns", partners(0))

    x_in, c1, c2 = call(
        interior,
        [vmem()] * 6,
        [(R, 9, K, W), (4, R - 4, K, W), (4, R - 8, K, W)],
        [pltpu.VMEM((4, K, W), F32)],
        cost=10_000_000,
    )(rows, left, right, merged, y_in, vertical)

    outs = call(
        boundary,
        [vmem()] * 11,
        [(K * R, W)] * 4,
        [
            pltpu.VMEM((2, SIDE_BLOCKS, K, W), F32),
            pltpu.VMEM((8, 9, K, W), F32),
            pltpu.VMEM((8, 9, K, W), F32),
            pltpu.VMEM((8, K, W), F32),
            pltpu.VMEM((4, 8, K, W), F32),
            pltpu.VMEM((4, K, W), F32),
            pltpu.VMEM((2, FIELDS, K, W), F32),
        ],
        cost=10_000_000,
    )(rows, left, right, merged, y_in, vertical, x_in, c1, c2, second, first)
    return tuple(a.reshape(K, R, W) for a in outs)


def solution(mesh):
    spec = P(None, "ns", "ew")
    return jax.shard_map(
        local, mesh=mesh, in_specs=(spec,) * 7, out_specs=(spec,) * 4, check_vma=False
    )
```

```python
import jax
import jax.numpy as jnp
from jax import lax
from jax.experimental import pallas as pl
from jax.experimental.pallas import tpu as pltpu
from jax.sharding import PartitionSpec as P

horizontal_mix = 0.05
vertical_mix = 0.2

F32 = jnp.float32
K = 32
R = 16
W = 128
G = W // R
HALO = 4
FIELDS = 7
U, V, M = 4, 5, 6
PAIRS = 4
SIDE_BLOCKS = 28
ROWS_AT = (0, 4, 8, 12, 24, 16, 20)
CORNERS_AT = 26
SOUTH, NORTH = 0, 1
MIB = 1 << 20


def lanes():
    return lax.broadcasted_iota(jnp.int32, (K, W), 1)


def turn(x, amount):
    return pltpu.roll(x, amount % W, 1)


def pack_edges(*refs):
    sources = refs[:FIELDS]
    rows, own, to_east, to_west, raw, raw_wet, arrived = refs[FIELDS:]
    copies = []
    for f in range(FIELDS):
        target = raw_wet if f == M else raw.at[f]
        copies.append(pltpu.make_async_copy(sources[f], target, arrived.at[f]))
        copies[-1].start()
    lane = lanes()
    group = lane // G
    packed = []
    for f in range(FIELDS):
        copies[f].wait()
        source = raw_wet if f == M else raw.at[f]
        edges = jnp.zeros((K, W), F32)
        for r in range(R):
            x = source[pl.ds(r, K, stride=R), :].astype(F32)
            rows[f, r] = x
            edges = jnp.where(group == r, turn(x, G * r + HALO), edges)
        own[f] = edges
        packed.append(edges)
    west_half = lane % G < HALO
    packed.append(jnp.zeros((K, W), F32))
    for p in range(PAIRS):
        a, b = packed[2 * p], packed[2 * p + 1]
        to_east[p] = jnp.where(west_half, a, turn(b, HALO))
        to_west[p] = jnp.where(west_half, turn(b, -HALO), a)


def pack_sides(rows, own, from_west, from_east, _, left, right, merged, first, second):
    odd = lax.axis_index("ns") % 2
    lane = lanes()
    column = lane % G
    west_half = column < HALO
    for f in range(FIELDS):
        a, b = from_west[f // 2], from_east[f // 2]
        if f % 2:
            a, b = turn(a, -HALO), turn(b, HALO)
        left_f = jnp.where(west_half, a, own[f])
        right_f = jnp.where(west_half, own[f], b)
        left[f] = left_f
        right[f] = right_f
        merged[f] = jnp.where(west_half, left_f, right_f)
    for out, north in ((first, 1 - odd), (second, odd)):
        for f in range(FIELDS):
            count = 2 if f == U else HALO
            start = (R - count) * north
            for r in range(count):
                out[ROWS_AT[f] + r] = rows[f, start + r]
        for side, edges in enumerate((left, right)):
            block = jnp.zeros((K, W), F32)
            for f in range(FIELDS):
                amount = lax.rem(2 * G * f + W - (W - 2 * G) * north, W)
                moved = pltpu.roll(edges[f], amount, 1)
                block = jnp.where(lane // (2 * G) == f, moved, block)
            out[CORNERS_AT + side] = block


def coefficients(speed, mask):
    opened = {d: mask[d] * mask[d + 1] for d in (-2, -1, 0, 1)}
    s = {d: speed[d] * opened[d] * (1.0 / 12.0) for d in opened}
    a = {d: jnp.abs(s[d]) for d in s}
    w0 = {d: -(s[d] + a[d]) for d in (-1, 0, 1)}
    w3 = {d: a[d] - s[d] for d in (-2, -1, 0)}
    w1, w2 = {}, {}
    for d in (-1, 0):
        even, odd = 7.0 * s[d], 3.0 * a[d] + horizontal_mix * opened[d]
        w1[d], w2[d] = even + odd, even - odd
    forward = [w0[-1], w1[-1] - w0[0], w3[-1] - w2[0], -w3[0]]
    transposed = [-w3[-2], w3[-2] - w2[-1], w1[0] - w0[1], w0[1]]
    return forward + transposed + [w2[-1] - w1[0]]


def shifted(c, h, d, lane, step=1):
    if d == 0:
        return c
    if d > 0:
        return turn(jnp.where(lane < step * d, h, c), -step * d)
    return turn(jnp.where(lane >= W + step * d, h, c), -step * d)


def x_coefficients(u, uh, m, mh, lane):
    return coefficients(
        {d: shifted(u, uh, d, lane) for d in (-2, -1, 0, 1)},
        {d: shifted(m, mh, d, lane) for d in (-2, -1, 0, 1, 2)},
    )


def vertical_coefficient(m):
    inner = lax.broadcasted_iota(jnp.int32, (K, W), 0) < K - 1
    return jnp.where(inner, vertical_mix * m * pltpu.roll(m, K - 1, 0), 0.0)


def step_row(cell, halo, x_of, y_of, vertical, store, lane):
    results = []
    for direction in (0, 1):
        here = (2 * direction, 2 * direction + 1)
        halos, verticals = [], []
        for f in here:
            c = cell(f, 0)[...]
            flux = vertical * (c - pltpu.roll(c, K - 1, 0))
            verticals.append(pltpu.roll(flux, 1, 0) - flux)
            halos.append(halo(f))
        for q in range(0, K, 8):
            part = pl.ds(q, 8)
            lane_q = lane[:8]
            xs = [x_of.at[4 * direction + k][part] for k in range(4)]
            ys = [y_of.at[4 * direction + k][part] for k in range(4)]
            centre = 1.0 + x_of.at[8][part] + y_of.at[8][part]
            for f, h, z in zip(here, halos, verticals):
                c = cell(f, 0)[part]
                total = centre * c + z[q : q + 8]
                for coefficient, d in zip(xs, (-2, -1, 1, 2)):
                    total += coefficient * shifted(c, h[q : q + 8], d, lane_q)
                for coefficient, d in zip(ys, (-2, -1, 1, 2)):
                    total += coefficient * cell(f, d)[part]
                results.append((f, part, total))
    for result in results:
        store(*result)


def halo_columns(merged, j):
    return pltpu.roll(merged, lax.rem(2 * W - HALO - G * j, W), 1)


def edge_step(left, right, left_rows, right_rows, store):
    lane = lanes()
    column = lane % G
    west_half = column < HALO
    sides = []
    for side, rows in ((left, left_rows), (right, right_rows)):
        u, v, m = side[U], side[V], side[M]
        xs = coefficients(
            {d: turn(u, -d) for d in (-2, -1, 0, 1)},
            {d: turn(m, -d) for d in (-2, -1, 0, 1, 2)},
        )
        vh, mh = rows(V), rows(M)
        ys = coefficients(
            {d: shifted(v, vh, d, lane, G) for d in (-2, -1, 0, 1)},
            {d: shifted(m, mh, d, lane, G) for d in (-2, -1, 0, 1, 2)},
        )
        centre = 1.0 + xs[8] + ys[8]
        vertical = vertical_coefficient(m)
        results = []
        for f in range(4):
            c, ch = side[f], rows(f)
            at = 4 * (f // 2)
            flux = vertical * (c - pltpu.roll(c, K - 1, 0))
            total = centre * c + (pltpu.roll(flux, 1, 0) - flux)
            for coefficient, d in zip(xs[at : at + 4], (-2, -1, 1, 2)):
                total += coefficient * turn(c, -d)
            for coefficient, d in zip(ys[at : at + 4], (-2, -1, 1, 2)):
                total += coefficient * shifted(c, ch, d, lane, G)
            results.append(total)
        sides.append(results)
    for f in range(4):
        store(f, jnp.where(west_half, sides[0][f], sides[1][f]))


def y_coefficients_at(row, j):
    return coefficients(
        {d: row(V, j + d)[...] for d in (-2, -1, 0, 1)},
        {d: row(M, j + d)[...] for d in (-2, -1, 0, 1, 2)},
    )


def prepare(rows, y_out, vertical_out):
    def body(j, carry):
        got = y_coefficients_at(lambda f, r: rows.at[f, r], j)
        for k in range(9):
            y_out[j - 2, k] = got[k]
        return carry

    lax.fori_loop(2, R - 2, body, 0)

    def levels(j, carry):
        vertical_out[j] = vertical_coefficient(rows[M, j])
        return carry

    lax.fori_loop(0, R, levels, 0)


def by_fours(start, stop, body):
    def four(i, carry):
        for k in range(4):
            body(start + 4 * i + k, carry)
        return carry

    lax.fori_loop(0, (stop - start) // 4, four, 0)


def interior(rows, left, right, merged, y_in, vertical_in, x_out, c1_out, c2_out, merged1):
    lane = lanes()

    def x_body(j, carry):
        got = x_coefficients(
            rows[U, j], halo_columns(merged[U], j), rows[M, j], halo_columns(merged[M], j), lane
        )
        for k in range(9):
            x_out[j, k] = got[k]
        return carry

    by_fours(0, R, x_body)

    def keep(f, value):
        merged1[f] = value

    edge_step(left, right, lambda f: left[f], lambda f: right[f], keep)

    def first(j, carry):
        def store(f, part, value):
            c1_out.at[f, j - 2][part] = value

        step_row(
            lambda f, d: rows.at[f, j + d],
            lambda f: halo_columns(merged[f], j),
            x_out.at[j],
            y_in.at[j - 2],
            vertical_in[j],
            store,
            lane,
        )
        return carry

    by_fours(2, R - 2, first)

    def second(j, carry):
        def store(f, part, value):
            c2_out.at[f, j - 4][part] = value

        step_row(
            lambda f, d: c1_out.at[f, j - 2 + d],
            lambda f: halo_columns(merged1[f], j),
            x_out.at[j],
            y_in.at[j - 2],
            vertical_in[j],
            store,
            lane,
        )
        return carry

    by_fours(4, R - 4, second)


def boundary(*refs):
    rows, left, right, merged, y_in, vertical_in, x_in, c1_in, c2_in, second, first = refs[:11]
    outs = refs[11:15]
    sides, x_new, y_new, vertical_new, c1_new, merged1, rows_halo = refs[15:]
    lane = lanes()
    place = lax.axis_index("ns")
    last = lax.axis_size("ns") - 1
    odd = place % 2
    there = (place > 0, place < last)

    def unpack(b, carry):
        for source, side in ((first, 1 - odd), (second, odd)):
            here = jnp.where(side == NORTH, place < last, place > 0)
            sides[side, b] = jnp.where(here, source[b], 0.0)
        return carry

    lax.fori_loop(0, SIDE_BLOCKS, unpack, 0)

    def row(f, j):
        if j < 0:
            return sides.at[SOUTH, ROWS_AT[f] + j + (2 if f == U else HALO)]
        if j >= R:
            return sides.at[NORTH, ROWS_AT[f] + j - R]
        return rows.at[f, j]

    for s in range(2):
        for f in range(FIELDS):
            south = turn(sides[SOUTH, CORNERS_AT + s], W - 2 * G - 2 * G * f)
            north = turn(sides[NORTH, CORNERS_AT + s], -2 * G * f)
            rows_halo[s, f] = jnp.where(lane >= W // 2, south, north)

    def keep(f, value):
        merged1[f] = value

    edge_step(
        left, right, lambda f: rows_halo[0, f], lambda f: rows_halo[1, f], keep
    )

    west_half = lane % G < HALO

    def halo(f, j):
        if 0 <= j < R:
            return halo_columns(merged[f], j)
        corner = jnp.where(west_half, rows_halo[0, f], rows_halo[1, f])
        return halo_columns(corner, j % R)

    edge_rows = (-2, -1, 0, 1, R - 2, R - 1, R, R + 1)
    new_at = {j: i for i, j in enumerate(edge_rows)}
    for j in edge_rows:
        got = y_coefficients_at(row, j)
        for k in range(9):
            y_new[new_at[j], k] = got[k]
        if not 0 <= j < R:
            got = x_coefficients(row(U, j)[...], halo(U, j), row(M, j)[...], halo(M, j), lane)
            for k in range(9):
                x_new[new_at[j], k] = got[k]
            vertical_new[new_at[j]] = vertical_coefficient(row(M, j)[...])

    def x_of(j):
        return x_in.at[j] if 0 <= j < R else x_new.at[new_at[j]]

    def y_of(j):
        return y_new.at[new_at[j]] if j in new_at else y_in.at[j - 2]

    def vertical_of(j):
        return vertical_in[j] if 0 <= j < R else vertical_new[new_at[j]]

    for j in edge_rows:
        def store(f, part, value, j=j):
            if f >= 2 and not 0 <= j < R:
                value = jnp.where(there[0 if j < 0 else 1], value, 0.0)
            c1_new.at[f, new_at[j]][part] = value

        step_row(
            lambda f, d: row(f, j + d),
            lambda f: halo(f, j),
            x_of(j),
            y_of(j),
            vertical_of(j),
            store,
            lane,
        )

    def row1(f, j):
        return c1_new.at[f, new_at[j]] if j in new_at else c1_in.at[f, j - 2]

    for j in (0, 1, 2, 3, R - 4, R - 3, R - 2, R - 1):
        def store(f, part, value, j=j):
            outs[f][pl.ds(part.start * R + j, 8, stride=R), :] = value

        step_row(
            lambda f, d: row1(f, j + d),
            lambda f: halo_columns(merged1[f], j),
            x_of(j),
            y_of(j),
            vertical_of(j),
            store,
            lane,
        )

    def copy(j, carry):
        for f in range(4):
            outs[f][pl.ds(j, K, stride=R), :] = c2_in[f, j - 4]
        return carry

    lax.fori_loop(4, R - 4, copy, 0)


def vmem():
    return pl.BlockSpec(memory_space=pltpu.VMEM)


def call(kernel, in_specs, out_shapes, scratch=(), limit=16 * MIB, cost=0):
    return pl.pallas_call(
        kernel,
        out_shape=[jax.ShapeDtypeStruct(shape, F32) for shape in out_shapes],
        in_specs=in_specs,
        out_specs=[vmem()] * len(out_shapes),
        scratch_shapes=list(scratch),
        compiler_params=pltpu.CompilerParams(vmem_limit_bytes=limit),
        cost_estimate=pl.CostEstimate(flops=cost, bytes_accessed=MIB, transcendentals=0),
    )


def partners(odd, n_ew, n_ns):
    pairs = []
    for e in range(n_ew):
        for s in range(n_ns):
            step = 1 if (s - odd) % 2 == 0 else -1
            if 0 <= s + step < n_ns:
                to = (e, s + step)
            else:
                to = (e ^ 1 if e ^ 1 < n_ew else e, s)
            pairs.append((e * n_ns + s, to[0] * n_ns + to[1]))
    return pairs


def local(temp, salt, u_east, v_north, wet, cot_temp, cot_salt):
    flat = [a.reshape(K * R, W) for a in (temp, salt, cot_temp, cot_salt, u_east, v_north, wet)]

    rows, own, to_east, to_west = call(
        pack_edges,
        [pl.BlockSpec(memory_space=pltpu.HBM)] * FIELDS,
        [(FIELDS, R, K, W), (FIELDS, K, W), (PAIRS, K, W), (PAIRS, K, W)],
        [
            pltpu.VMEM((FIELDS - 1, K * R, W), F32),
            pltpu.VMEM((K * R, W), jnp.int32),
            pltpu.SemaphoreType.DMA((FIELDS,)),
        ],
    )(*[pltpu.with_memory_space_constraint(a, pltpu.HBM) for a in flat])

    n = lax.axis_size("ew")
    from_west = lax.ppermute(to_east, "ew", [(i, (i + 1) % n) for i in range(n)])
    from_east = lax.ppermute(to_west, "ew", [((i + 1) % n, i) for i in range(n)])

    y_in, vertical = call(
        prepare, [vmem()], [(R - 4, 9, K, W), (R, K, W)], cost=10_000_000
    )(rows)

    left, right, merged, first, second = call(
        pack_sides,
        [vmem()] * 4 + [pl.BlockSpec(memory_space=pl.ANY)],
        [(FIELDS, K, W)] * 3 + [(SIDE_BLOCKS, K, W)] * 2,
    )(rows, own, from_west, from_east, vertical)

    n = lax.axis_size("ns")

    second = lax.ppermute(second, ("ew", "ns"), partners(1, lax.axis_size("ew"), n))
    first = lax.ppermute(first, ("ew", "ns"), partners(0, lax.axis_size("ew"), n))

    x_in, c1, c2 = call(
        interior,
        [vmem()] * 6,
        [(R, 9, K, W), (4, R - 4, K, W), (4, R - 8, K, W)],
        [pltpu.VMEM((4, K, W), F32)],
        cost=10_000_000,
    )(rows, left, right, merged, y_in, vertical)

    outs = call(
        boundary,
        [vmem()] * 11,
        [(K * R, W)] * 4,
        [
            pltpu.VMEM((2, SIDE_BLOCKS, K, W), F32),
            pltpu.VMEM((8, 9, K, W), F32),
            pltpu.VMEM((8, 9, K, W), F32),
            pltpu.VMEM((8, K, W), F32),
            pltpu.VMEM((4, 8, K, W), F32),
            pltpu.VMEM((4, K, W), F32),
            pltpu.VMEM((2, FIELDS, K, W), F32),
        ],
        cost=10_000_000,
    )(rows, left, right, merged, y_in, vertical, x_in, c1, c2, second, first)
    return tuple(a.reshape(K, R, W) for a in outs)


def solution(mesh):
    spec = P(None, "ns", "ew")
    return jax.shard_map(
        local, mesh=mesh, in_specs=(spec,) * 7, out_specs=(spec,) * 4, check_vma=False
    )
```

```python
import jax
import jax.numpy as jnp
from jax import lax
from jax.experimental import pallas as pl
from jax.experimental.pallas import tpu as pltpu
from jax.sharding import PartitionSpec as P

horizontal_mix = 0.05
vertical_mix = 0.2

F32 = jnp.float32
K = 32
R = 16
W = 128
G = W // R
HALO = 4
FIELDS = 7
U, V, M = 4, 5, 6
PAIRS = 4
SIDE_BLOCKS = 26
ROWS_AT = (0, 4, 8, 12, 24, 16, 20)
SOUTH, NORTH = 0, 1
MIB = 1 << 20


def lanes():
    return lax.broadcasted_iota(jnp.int32, (K, W), 1)


def turn(x, amount):
    return pltpu.roll(x, amount % W, 1)


def pack_edges(*refs):
    sources = refs[:FIELDS]
    rows, raw, own, to_east, to_west, raw_flow, raw_wet, arrived = refs[FIELDS:]
    copies = []
    for f in range(FIELDS):
        target = raw.at[f, pl.ds(R, K * R)] if f < 4 else raw_wet if f == M else raw_flow.at[f - U]
        copies.append(pltpu.make_async_copy(sources[f], target, arrived.at[f]))
        copies[-1].start()
    for f in range(4):
        raw[f, pl.ds(0, R)] = jnp.zeros((R, W), F32)
        raw[f, pl.ds((K + 1) * R, R)] = jnp.zeros((R, W), F32)
    lane = lanes()
    group = lane // G
    packed = []
    for f in range(FIELDS):
        copies[f].wait()
        source = raw.at[f] if f < 4 else raw_wet if f == M else raw_flow.at[f - U]
        edges = jnp.zeros((K, W), F32)
        for r in range(R):
            x = source[pl.ds(R + r if f < 4 else r, K, stride=R), :].astype(F32)
            rows[f, r] = x
            edges = jnp.where(group == r, turn(x, G * r + HALO), edges)
        own[f] = edges
        packed.append(edges)
    west_half = lane % G < HALO
    packed.append(jnp.zeros((K, W), F32))
    for p in range(PAIRS):
        a, b = packed[2 * p], packed[2 * p + 1]
        to_east[p] = jnp.where(west_half, a, turn(b, HALO))
        to_west[p] = jnp.where(west_half, turn(b, -HALO), a)


def pack_sides(rows, first, second):
    odd = lax.axis_index("ns") % 2
    for out, north in ((first, 1 - odd), (second, odd)):
        for f in range(FIELDS):
            count = 2 if f == U else HALO
            start = (R - count) * north
            for r in range(count):
                out[ROWS_AT[f] + r] = rows[f, start + r]


def pack_corners(own, from_west, from_east, _, left, right, merged, first, second):
    odd = lax.axis_index("ns") % 2
    lane = lanes()
    west_half = lane % G < HALO
    for f in range(FIELDS):
        a, b = from_west[f // 2], from_east[f // 2]
        if f % 2:
            a, b = turn(a, -HALO), turn(b, HALO)
        left_f = jnp.where(west_half, a, own[f])
        right_f = jnp.where(west_half, own[f], b)
        left[f] = left_f
        right[f] = right_f
        merged[f] = jnp.where(west_half, left_f, right_f)
    for out, north in ((first, 1 - odd), (second, odd)):
        for side, edges in enumerate((left, right)):
            block = jnp.zeros((K, W), F32)
            for f in range(FIELDS):
                amount = lax.rem(2 * G * f + W - (W - 2 * G) * north, W)
                moved = pltpu.roll(edges[f], amount, 1)
                block = jnp.where(lane // (2 * G) == f, moved, block)
            out[side] = block


def coefficients(speed, mask):
    opened = {d: mask[d] * mask[d + 1] for d in (-2, -1, 0, 1)}
    s = {d: speed[d] * opened[d] * (1.0 / 12.0) for d in opened}
    a = {d: jnp.abs(s[d]) for d in s}
    w0 = {d: -(s[d] + a[d]) for d in (-1, 0, 1)}
    w3 = {d: a[d] - s[d] for d in (-2, -1, 0)}
    w1, w2 = {}, {}
    for d in (-1, 0):
        even, odd = 7.0 * s[d], 3.0 * a[d] + horizontal_mix * opened[d]
        w1[d], w2[d] = even + odd, even - odd
    forward = [w0[-1], w1[-1] - w0[0], w3[-1] - w2[0], -w3[0]]
    transposed = [-w3[-2], w3[-2] - w2[-1], w1[0] - w0[1], w0[1]]
    return forward + transposed + [w2[-1] - w1[0]]


def shifted(c, h, d, lane, step=1):
    if d == 0:
        return c
    if d > 0:
        return turn(jnp.where(lane < step * d, h, c), -step * d)
    return turn(jnp.where(lane >= W + step * d, h, c), -step * d)


def x_coefficients(u, uh, m, mh, lane):
    return coefficients(
        {d: shifted(u, uh, d, lane) for d in (-2, -1, 0, 1)},
        {d: shifted(m, mh, d, lane) for d in (-2, -1, 0, 1, 2)},
    )


def level_coefficients(m):
    inner = lax.broadcasted_iota(jnp.int32, (K, W), 0) < K - 1
    after = jnp.where(inner, vertical_mix * m * pltpu.roll(m, K - 1, 0), 0.0)
    before = pltpu.roll(after, 1, 0)
    return after, before, 1.0 - after - before


def chunk(q):
    return pl.ds(8 * q, 8)


def strided(q, j, stride, shift=0):
    return pl.ds((8 * q + 1 + shift) * stride + j, 8, stride=stride)


def step_row(store, load, x=None, y=None, z=None, base=None):
    lane = lanes()[:8]
    results = []
    for q in range(K // 8):
        part = chunk(q)
        centre = None
        for term in (x and x[0].at[8], y and y.at[8], z and z[0].at[2]):
            if term is not None:
                centre = term[part] if centre is None else centre + term[part]
        if z:
            after, before = z[0].at[0][part], z[0].at[1][part]
        for direction in (0, 1):
            ks = range(4 * direction, 4 * direction + 4)
            xs = [x[0].at[k][part] for k in ks] if x else []
            ys = [y.at[k][part] for k in ks] if y else []
            for f in (2 * direction, 2 * direction + 1):
                c = load(f, 0, q)
                total = centre * c
                if base:
                    total += base(f, q)
                if x:
                    h = x[1](f, q)
                for coefficient, d in zip(xs, (-2, -1, 1, 2)):
                    total += coefficient * shifted(c, h, d, lane)
                for coefficient, d in zip(ys, (-2, -1, 1, 2)):
                    total += coefficient * load(f, d, q)
                if z:
                    c_after, c_before = z[1](f, q)
                    total += after * c_after + before * c_before
                results.append((f, q, total))
    for result in results:
        store(*result)


def halo_columns(merged, j):
    return pltpu.roll(merged, lax.rem(2 * W - HALO - G * j, W), 1)


def edge_columns_and_levels(edges):
    u, m = edges[U], edges[M]
    xs = coefficients(
        {d: turn(u, -d) for d in (-2, -1, 0, 1)},
        {d: turn(m, -d) for d in (-2, -1, 0, 1, 2)},
    )
    after, before, centre = level_coefficients(m)
    results = []
    for f in range(4):
        c = edges[f]
        total = (centre + xs[8]) * c
        total += after * pltpu.roll(c, K - 1, 0) + before * pltpu.roll(c, 1, 0)
        for coefficient, d in zip(xs[4 * (f // 2) :], (-2, -1, 1, 2)):
            total += coefficient * turn(c, -d)
        results.append(total)
    return results


def edge_rows(edges, beyond):
    lane = lanes()
    v, m = edges[V], edges[M]
    vh, mh = beyond(V), beyond(M)
    ys = coefficients(
        {d: shifted(v, vh, d, lane, G) for d in (-2, -1, 0, 1)},
        {d: shifted(m, mh, d, lane, G) for d in (-2, -1, 0, 1, 2)},
    )
    results = []
    for f in range(4):
        c, ch = edges[f], beyond(f)
        total = ys[8] * c
        for coefficient, d in zip(ys[4 * (f // 2) :], (-2, -1, 1, 2)):
            total += coefficient * shifted(c, ch, d, lane, G)
        results.append(total)
    return results


def y_coefficients_at(row, j):
    return coefficients(
        {d: row(V, j + d)[...] for d in (-2, -1, 0, 1)},
        {d: row(M, j + d)[...] for d in (-2, -1, 0, 1, 2)},
    )


def by_fours(start, stop, body):
    def four(i, carry):
        for k in range(4):
            body(start + 4 * i + k)
        return carry

    lax.fori_loop(0, (stop - start) // 4, four, 0)


def raw_levels(raw, j):
    return lambda f, q: (raw.at[f][strided(q, j, R, 1), :], raw.at[f][strided(q, j, R, -1), :])


def prepare(rows, raw, y_out, level_out, base_out):
    def levels(j):
        for k, value in enumerate(level_coefficients(rows[M, j])):
            level_out[j, k] = value

    by_fours(0, R, levels)

    def across(j):
        got = y_coefficients_at(lambda f, r: rows.at[f, r], j)
        for k in range(9):
            y_out[j - 2, k] = got[k]

    by_fours(2, R - 2, across)

    def first(j):
        def store(f, q, value):
            base_out.at[f, j - 2][chunk(q)] = value

        step_row(
            store,
            lambda f, d, q: rows.at[f, j + d][chunk(q)],
            y=y_out.at[j - 2],
            z=(level_out.at[j], raw_levels(raw, j)),
        )

    by_fours(2, R - 2, first)


def interior(*refs):
    rows, raw, left, right, merged, y_in, level_in, base_in = refs[:8]
    x_out, c1_out, part1_out, c2_out, part2_out, edge_out, merged1 = refs[8:]
    lane = lanes()
    west_half = lane % G < HALO
    for f in range(4):
        c1_out[f, pl.ds(0, R)] = jnp.zeros((R, W), F32)
        c1_out[f, pl.ds((K + 1) * R, R)] = jnp.zeros((R, W), F32)

    def x_body(j):
        got = x_coefficients(
            rows[U, j], halo_columns(merged[U], j), rows[M, j], halo_columns(merged[M], j), lane
        )
        for k in range(9):
            x_out[j, k] = got[k]

    by_fours(0, R, x_body)

    both = []
    for side, edges in enumerate((left, right)):
        partial = edge_columns_and_levels(edges)
        across = edge_rows(edges, lambda f: edges[f])
        for f in range(4):
            edge_out[side, f] = partial[f]
        both.append([p + a for p, a in zip(partial, across)])
    for f in range(4):
        merged1[f] = jnp.where(west_half, both[0][f], both[1][f])

    def halo(source, j):
        return lambda f, q: halo_columns(source.at[f][chunk(q)], j)

    def first(j):
        def store(f, q, value):
            c1_out.at[f][strided(q, j, R), :] = value

        step_row(
            store,
            lambda f, d, q: rows.at[f, j][chunk(q)],
            x=(x_out.at[j], halo(merged, j)),
            base=lambda f, q: base_in.at[f, j - 2][chunk(q)],
        )

    by_fours(2, R - 2, first)

    for i, j in enumerate((0, 1, R - 2, R - 1)):
        def store(f, q, value):
            part1_out.at[f, i][chunk(q)] = value

        step_row(
            store,
            lambda f, d, q: rows.at[f, j][chunk(q)],
            x=(x_out.at[j], halo(merged, j)),
            z=(level_in.at[j], raw_levels(raw, j)),
        )

    def second(j):
        def store(f, q, value):
            c2_out.at[f, j - 4][chunk(q)] = value

        step_row(
            store,
            lambda f, d, q: c1_out.at[f][strided(q, j + d, R), :],
            x=(x_out.at[j], halo(merged1, j)),
            y=y_in.at[j - 2],
            z=(level_in.at[j], raw_levels(c1_out, j)),
        )

    by_fours(4, R - 4, second)

    for i, j in enumerate((2, 3, R - 4, R - 3)):
        def store(f, q, value):
            part2_out.at[f, i][chunk(q)] = value

        step_row(
            store,
            lambda f, d, q: c1_out.at[f][strided(q, j, R), :],
            x=(x_out.at[j], halo(merged1, j)),
            z=(level_in.at[j], raw_levels(c1_out, j)),
        )


def boundary(*refs):
    rows, left, right, merged, y_in, level_in, x_in, c1_in, part1_in, c2_in, part2_in, edge_in = refs[:12]
    messages = refs[12:16]
    outs = refs[16:20]
    sides, corners, x_new, y_new, level_new, c1_new, merged1, beyond = refs[20:]
    lane = lanes()
    west_half = lane % G < HALO
    place = lax.axis_index("ns")
    last = lax.axis_size("ns") - 1
    odd = place % 2
    inside = {SOUTH: place > 0, NORTH: place < last}
    slots = 8
    near = (-2, -1, 0, 1, R - 2, R - 1, R, R + 1)
    new_at = {j: i for i, j in enumerate(near)}
    for f in range(4):
        c1_new[f, pl.ds(0, slots)] = jnp.zeros((slots, W), F32)
        c1_new[f, pl.ds((K + 1) * slots, slots)] = jnp.zeros((slots, W), F32)

    for source, target in ((0, sides), (1, corners)):
        def unpack(b, carry):
            for message, side in ((messages[source], odd), (messages[source + 2], 1 - odd)):
                here = jnp.where(side == NORTH, place < last, place > 0)
                target[side, b] = jnp.where(here, message[b], 0.0)
            return carry

        lax.fori_loop(0, target.shape[1], unpack, 0, unroll=2)

    def row(f, j):
        if j < 0:
            return sides.at[SOUTH, ROWS_AT[f] + j + (2 if f == U else HALO)]
        if j >= R:
            return sides.at[NORTH, ROWS_AT[f] + j - R]
        return rows.at[f, j]

    for s in range(2):
        for f in range(FIELDS):
            south = turn(corners[SOUTH, s], W - 2 * G - 2 * G * f)
            north = turn(corners[NORTH, s], -2 * G * f)
            beyond[s, f] = jnp.where(lane >= W // 2, south, north)

    both = []
    for s, edges in enumerate((left, right)):
        across = edge_rows(edges, lambda f: beyond[s, f])
        both.append([edge_in[s, f] + a for f, a in enumerate(across)])
    for f in range(4):
        merged1[f] = jnp.where(west_half, both[0][f], both[1][f])

    def halo_beyond(f, j):
        return halo_columns(jnp.where(west_half, beyond[0, f], beyond[1, f]), j % R)

    for j in near:
        got = y_coefficients_at(row, j)
        for k in range(9):
            y_new[new_at[j], k] = got[k]
        if not 0 <= j < R:
            got = x_coefficients(
                row(U, j)[...], halo_beyond(U, j), row(M, j)[...], halo_beyond(M, j), lane
            )
            for k in range(9):
                x_new[new_at[j], k] = got[k]
            for k, value in enumerate(level_coefficients(row(M, j)[...])):
                level_new[new_at[j], k] = value

    for j in near:
        side = SOUTH if j < R // 2 else NORTH

        def store(f, q, value):
            if f >= 2 and not 0 <= j < R:
                value = jnp.where(inside[side], value, 0.0)
            c1_new.at[f][strided(q, new_at[j], slots), :] = value

        def load(f, d, q):
            return row(f, j + d)[chunk(q)]

        if 0 <= j < R:
            i = (0, 1, R - 2, R - 1).index(j)
            step_row(
                store, load, y=y_new.at[new_at[j]], base=lambda f, q: part1_in.at[f, i][chunk(q)]
            )
        else:
            halos = [halo_beyond(f, j) for f in range(4)]
            after = [pltpu.roll(row(f, j)[...], K - 1, 0) for f in range(4)]
            before = [pltpu.roll(row(f, j)[...], 1, 0) for f in range(4)]
            at = lambda x, q: x[8 * q : 8 * q + 8]
            step_row(
                store,
                load,
                x=(x_new.at[new_at[j]], lambda f, q: at(halos[f], q)),
                y=y_new.at[new_at[j]],
                z=(level_new.at[new_at[j]], lambda f, q: (at(after[f], q), at(before[f], q))),
            )

    def load1(f, j, q):
        if j in new_at:
            return c1_new.at[f][strided(q, new_at[j], slots), :]
        return c1_in.at[f][strided(q, j, R), :]

    for j in (0, 1, 2, 3, R - 4, R - 3, R - 2, R - 1):
        def store(f, q, value):
            outs[f][pl.ds(8 * q * R + j, 8, stride=R), :] = value

        def load(f, d, q):
            return load1(f, j + d, q)

        if j in new_at:
            def neighbours(f, q):
                ref, at = c1_new.at[f], new_at[j]
                return ref[strided(q, at, slots, 1), :], ref[strided(q, at, slots, -1), :]

            step_row(
                store,
                load,
                x=(x_in.at[j], lambda f, q: halo_columns(merged1.at[f][chunk(q)], j)),
                y=y_new.at[new_at[j]],
                z=(level_in.at[j], neighbours),
            )
        else:
            i = (2, 3, R - 4, R - 3).index(j)
            step_row(
                store, load, y=y_in.at[j - 2], base=lambda f, q: part2_in.at[f, i][chunk(q)]
            )

    def copy(j, carry):
        for f in range(4):
            outs[f][pl.ds(j, K, stride=R), :] = c2_in[f, j - 4]
        return carry

    lax.fori_loop(4, R - 4, copy, 0, unroll=2)


def vmem():
    return pl.BlockSpec(memory_space=pltpu.VMEM)


def call(kernel, in_specs, out_shapes, scratch=(), limit=16 * MIB, cost=0):
    return pl.pallas_call(
        kernel,
        out_shape=[jax.ShapeDtypeStruct(shape, F32) for shape in out_shapes],
        in_specs=in_specs,
        out_specs=[vmem()] * len(out_shapes),
        scratch_shapes=list(scratch),
        compiler_params=pltpu.CompilerParams(vmem_limit_bytes=limit),
        cost_estimate=pl.CostEstimate(flops=cost, bytes_accessed=MIB, transcendentals=0),
    )


def partners(odd, n_ew, n_ns):
    pairs = []
    for e in range(n_ew):
        for s in range(n_ns):
            step = 1 if (s - odd) % 2 == 0 else -1
            if 0 <= s + step < n_ns:
                to = (e, s + step)
            else:
                to = (e ^ 1 if e ^ 1 < n_ew else e, s)
            pairs.append((e * n_ns + s, to[0] * n_ns + to[1]))
    return pairs


def local(temp, salt, u_east, v_north, wet, cot_temp, cot_salt):
    flat = [a.reshape(K * R, W) for a in (temp, salt, cot_temp, cot_salt, u_east, v_north, wet)]

    row = (K, W)
    padded = ((K + 2) * R, W)
    rows, raw, own, to_east, to_west = call(
        pack_edges,
        [pl.BlockSpec(memory_space=pltpu.HBM)] * FIELDS,
        [(FIELDS, R) + row, (4,) + padded, (FIELDS,) + row, (PAIRS,) + row, (PAIRS,) + row],
        [
            pltpu.VMEM((2, K * R, W), F32),
            pltpu.VMEM((K * R, W), jnp.int32),
            pltpu.SemaphoreType.DMA((FIELDS,)),
        ],
    )(*[pltpu.with_memory_space_constraint(a, pltpu.HBM) for a in flat])

    n_ew, n_ns = lax.axis_size("ew"), lax.axis_size("ns")
    from_west = lax.ppermute(to_east, "ew", [(i, (i + 1) % n_ew) for i in range(n_ew)])
    from_east = lax.ppermute(to_west, "ew", [((i + 1) % n_ew, i) for i in range(n_ew)])

    def swap(odd, message):
        return lax.ppermute(message, ("ew", "ns"), partners(odd, n_ew, n_ns))

    first, second = call(pack_sides, [vmem()], [(SIDE_BLOCKS,) + row] * 2)(rows)
    second = swap(1, second)
    first = swap(0, first)

    y_in, level, base = call(
        prepare,
        [vmem()] * 2,
        [(R - 4, 9) + row, (R, 3) + row, (4, R - 4) + row],
        cost=10_000_000,
    )(rows, raw)

    left, right, merged, first_corners, second_corners = call(
        pack_corners,
        [vmem()] * 3 + [pl.BlockSpec(memory_space=pl.ANY)],
        [(FIELDS,) + row] * 3 + [(2,) + row] * 2,
    )(own, from_west, from_east, level)
    second_corners = swap(1, second_corners)
    first_corners = swap(0, first_corners)

    x_in, c1, part1, c2, part2, edge = call(
        interior,
        [vmem()] * 8,
        [(R, 9) + row, (4,) + padded, (4, 4) + row, (4, R - 8) + row, (4, 4) + row, (2, 4) + row],
        [pltpu.VMEM((4,) + row, F32)],
        cost=10_000_000,
    )(rows, raw, left, right, merged, y_in, level, base)

    outs = call(
        boundary,
        [vmem()] * 16,
        [(K * R, W)] * 4,
        [
            pltpu.VMEM((2, SIDE_BLOCKS) + row, F32),
            pltpu.VMEM((2, 2) + row, F32),
            pltpu.VMEM((8, 9) + row, F32),
            pltpu.VMEM((8, 9) + row, F32),
            pltpu.VMEM((8, 3) + row, F32),
            pltpu.VMEM((4, (K + 2) * 8, W), F32),
            pltpu.VMEM((4,) + row, F32),
            pltpu.VMEM((2, FIELDS) + row, F32),
        ],
        cost=10_000_000,
    )(
        *(rows, left, right, merged, y_in, level, x_in, c1, part1, c2, part2, edge),
        *(second, second_corners, first, first_corners),
    )
    return tuple(a.reshape(K, R, W) for a in outs)


def solution(mesh):
    spec = P(None, "ns", "ew")
    return jax.shard_map(
        local, mesh=mesh, in_specs=(spec,) * 7, out_specs=(spec,) * 4, check_vma=False
    )
```

```python
import jax
import jax.numpy as jnp
from jax import lax
from jax.experimental import pallas as pl
from jax.experimental.pallas import tpu as pltpu
from jax.sharding import PartitionSpec as P

horizontal_mix = 0.05
vertical_mix = 0.2

F32 = jnp.float32
K = 32
R = 16
W = 128
G = W // R
HALO = 4
FIELDS = 7
U, V, M = 4, 5, 6
PAIRS = 4
SIDE_BLOCKS = 26
ROWS_AT = (0, 4, 8, 12, 24, 16, 20)
SOUTH, NORTH = 0, 1
MIB = 1 << 20


def lanes():
    return lax.broadcasted_iota(jnp.int32, (K, W), 1)


def turn(x, amount):
    return pltpu.roll(x, amount % W, 1)


def pack_edges(*refs):
    sources = refs[:FIELDS]
    rows, raw, own, to_east, to_west, raw_flow, raw_wet, arrived = refs[FIELDS:]
    copies = []
    for f in range(FIELDS):
        target = raw.at[f, pl.ds(R, K * R)] if f < 4 else raw_wet if f == M else raw_flow.at[f - U]
        copies.append(pltpu.make_async_copy(sources[f], target, arrived.at[f]))
        copies[-1].start()
    for f in range(4):
        raw[f, pl.ds(0, R)] = jnp.zeros((R, W), F32)
        raw[f, pl.ds((K + 1) * R, R)] = jnp.zeros((R, W), F32)
    lane = lanes()
    group = lane // G
    packed = []
    for f in range(FIELDS):
        copies[f].wait()
        source = raw.at[f] if f < 4 else raw_wet if f == M else raw_flow.at[f - U]
        edges = jnp.zeros((K, W), F32)
        for r in range(R):
            x = source[pl.ds(R + r if f < 4 else r, K, stride=R), :].astype(F32)
            rows[f, r] = x
            edges = jnp.where(group == r, turn(x, G * r + HALO), edges)
        own[f] = edges
        packed.append(edges)
    west_half = lane % G < HALO
    packed.append(jnp.zeros((K, W), F32))
    for p in range(PAIRS):
        a, b = packed[2 * p], packed[2 * p + 1]
        to_east[p] = jnp.where(west_half, a, turn(b, HALO))
        to_west[p] = jnp.where(west_half, turn(b, -HALO), a)


def pack_sides(rows, first, second):
    odd = lax.axis_index("ns") % 2
    for out, north in ((first, 1 - odd), (second, odd)):
        for f in range(FIELDS):
            count = 2 if f == U else HALO
            start = (R - count) * north
            for r in range(count):
                out[ROWS_AT[f] + r] = rows[f, start + r]


def pack_corners(own, from_west, from_east, _, left, right, merged, first, second):
    odd = lax.axis_index("ns") % 2
    lane = lanes()
    west_half = lane % G < HALO
    for f in range(FIELDS):
        a, b = from_west[f // 2], from_east[f // 2]
        if f % 2:
            a, b = turn(a, -HALO), turn(b, HALO)
        left_f = jnp.where(west_half, a, own[f])
        right_f = jnp.where(west_half, own[f], b)
        left[f] = left_f
        right[f] = right_f
        merged[f] = jnp.where(west_half, left_f, right_f)
    for out, north in ((first, 1 - odd), (second, odd)):
        for side, edges in enumerate((left, right)):
            block = jnp.zeros((K, W), F32)
            for f in range(FIELDS):
                amount = lax.rem(2 * G * f + W - (W - 2 * G) * north, W)
                moved = pltpu.roll(edges[f], amount, 1)
                block = jnp.where(lane // (2 * G) == f, moved, block)
            out[side] = block


def coefficients(speed, mask):
    opened = {d: mask[d] * mask[d + 1] for d in (-2, -1, 0, 1)}
    s = {d: speed[d] * opened[d] * (1.0 / 12.0) for d in opened}
    a = {d: jnp.abs(s[d]) for d in s}
    w0 = {d: -(s[d] + a[d]) for d in (-1, 0, 1)}
    w3 = {d: a[d] - s[d] for d in (-2, -1, 0)}
    w1, w2 = {}, {}
    for d in (-1, 0):
        even, odd = 7.0 * s[d], 3.0 * a[d] + horizontal_mix * opened[d]
        w1[d], w2[d] = even + odd, even - odd
    forward = [w0[-1], w1[-1] - w0[0], w3[-1] - w2[0], -w3[0]]
    transposed = [-w3[-2], w3[-2] - w2[-1], w1[0] - w0[1], w0[1]]
    return forward + transposed + [w2[-1] - w1[0]]


def shifted(c, h, d, lane, step=1):
    if d == 0:
        return c
    if d > 0:
        return turn(jnp.where(lane < step * d, h, c), -step * d)
    return turn(jnp.where(lane >= W + step * d, h, c), -step * d)


def x_coefficients(u, uh, m, mh, lane):
    return coefficients(
        {d: shifted(u, uh, d, lane) for d in (-2, -1, 0, 1)},
        {d: shifted(m, mh, d, lane) for d in (-2, -1, 0, 1, 2)},
    )


def level_coefficients(m):
    inner = lax.broadcasted_iota(jnp.int32, (K, W), 0) < K - 1
    after = jnp.where(inner, vertical_mix * m * pltpu.roll(m, K - 1, 0), 0.0)
    before = pltpu.roll(after, 1, 0)
    return after, before, 1.0 - after - before


def chunk(q):
    return pl.ds(8 * q, 8)


def strided(q, j, stride, shift=0):
    return pl.ds((8 * q + 1 + shift) * stride + j, 8, stride=stride)


def step_row(store, load, x=None, y=None, z=None, base=None):
    lane = lanes()[:8]
    results = []
    for q in range(K // 8):
        part = chunk(q)
        centre = None
        for term in (x and x[0].at[8], y and y.at[8], z and z[0].at[2]):
            if term is not None:
                centre = term[part] if centre is None else centre + term[part]
        if z:
            after, before = z[0].at[0][part], z[0].at[1][part]
        for direction in (0, 1):
            ks = range(4 * direction, 4 * direction + 4)
            xs = [x[0].at[k][part] for k in ks] if x else []
            ys = [y.at[k][part] for k in ks] if y else []
            for f in (2 * direction, 2 * direction + 1):
                c = load(f, 0, q)
                total = centre * c
                if base:
                    total += base(f, q)
                if x:
                    h = x[1](f, q)
                for coefficient, d in zip(xs, (-2, -1, 1, 2)):
                    total += coefficient * shifted(c, h, d, lane)
                for coefficient, d in zip(ys, (-2, -1, 1, 2)):
                    total += coefficient * load(f, d, q)
                if z:
                    c_after, c_before = z[1](f, q)
                    total += after * c_after + before * c_before
                results.append((f, q, total))
    for result in results:
        store(*result)


def halo_columns(merged, j):
    return pltpu.roll(merged, lax.rem(2 * W - HALO - G * j, W), 1)


def edge_columns_and_levels(edges):
    u, m = edges[U], edges[M]
    xs = coefficients(
        {d: turn(u, -d) for d in (-2, -1, 0, 1)},
        {d: turn(m, -d) for d in (-2, -1, 0, 1, 2)},
    )
    after, before, centre = level_coefficients(m)
    results = []
    for f in range(4):
        c = edges[f]
        total = (centre + xs[8]) * c
        total += after * pltpu.roll(c, K - 1, 0) + before * pltpu.roll(c, 1, 0)
        for coefficient, d in zip(xs[4 * (f // 2) :], (-2, -1, 1, 2)):
            total += coefficient * turn(c, -d)
        results.append(total)
    return results


def edge_rows(edges, beyond):
    lane = lanes()
    v, m = edges[V], edges[M]
    vh, mh = beyond(V), beyond(M)
    ys = coefficients(
        {d: shifted(v, vh, d, lane, G) for d in (-2, -1, 0, 1)},
        {d: shifted(m, mh, d, lane, G) for d in (-2, -1, 0, 1, 2)},
    )
    results = []
    for f in range(4):
        c, ch = edges[f], beyond(f)
        total = ys[8] * c
        for coefficient, d in zip(ys[4 * (f // 2) :], (-2, -1, 1, 2)):
            total += coefficient * shifted(c, ch, d, lane, G)
        results.append(total)
    return results


def y_coefficients_at(row, j):
    return coefficients(
        {d: row(V, j + d)[...] for d in (-2, -1, 0, 1)},
        {d: row(M, j + d)[...] for d in (-2, -1, 0, 1, 2)},
    )


def by_fours(start, stop, body):
    def four(i, carry):
        for k in range(4):
            body(start + 4 * i + k)
        return carry

    lax.fori_loop(0, (stop - start) // 4, four, 0)


def raw_levels(raw, j):
    return lambda f, q: (raw.at[f][strided(q, j, R, 1), :], raw.at[f][strided(q, j, R, -1), :])


def rolled_levels(load):
    after = [pltpu.roll(load(f), K - 1, 0) for f in range(4)]
    before = [pltpu.roll(load(f), 1, 0) for f in range(4)]
    return lambda f, q: (after[f][8 * q : 8 * q + 8], before[f][8 * q : 8 * q + 8])


def prepare(rows, raw, y_out, level_out, base_out):
    def levels(j):
        for k, value in enumerate(level_coefficients(rows[M, j])):
            level_out[j, k] = value

    by_fours(0, R, levels)

    def across(j):
        got = y_coefficients_at(lambda f, r: rows.at[f, r], j)
        for k in range(9):
            y_out[j - 2, k] = got[k]

    by_fours(2, R - 2, across)

    def first(j):
        def store(f, q, value):
            base_out.at[f, j - 2][chunk(q)] = value

        step_row(
            store,
            lambda f, d, q: rows.at[f, j + d][chunk(q)],
            y=y_out.at[j - 2],
            z=(level_out.at[j], raw_levels(raw, j)),
        )

    by_fours(2, R - 2, first)


def interior(*refs):
    rows, raw, left, right, merged, y_in, level_in, base_in = refs[:8]
    x_out, c1_out, part1_out, c2_out, part2_out, edge_out, merged1 = refs[8:]
    lane = lanes()
    west_half = lane % G < HALO
    def x_body(j):
        got = x_coefficients(
            rows[U, j], halo_columns(merged[U], j), rows[M, j], halo_columns(merged[M], j), lane
        )
        for k in range(9):
            x_out[j, k] = got[k]

    by_fours(0, R, x_body)

    both = []
    for side, edges in enumerate((left, right)):
        partial = edge_columns_and_levels(edges)
        across = edge_rows(edges, lambda f: edges[f])
        for f in range(4):
            edge_out[side, f] = partial[f]
        both.append([p + a for p, a in zip(partial, across)])
    for f in range(4):
        merged1[f] = jnp.where(west_half, both[0][f], both[1][f])

    def halo(source, j):
        halos = [halo_columns(source[f], j) for f in range(4)]
        return lambda f, q: halos[f][8 * q : 8 * q + 8]

    def first(j):
        def store(f, q, value):
            c1_out.at[f, j - 2][chunk(q)] = value

        step_row(
            store,
            lambda f, d, q: rows.at[f, j][chunk(q)],
            x=(x_out.at[j], halo(merged, j)),
            base=lambda f, q: base_in.at[f, j - 2][chunk(q)],
        )

    by_fours(2, R - 2, first)

    for i, j in enumerate((0, 1, R - 2, R - 1)):
        def store(f, q, value):
            part1_out.at[f, i][chunk(q)] = value

        step_row(
            store,
            lambda f, d, q: rows.at[f, j][chunk(q)],
            x=(x_out.at[j], halo(merged, j)),
            z=(level_in.at[j], raw_levels(raw, j)),
        )

    def second(j):
        def store(f, q, value):
            c2_out.at[f, j - 4][chunk(q)] = value

        step_row(
            store,
            lambda f, d, q: c1_out.at[f, j - 2 + d][chunk(q)],
            x=(x_out.at[j], halo(merged1, j)),
            y=y_in.at[j - 2],
            z=(level_in.at[j], rolled_levels(lambda f: c1_out[f, j - 2])),
        )

    by_fours(4, R - 4, second)

    for i, j in enumerate((2, 3, R - 4, R - 3)):
        def store(f, q, value):
            part2_out.at[f, i][chunk(q)] = value

        step_row(
            store,
            lambda f, d, q: c1_out.at[f, j - 2][chunk(q)],
            x=(x_out.at[j], halo(merged1, j)),
            z=(level_in.at[j], rolled_levels(lambda f: c1_out[f, j - 2])),
        )


def boundary(*refs):
    rows, left, right, merged, y_in, level_in, x_in, c1_in, part1_in, c2_in, part2_in, edge_in = refs[:12]
    messages = refs[12:16]
    outs = refs[16:20]
    sides, corners, x_new, y_new, level_new, c1_new, merged1, beyond = refs[20:]
    lane = lanes()
    west_half = lane % G < HALO
    place = lax.axis_index("ns")
    last = lax.axis_size("ns") - 1
    odd = place % 2
    inside = {SOUTH: place > 0, NORTH: place < last}
    near = (-2, -1, 0, 1, R - 2, R - 1, R, R + 1)
    new_at = {j: i for i, j in enumerate(near)}
    for source, target in ((0, sides), (1, corners)):
        def unpack(b, carry):
            for message, side in ((messages[source], odd), (messages[source + 2], 1 - odd)):
                here = jnp.where(side == NORTH, place < last, place > 0)
                target[side, b] = jnp.where(here, message[b], 0.0)
            return carry

        lax.fori_loop(0, target.shape[1], unpack, 0, unroll=2)

    def row(f, j):
        if j < 0:
            return sides.at[SOUTH, ROWS_AT[f] + j + (2 if f == U else HALO)]
        if j >= R:
            return sides.at[NORTH, ROWS_AT[f] + j - R]
        return rows.at[f, j]

    for s in range(2):
        for f in range(FIELDS):
            south = turn(corners[SOUTH, s], W - 2 * G - 2 * G * f)
            north = turn(corners[NORTH, s], -2 * G * f)
            beyond[s, f] = jnp.where(lane >= W // 2, south, north)

    both = []
    for s, edges in enumerate((left, right)):
        across = edge_rows(edges, lambda f: beyond[s, f])
        both.append([edge_in[s, f] + a for f, a in enumerate(across)])
    for f in range(4):
        merged1[f] = jnp.where(west_half, both[0][f], both[1][f])

    def halo_beyond(f, j):
        return halo_columns(jnp.where(west_half, beyond[0, f], beyond[1, f]), j % R)

    for j in near:
        got = y_coefficients_at(row, j)
        for k in range(9):
            y_new[new_at[j], k] = got[k]
        if not 0 <= j < R:
            got = x_coefficients(
                row(U, j)[...], halo_beyond(U, j), row(M, j)[...], halo_beyond(M, j), lane
            )
            for k in range(9):
                x_new[new_at[j], k] = got[k]
            for k, value in enumerate(level_coefficients(row(M, j)[...])):
                level_new[new_at[j], k] = value

    for j in near:
        side = SOUTH if j < R // 2 else NORTH

        def store(f, q, value):
            if f >= 2 and not 0 <= j < R:
                value = jnp.where(inside[side], value, 0.0)
            c1_new.at[f, new_at[j]][chunk(q)] = value

        def load(f, d, q):
            return row(f, j + d)[chunk(q)]

        if 0 <= j < R:
            i = (0, 1, R - 2, R - 1).index(j)
            step_row(
                store, load, y=y_new.at[new_at[j]], base=lambda f, q: part1_in.at[f, i][chunk(q)]
            )
        else:
            halos = [halo_beyond(f, j) for f in range(4)]
            step_row(
                store,
                load,
                x=(x_new.at[new_at[j]], lambda f, q: halos[f][8 * q : 8 * q + 8]),
                y=y_new.at[new_at[j]],
                z=(level_new.at[new_at[j]], rolled_levels(lambda f: row(f, j)[...])),
            )

    def load1(f, j, q):
        if j in new_at:
            return c1_new.at[f, new_at[j]][chunk(q)]
        return c1_in.at[f, j - 2][chunk(q)]

    for j in (0, 1, 2, 3, R - 4, R - 3, R - 2, R - 1):
        def store(f, q, value):
            outs[f][pl.ds(8 * q * R + j, 8, stride=R), :] = value

        def load(f, d, q):
            return load1(f, j + d, q)

        if j in new_at:
            halos = [halo_columns(merged1[f], j) for f in range(4)]
            step_row(
                store,
                load,
                x=(x_in.at[j], lambda f, q: halos[f][8 * q : 8 * q + 8]),
                y=y_new.at[new_at[j]],
                z=(level_in.at[j], rolled_levels(lambda f: c1_new[f, new_at[j]])),
            )
        else:
            i = (2, 3, R - 4, R - 3).index(j)
            step_row(
                store, load, y=y_in.at[j - 2], base=lambda f, q: part2_in.at[f, i][chunk(q)]
            )

    def copy(j, carry):
        for f in range(4):
            outs[f][pl.ds(j, K, stride=R), :] = c2_in[f, j - 4]
        return carry

    lax.fori_loop(4, R - 4, copy, 0, unroll=2)


def vmem():
    return pl.BlockSpec(memory_space=pltpu.VMEM)


def call(kernel, in_specs, out_shapes, scratch=(), limit=16 * MIB, cost=0):
    return pl.pallas_call(
        kernel,
        out_shape=[jax.ShapeDtypeStruct(shape, F32) for shape in out_shapes],
        in_specs=in_specs,
        out_specs=[vmem()] * len(out_shapes),
        scratch_shapes=list(scratch),
        compiler_params=pltpu.CompilerParams(vmem_limit_bytes=limit),
        cost_estimate=pl.CostEstimate(flops=cost, bytes_accessed=MIB, transcendentals=0),
    )


def partners(odd, n_ew, n_ns):
    pairs = []
    for e in range(n_ew):
        for s in range(n_ns):
            step = 1 if (s - odd) % 2 == 0 else -1
            if 0 <= s + step < n_ns:
                to = (e, s + step)
            else:
                to = (e ^ 1 if e ^ 1 < n_ew else e, s)
            pairs.append((e * n_ns + s, to[0] * n_ns + to[1]))
    return pairs


def local(temp, salt, u_east, v_north, wet, cot_temp, cot_salt):
    flat = [a.reshape(K * R, W) for a in (temp, salt, cot_temp, cot_salt, u_east, v_north, wet)]

    row = (K, W)
    padded = ((K + 2) * R, W)
    rows, raw, own, to_east, to_west = call(
        pack_edges,
        [pl.BlockSpec(memory_space=pltpu.HBM)] * FIELDS,
        [(FIELDS, R) + row, (4,) + padded, (FIELDS,) + row, (PAIRS,) + row, (PAIRS,) + row],
        [
            pltpu.VMEM((2, K * R, W), F32),
            pltpu.VMEM((K * R, W), jnp.int32),
            pltpu.SemaphoreType.DMA((FIELDS,)),
        ],
    )(*[pltpu.with_memory_space_constraint(a, pltpu.HBM) for a in flat])

    n_ew, n_ns = lax.axis_size("ew"), lax.axis_size("ns")
    from_west = lax.ppermute(to_east, "ew", [(i, (i + 1) % n_ew) for i in range(n_ew)])
    from_east = lax.ppermute(to_west, "ew", [((i + 1) % n_ew, i) for i in range(n_ew)])

    def swap(odd, message):
        return lax.ppermute(message, ("ew", "ns"), partners(odd, n_ew, n_ns))

    first, second = call(pack_sides, [vmem()], [(SIDE_BLOCKS,) + row] * 2)(rows)
    second = swap(1, second)
    first = swap(0, first)

    y_in, level, base = call(
        prepare,
        [vmem()] * 2,
        [(R - 4, 9) + row, (R, 3) + row, (4, R - 4) + row],
        cost=10_000_000,
    )(rows, raw)

    left, right, merged, first_corners, second_corners = call(
        pack_corners,
        [vmem()] * 3 + [pl.BlockSpec(memory_space=pl.ANY)],
        [(FIELDS,) + row] * 3 + [(2,) + row] * 2,
    )(own, from_west, from_east, level)
    second_corners = swap(1, second_corners)
    first_corners = swap(0, first_corners)

    x_in, c1, part1, c2, part2, edge = call(
        interior,
        [vmem()] * 8,
        [(R, 9) + row, (4, R - 4) + row, (4, 4) + row, (4, R - 8) + row, (4, 4) + row, (2, 4) + row],
        [pltpu.VMEM((4,) + row, F32)],
        cost=10_000_000,
    )(rows, raw, left, right, merged, y_in, level, base)

    outs = call(
        boundary,
        [vmem()] * 16,
        [(K * R, W)] * 4,
        [
            pltpu.VMEM((2, SIDE_BLOCKS) + row, F32),
            pltpu.VMEM((2, 2) + row, F32),
            pltpu.VMEM((8, 9) + row, F32),
            pltpu.VMEM((8, 9) + row, F32),
            pltpu.VMEM((8, 3) + row, F32),
            pltpu.VMEM((4, 8) + row, F32),
            pltpu.VMEM((4,) + row, F32),
            pltpu.VMEM((2, FIELDS) + row, F32),
        ],
        cost=10_000_000,
    )(
        *(rows, left, right, merged, y_in, level, x_in, c1, part1, c2, part2, edge),
        *(second, second_corners, first, first_corners),
    )
    return tuple(a.reshape(K, R, W) for a in outs)


def solution(mesh):
    spec = P(None, "ns", "ew")
    return jax.shard_map(
        local, mesh=mesh, in_specs=(spec,) * 7, out_specs=(spec,) * 4, check_vma=False
    )
```

```python
import jax
import jax.numpy as jnp
from jax import lax
from jax.experimental import pallas as pl
from jax.experimental.pallas import tpu as pltpu
from jax.sharding import PartitionSpec as P

horizontal_mix = 0.05
vertical_mix = 0.2

F32 = jnp.float32
K = 32
R = 16
W = 128
G = W // R
HALO = 4
FIELDS = 7
U, V, M = 4, 5, 6
PAIRS = 4
SIDE_BLOCKS = 26
ROWS_AT = (0, 4, 8, 12, 24, 16, 20)
SOUTH, NORTH = 0, 1
MIB = 1 << 20


def lanes():
    return lax.broadcasted_iota(jnp.int32, (K, W), 1)


def turn(x, amount):
    return pltpu.roll(x, amount % W, 1)


def pack_edges(*refs):
    sources = refs[:FIELDS]
    rows, raw, own, to_east, to_west, raw_flow, raw_wet, arrived = refs[FIELDS:]
    copies = []
    for f in range(FIELDS):
        target = raw.at[f, pl.ds(R, K * R)] if f < 4 else raw_wet if f == M else raw_flow.at[f - U]
        copies.append(pltpu.make_async_copy(sources[f], target, arrived.at[f]))
        copies[-1].start()
    for f in range(4):
        raw[f, pl.ds(0, R)] = jnp.zeros((R, W), F32)
        raw[f, pl.ds((K + 1) * R, R)] = jnp.zeros((R, W), F32)
    lane = lanes()
    group = lane // G
    packed = []
    for f in range(FIELDS):
        copies[f].wait()
        source = raw.at[f] if f < 4 else raw_wet if f == M else raw_flow.at[f - U]
        edges = jnp.zeros((K, W), F32)
        for r in range(R):
            x = source[pl.ds(R + r if f < 4 else r, K, stride=R), :].astype(F32)
            rows[f, r] = x
            edges = jnp.where(group == r, turn(x, G * r + HALO), edges)
        own[f] = edges
        packed.append(edges)
    west_half = lane % G < HALO
    packed.append(jnp.zeros((K, W), F32))
    for p in range(PAIRS):
        a, b = packed[2 * p], packed[2 * p + 1]
        to_east[p] = jnp.where(west_half, a, turn(b, HALO))
        to_west[p] = jnp.where(west_half, turn(b, -HALO), a)


def pack_corners(own, from_west, from_east, _, left, right, merged, first, second):
    odd = lax.axis_index("ns") % 2
    lane = lanes()
    west_half = lane % G < HALO
    for f in range(FIELDS):
        a, b = from_west[f // 2], from_east[f // 2]
        if f % 2:
            a, b = turn(a, -HALO), turn(b, HALO)
        left_f = jnp.where(west_half, a, own[f])
        right_f = jnp.where(west_half, own[f], b)
        left[f] = left_f
        right[f] = right_f
        merged[f] = jnp.where(west_half, left_f, right_f)
    for out, north in ((first, 1 - odd), (second, odd)):
        for side, edges in enumerate((left, right)):
            block = jnp.zeros((K, W), F32)
            for f in range(FIELDS):
                amount = lax.rem(2 * G * f + W - (W - 2 * G) * north, W)
                moved = pltpu.roll(edges[f], amount, 1)
                block = jnp.where(lane // (2 * G) == f, moved, block)
            out[side] = block


def coefficients(speed, mask):
    opened = {d: mask[d] * mask[d + 1] for d in (-2, -1, 0, 1)}
    s = {d: speed[d] * opened[d] * (1.0 / 12.0) for d in opened}
    a = {d: jnp.abs(s[d]) for d in s}
    w0 = {d: -(s[d] + a[d]) for d in (-1, 0, 1)}
    w3 = {d: a[d] - s[d] for d in (-2, -1, 0)}
    w1, w2 = {}, {}
    for d in (-1, 0):
        even, odd = 7.0 * s[d], 3.0 * a[d] + horizontal_mix * opened[d]
        w1[d], w2[d] = even + odd, even - odd
    forward = [w0[-1], w1[-1] - w0[0], w3[-1] - w2[0], -w3[0]]
    transposed = [-w3[-2], w3[-2] - w2[-1], w1[0] - w0[1], w0[1]]
    return forward + transposed + [w2[-1] - w1[0]]


def shifted(c, h, d, lane, step=1):
    if d == 0:
        return c
    if d > 0:
        return turn(jnp.where(lane < step * d, h, c), -step * d)
    return turn(jnp.where(lane >= W + step * d, h, c), -step * d)


def x_coefficients(u, uh, m, mh, lane):
    return coefficients(
        {d: shifted(u, uh, d, lane) for d in (-2, -1, 0, 1)},
        {d: shifted(m, mh, d, lane) for d in (-2, -1, 0, 1, 2)},
    )


def level_coefficients(m):
    inner = lax.broadcasted_iota(jnp.int32, (K, W), 0) < K - 1
    after = jnp.where(inner, vertical_mix * m * pltpu.roll(m, K - 1, 0), 0.0)
    before = pltpu.roll(after, 1, 0)
    return after, before, 1.0 - after - before


def chunk(q):
    return pl.ds(8 * q, 8)


def strided(q, j, stride, shift=0):
    return pl.ds((8 * q + 1 + shift) * stride + j, 8, stride=stride)


def step_row(store, load, x=None, y=None, z=None, base=None):
    lane = lanes()[:8]
    results = []
    for q in range(K // 8):
        part = chunk(q)
        centre = None
        for term in (x and x[0].at[8], y and y.at[8], z and z[0].at[2]):
            if term is not None:
                centre = term[part] if centre is None else centre + term[part]
        if z:
            after, before = z[0].at[0][part], z[0].at[1][part]
        for direction in (0, 1):
            ks = range(4 * direction, 4 * direction + 4)
            xs = [x[0].at[k][part] for k in ks] if x else []
            ys = [y.at[k][part] for k in ks] if y else []
            for f in (2 * direction, 2 * direction + 1):
                c = load(f, 0, q)
                total = centre * c
                if base:
                    total += base(f, q)
                if x:
                    h = x[1](f, q)
                for coefficient, d in zip(xs, (-2, -1, 1, 2)):
                    total += coefficient * shifted(c, h, d, lane)
                for coefficient, d in zip(ys, (-2, -1, 1, 2)):
                    total += coefficient * load(f, d, q)
                if z:
                    c_after, c_before = z[1](f, q)
                    total += after * c_after + before * c_before
                results.append((f, q, total))
    for result in results:
        store(*result)


def halo_columns(merged, j):
    return pltpu.roll(merged, lax.rem(2 * W - HALO - G * j, W), 1)


def edge_columns_and_levels(edges):
    u, m = edges[U], edges[M]
    xs = coefficients(
        {d: turn(u, -d) for d in (-2, -1, 0, 1)},
        {d: turn(m, -d) for d in (-2, -1, 0, 1, 2)},
    )
    after, before, centre = level_coefficients(m)
    results = []
    for f in range(4):
        c = edges[f]
        total = (centre + xs[8]) * c
        total += after * pltpu.roll(c, K - 1, 0) + before * pltpu.roll(c, 1, 0)
        for coefficient, d in zip(xs[4 * (f // 2) :], (-2, -1, 1, 2)):
            total += coefficient * turn(c, -d)
        results.append(total)
    return results


def edge_rows(edges, beyond):
    lane = lanes()
    v, m = edges[V], edges[M]
    vh, mh = beyond(V), beyond(M)
    ys = coefficients(
        {d: shifted(v, vh, d, lane, G) for d in (-2, -1, 0, 1)},
        {d: shifted(m, mh, d, lane, G) for d in (-2, -1, 0, 1, 2)},
    )
    results = []
    for f in range(4):
        c, ch = edges[f], beyond(f)
        total = ys[8] * c
        for coefficient, d in zip(ys[4 * (f // 2) :], (-2, -1, 1, 2)):
            total += coefficient * shifted(c, ch, d, lane, G)
        results.append(total)
    return results


def y_coefficients_at(row, j):
    return coefficients(
        {d: row(V, j + d)[...] for d in (-2, -1, 0, 1)},
        {d: row(M, j + d)[...] for d in (-2, -1, 0, 1, 2)},
    )


def by_fours(start, stop, body):
    def four(i, carry):
        for k in range(4):
            body(start + 4 * i + k)
        return carry

    lax.fori_loop(0, (stop - start) // 4, four, 0)


def raw_levels(raw, j):
    return lambda f, q: (raw.at[f][strided(q, j, R, 1), :], raw.at[f][strided(q, j, R, -1), :])


def rolled_levels(load):
    after = [pltpu.roll(load(f), K - 1, 0) for f in range(4)]
    before = [pltpu.roll(load(f), 1, 0) for f in range(4)]
    return lambda f, q: (after[f][8 * q : 8 * q + 8], before[f][8 * q : 8 * q + 8])


def pack_sides(rows, first, second):
    odd = lax.axis_index("ns") % 2
    for out, north in ((first, 1 - odd), (second, odd)):
        for f in range(FIELDS):
            count = 2 if f == U else HALO
            start = (R - count) * north
            for r in range(count):
                out[ROWS_AT[f] + r] = rows[f, start + r]


def prepare(rows, raw, y_out, level_out, base_out, first_out, second_out):
    pack_sides(rows, first_out, second_out)

    def levels(j):
        for k, value in enumerate(level_coefficients(rows[M, j])):
            level_out[j, k] = value

    by_fours(0, R, levels)

    def across(j):
        got = y_coefficients_at(lambda f, r: rows.at[f, r], j)
        for k in range(9):
            y_out[j - 2, k] = got[k]

    by_fours(2, R - 2, across)

    def first(j):
        def store(f, q, value):
            base_out.at[f, j - 2][chunk(q)] = value

        step_row(
            store,
            lambda f, d, q: rows.at[f, j + d][chunk(q)],
            y=y_out.at[j - 2],
            z=(level_out.at[j], raw_levels(raw, j)),
        )

    by_fours(2, R - 2, first)


def interior(*refs):
    rows, raw, left, right, merged, y_in, level_in, base_in = refs[:8]
    x_out, c1_out, part1_out, c2_out, part2_out, edge_out, merged1 = refs[8:]
    lane = lanes()
    west_half = lane % G < HALO
    def x_body(j):
        got = x_coefficients(
            rows[U, j], halo_columns(merged[U], j), rows[M, j], halo_columns(merged[M], j), lane
        )
        for k in range(9):
            x_out[j, k] = got[k]

    for j in range(R):
        x_body(j)

    both = []
    for side, edges in enumerate((left, right)):
        partial = edge_columns_and_levels(edges)
        across = edge_rows(edges, lambda f: edges[f])
        for f in range(4):
            edge_out[side, f] = partial[f]
        both.append([p + a for p, a in zip(partial, across)])
    for f in range(4):
        merged1[f] = jnp.where(west_half, both[0][f], both[1][f])

    def halo(source, j):
        halos = [halo_columns(source[f], j) for f in range(4)]
        return lambda f, q: halos[f][8 * q : 8 * q + 8]

    def first(j):
        def store(f, q, value):
            c1_out.at[f, j - 2][chunk(q)] = value

        step_row(
            store,
            lambda f, d, q: rows.at[f, j][chunk(q)],
            x=(x_out.at[j], halo(merged, j)),
            base=lambda f, q: base_in.at[f, j - 2][chunk(q)],
        )

    for j in range(2, R - 2):
        first(j)

    for i, j in enumerate((0, 1, R - 2, R - 1)):
        def store(f, q, value):
            part1_out.at[f, i][chunk(q)] = value

        step_row(
            store,
            lambda f, d, q: rows.at[f, j][chunk(q)],
            x=(x_out.at[j], halo(merged, j)),
            z=(level_in.at[j], raw_levels(raw, j)),
        )

    def second(j):
        def store(f, q, value):
            c2_out.at[f, j - 4][chunk(q)] = value

        step_row(
            store,
            lambda f, d, q: c1_out.at[f, j - 2 + d][chunk(q)],
            x=(x_out.at[j], halo(merged1, j)),
            y=y_in.at[j - 2],
            z=(level_in.at[j], rolled_levels(lambda f: c1_out[f, j - 2])),
        )

    for j in range(4, R - 4):
        second(j)

    for i, j in enumerate((2, 3, R - 4, R - 3)):
        def store(f, q, value):
            part2_out.at[f, i][chunk(q)] = value

        step_row(
            store,
            lambda f, d, q: c1_out.at[f, j - 2][chunk(q)],
            x=(x_out.at[j], halo(merged1, j)),
            z=(level_in.at[j], rolled_levels(lambda f: c1_out[f, j - 2])),
        )


def boundary(*refs):
    rows, left, right, merged, y_in, level_in, x_in, c1_in, part1_in, c2_in, part2_in, edge_in = refs[:12]
    messages = refs[12:16]
    outs = refs[16:20]
    sides, corners, x_new, y_new, level_new, c1_new, merged1, beyond = refs[20:]
    lane = lanes()
    west_half = lane % G < HALO
    place = lax.axis_index("ns")
    last = lax.axis_size("ns") - 1
    odd = place % 2
    inside = {SOUTH: place > 0, NORTH: place < last}
    near = (-2, -1, 0, 1, R - 2, R - 1, R, R + 1)
    new_at = {j: i for i, j in enumerate(near)}
    for source, target in ((0, sides), (1, corners)):
        def unpack(b, carry):
            for message, side in ((messages[source], odd), (messages[source + 2], 1 - odd)):
                here = jnp.where(side == NORTH, place < last, place > 0)
                target[side, b] = jnp.where(here, message[b], 0.0)
            return carry

        lax.fori_loop(0, target.shape[1], unpack, 0, unroll=2)

    def row(f, j):
        if j < 0:
            return sides.at[SOUTH, ROWS_AT[f] + j + (2 if f == U else HALO)]
        if j >= R:
            return sides.at[NORTH, ROWS_AT[f] + j - R]
        return rows.at[f, j]

    for s in range(2):
        for f in range(FIELDS):
            south = turn(corners[SOUTH, s], W - 2 * G - 2 * G * f)
            north = turn(corners[NORTH, s], -2 * G * f)
            beyond[s, f] = jnp.where(lane >= W // 2, south, north)

    both = []
    for s, edges in enumerate((left, right)):
        across = edge_rows(edges, lambda f: beyond[s, f])
        both.append([edge_in[s, f] + a for f, a in enumerate(across)])
    for f in range(4):
        merged1[f] = jnp.where(west_half, both[0][f], both[1][f])

    def halo_beyond(f, j):
        return halo_columns(jnp.where(west_half, beyond[0, f], beyond[1, f]), j % R)

    for j in near:
        got = y_coefficients_at(row, j)
        for k in range(9):
            y_new[new_at[j], k] = got[k]
        if not 0 <= j < R:
            got = x_coefficients(
                row(U, j)[...], halo_beyond(U, j), row(M, j)[...], halo_beyond(M, j), lane
            )
            for k in range(9):
                x_new[new_at[j], k] = got[k]
            for k, value in enumerate(level_coefficients(row(M, j)[...])):
                level_new[new_at[j], k] = value

    for j in near:
        side = SOUTH if j < R // 2 else NORTH

        def store(f, q, value):
            if f >= 2 and not 0 <= j < R:
                value = jnp.where(inside[side], value, 0.0)
            c1_new.at[f, new_at[j]][chunk(q)] = value

        def load(f, d, q):
            return row(f, j + d)[chunk(q)]

        if 0 <= j < R:
            i = (0, 1, R - 2, R - 1).index(j)
            step_row(
                store, load, y=y_new.at[new_at[j]], base=lambda f, q: part1_in.at[f, i][chunk(q)]
            )
        else:
            halos = [halo_beyond(f, j) for f in range(4)]
            step_row(
                store,
                load,
                x=(x_new.at[new_at[j]], lambda f, q: halos[f][8 * q : 8 * q + 8]),
                y=y_new.at[new_at[j]],
                z=(level_new.at[new_at[j]], rolled_levels(lambda f: row(f, j)[...])),
            )

    def load1(f, j, q):
        if j in new_at:
            return c1_new.at[f, new_at[j]][chunk(q)]
        return c1_in.at[f, j - 2][chunk(q)]

    for j in (0, 1, 2, 3, R - 4, R - 3, R - 2, R - 1):
        def store(f, q, value):
            outs[f][pl.ds(8 * q * R + j, 8, stride=R), :] = value

        def load(f, d, q):
            return load1(f, j + d, q)

        if j in new_at:
            halos = [halo_columns(merged1[f], j) for f in range(4)]
            step_row(
                store,
                load,
                x=(x_in.at[j], lambda f, q: halos[f][8 * q : 8 * q + 8]),
                y=y_new.at[new_at[j]],
                z=(level_in.at[j], rolled_levels(lambda f: c1_new[f, new_at[j]])),
            )
        else:
            i = (2, 3, R - 4, R - 3).index(j)
            step_row(
                store, load, y=y_in.at[j - 2], base=lambda f, q: part2_in.at[f, i][chunk(q)]
            )

    def copy(j, carry):
        for f in range(4):
            outs[f][pl.ds(j, K, stride=R), :] = c2_in[f, j - 4]
        return carry

    lax.fori_loop(4, R - 4, copy, 0, unroll=2)


def vmem():
    return pl.BlockSpec(memory_space=pltpu.VMEM)


def call(kernel, in_specs, out_shapes, scratch=(), limit=16 * MIB, cost=0):
    return pl.pallas_call(
        kernel,
        out_shape=[jax.ShapeDtypeStruct(shape, F32) for shape in out_shapes],
        in_specs=in_specs,
        out_specs=[vmem()] * len(out_shapes),
        scratch_shapes=list(scratch),
        compiler_params=pltpu.CompilerParams(vmem_limit_bytes=limit),
        cost_estimate=pl.CostEstimate(flops=cost, bytes_accessed=MIB, transcendentals=0),
    )


def partners(odd, n_ew, n_ns):
    pairs = []
    for e in range(n_ew):
        for s in range(n_ns):
            step = 1 if (s - odd) % 2 == 0 else -1
            if 0 <= s + step < n_ns:
                to = (e, s + step)
            else:
                to = (e ^ 1 if e ^ 1 < n_ew else e, s)
            pairs.append((e * n_ns + s, to[0] * n_ns + to[1]))
    return pairs


def local(temp, salt, u_east, v_north, wet, cot_temp, cot_salt):
    flat = [a.reshape(K * R, W) for a in (temp, salt, cot_temp, cot_salt, u_east, v_north, wet)]

    row = (K, W)
    padded = ((K + 2) * R, W)
    rows, raw, own, to_east, to_west = call(
        pack_edges,
        [pl.BlockSpec(memory_space=pltpu.HBM)] * FIELDS,
        [(FIELDS, R) + row, (4,) + padded, (FIELDS,) + row, (PAIRS,) + row, (PAIRS,) + row],
        [
            pltpu.VMEM((2, K * R, W), F32),
            pltpu.VMEM((K * R, W), jnp.int32),
            pltpu.SemaphoreType.DMA((FIELDS,)),
        ],
    )(*[pltpu.with_memory_space_constraint(a, pltpu.HBM) for a in flat])

    n_ew, n_ns = lax.axis_size("ew"), lax.axis_size("ns")
    from_west = lax.ppermute(to_east, "ew", [(i, (i + 1) % n_ew) for i in range(n_ew)])
    from_east = lax.ppermute(to_west, "ew", [((i + 1) % n_ew, i) for i in range(n_ew)])

    def swap(odd, message):
        return lax.ppermute(message, ("ew", "ns"), partners(odd, n_ew, n_ns))

    y_in, level, base, first, second = call(
        prepare,
        [vmem()] * 2,
        [(R - 4, 9) + row, (R, 3) + row, (4, R - 4) + row] + [(SIDE_BLOCKS,) + row] * 2,
        cost=10_000_000,
    )(rows, raw)
    second = swap(1, second)
    first = swap(0, first)

    left, right, merged, first_corners, second_corners = call(
        pack_corners,
        [vmem()] * 3 + [pl.BlockSpec(memory_space=pl.ANY)],
        [(FIELDS,) + row] * 3 + [(2,) + row] * 2,
    )(own, from_west, from_east, level)
    second_corners = swap(1, second_corners)
    first_corners = swap(0, first_corners)

    x_in, c1, part1, c2, part2, edge = call(
        interior,
        [vmem()] * 8,
        [(R, 9) + row, (4, R - 4) + row, (4, 4) + row, (4, R - 8) + row, (4, 4) + row, (2, 4) + row],
        [pltpu.VMEM((4,) + row, F32)],
        cost=10_000_000,
    )(rows, raw, left, right, merged, y_in, level, base)

    outs = call(
        boundary,
        [vmem()] * 16,
        [(K * R, W)] * 4,
        [
            pltpu.VMEM((2, SIDE_BLOCKS) + row, F32),
            pltpu.VMEM((2, 2) + row, F32),
            pltpu.VMEM((8, 9) + row, F32),
            pltpu.VMEM((8, 9) + row, F32),
            pltpu.VMEM((8, 3) + row, F32),
            pltpu.VMEM((4, 8) + row, F32),
            pltpu.VMEM((4,) + row, F32),
            pltpu.VMEM((2, FIELDS) + row, F32),
        ],
        cost=10_000_000,
    )(
        *(rows, left, right, merged, y_in, level, x_in, c1, part1, c2, part2, edge),
        *(second, second_corners, first, first_corners),
    )
    return tuple(a.reshape(K, R, W) for a in outs)


def solution(mesh):
    spec = P(None, "ns", "ew")
    return jax.shard_map(
        local, mesh=mesh, in_specs=(spec,) * 7, out_specs=(spec,) * 4, check_vma=False
    )
```

```python
import jax
import jax.numpy as jnp
from jax import lax
from jax.experimental import pallas as pl
from jax.experimental.pallas import tpu as pltpu
from jax.sharding import PartitionSpec as P

horizontal_mix = 0.05
vertical_mix = 0.2

F32 = jnp.float32
K = 32
R = 16
W = 128
G = W // R
HALO = 4
FIELDS = 7
U, V, M = 4, 5, 6
PAIRS = 4
SIDE_BLOCKS = 28
ROWS_AT = (0, 4, 8, 12, 24, 16, 20)
CORNERS_AT = 26
SOUTH, NORTH = 0, 1
MIB = 1 << 20


def lanes():
    return lax.broadcasted_iota(jnp.int32, (K, W), 1)


def turn(x, amount):
    return pltpu.roll(x, amount % W, 1)


def pack_edges(*refs):
    sources = refs[:FIELDS]
    rows, raw, own, to_east, to_west, raw_flow, raw_wet, arrived = refs[FIELDS:]
    copies = []
    for f in range(FIELDS):
        target = raw.at[f, pl.ds(R, K * R)] if f < 4 else raw_wet if f == M else raw_flow.at[f - U]
        copies.append(pltpu.make_async_copy(sources[f], target, arrived.at[f]))
        copies[-1].start()
    for f in range(4):
        raw[f, pl.ds(0, R)] = jnp.zeros((R, W), F32)
        raw[f, pl.ds((K + 1) * R, R)] = jnp.zeros((R, W), F32)
    lane = lanes()
    group = lane // G
    packed = []
    for f in range(FIELDS):
        copies[f].wait()
        source = raw.at[f] if f < 4 else raw_wet if f == M else raw_flow.at[f - U]
        edges = jnp.zeros((K, W), F32)
        for r in range(R):
            x = source[pl.ds(R + r if f < 4 else r, K, stride=R), :].astype(F32)
            rows[f, r] = x
            edges = jnp.where(group == r, turn(x, G * r + HALO), edges)
        own[f] = edges
        packed.append(edges)
    west_half = lane % G < HALO
    packed.append(jnp.zeros((K, W), F32))
    for p in range(PAIRS):
        a, b = packed[2 * p], packed[2 * p + 1]
        to_east[p] = jnp.where(west_half, a, turn(b, HALO))
        to_west[p] = jnp.where(west_half, turn(b, -HALO), a)


def pack_sides(rows, own, from_west, from_east, _, left, right, merged, second, first):
    odd = lax.axis_index("ns") % 2
    lane = lanes()
    west_half = lane % G < HALO
    for f in range(FIELDS):
        a, b = from_west[f // 2], from_east[f // 2]
        if f % 2:
            a, b = turn(a, -HALO), turn(b, HALO)
        left_f = jnp.where(west_half, a, own[f])
        right_f = jnp.where(west_half, own[f], b)
        left[f] = left_f
        right[f] = right_f
        merged[f] = jnp.where(west_half, left_f, right_f)
    for out, north in ((second, odd), (first, 1 - odd)):
        for f in range(FIELDS):
            count = 2 if f == U else HALO
            start = (R - count) * north
            for r in range(count):
                out[ROWS_AT[f] + r] = rows[f, start + r]
        for side, edges in enumerate((left, right)):
            block = jnp.zeros((K, W), F32)
            for f in range(FIELDS):
                amount = lax.rem(2 * G * f + W - (W - 2 * G) * north, W)
                moved = pltpu.roll(edges[f], amount, 1)
                block = jnp.where(lane // (2 * G) == f, moved, block)
            out[CORNERS_AT + side] = block


def coefficients(speed, mask):
    opened = {d: mask[d] * mask[d + 1] for d in (-2, -1, 0, 1)}
    s = {d: speed[d] * opened[d] * (1.0 / 12.0) for d in opened}
    a = {d: jnp.abs(s[d]) for d in s}
    w0 = {d: -(s[d] + a[d]) for d in (-1, 0, 1)}
    w3 = {d: a[d] - s[d] for d in (-2, -1, 0)}
    w1, w2 = {}, {}
    for d in (-1, 0):
        even, odd = 7.0 * s[d], 3.0 * a[d] + horizontal_mix * opened[d]
        w1[d], w2[d] = even + odd, even - odd
    forward = [w0[-1], w1[-1] - w0[0], w3[-1] - w2[0], -w3[0]]
    transposed = [-w3[-2], w3[-2] - w2[-1], w1[0] - w0[1], w0[1]]
    return forward + transposed + [w2[-1] - w1[0]]


def shifted(c, h, d, lane, step=1):
    if d == 0:
        return c
    if d > 0:
        return turn(jnp.where(lane < step * d, h, c), -step * d)
    return turn(jnp.where(lane >= W + step * d, h, c), -step * d)


def x_coefficients(u, uh, m, mh, lane):
    return coefficients(
        {d: shifted(u, uh, d, lane) for d in (-2, -1, 0, 1)},
        {d: shifted(m, mh, d, lane) for d in (-2, -1, 0, 1, 2)},
    )


def level_coefficients(m):
    inner = lax.broadcasted_iota(jnp.int32, (K, W), 0) < K - 1
    after = jnp.where(inner, vertical_mix * m * pltpu.roll(m, K - 1, 0), 0.0)
    before = pltpu.roll(after, 1, 0)
    return after, before, 1.0 - after - before


def chunk(q):
    return pl.ds(8 * q, 8)


def strided(q, j, stride, shift=0):
    return pl.ds((8 * q + 1 + shift) * stride + j, 8, stride=stride)


def step_row(store, load, x=None, y=None, z=None, base=None):
    lane = lanes()[:8]
    results = []
    for q in range(K // 8):
        part = chunk(q)
        centre = None
        for term in (x and x[0].at[8], y and y.at[8], z and z[0].at[2]):
            if term is not None:
                centre = term[part] if centre is None else centre + term[part]
        if z:
            after, before = z[0].at[0][part], z[0].at[1][part]
        for direction in (0, 1):
            ks = range(4 * direction, 4 * direction + 4)
            xs = [x[0].at[k][part] for k in ks] if x else []
            ys = [y.at[k][part] for k in ks] if y else []
            for f in (2 * direction, 2 * direction + 1):
                c = load(f, 0, q)
                total = centre * c
                if base:
                    total += base(f, q)
                if x:
                    h = x[1](f, q)
                for coefficient, d in zip(xs, (-2, -1, 1, 2)):
                    total += coefficient * shifted(c, h, d, lane)
                for coefficient, d in zip(ys, (-2, -1, 1, 2)):
                    total += coefficient * load(f, d, q)
                if z:
                    c_after, c_before = z[1](f, q)
                    total += after * c_after + before * c_before
                results.append((f, q, total))
    for result in results:
        store(*result)


def halo_columns(merged, j):
    return pltpu.roll(merged, lax.rem(2 * W - HALO - G * j, W), 1)


def edge_columns_and_levels(edges):
    u, m = edges[U], edges[M]
    xs = coefficients(
        {d: turn(u, -d) for d in (-2, -1, 0, 1)},
        {d: turn(m, -d) for d in (-2, -1, 0, 1, 2)},
    )
    after, before, centre = level_coefficients(m)
    results = []
    for f in range(4):
        c = edges[f]
        total = (centre + xs[8]) * c
        total += after * pltpu.roll(c, K - 1, 0) + before * pltpu.roll(c, 1, 0)
        for coefficient, d in zip(xs[4 * (f // 2) :], (-2, -1, 1, 2)):
            total += coefficient * turn(c, -d)
        results.append(total)
    return results


def edge_rows(edges, beyond):
    lane = lanes()
    v, m = edges[V], edges[M]
    vh, mh = beyond(V), beyond(M)
    ys = coefficients(
        {d: shifted(v, vh, d, lane, G) for d in (-2, -1, 0, 1)},
        {d: shifted(m, mh, d, lane, G) for d in (-2, -1, 0, 1, 2)},
    )
    results = []
    for f in range(4):
        c, ch = edges[f], beyond(f)
        total = ys[8] * c
        for coefficient, d in zip(ys[4 * (f // 2) :], (-2, -1, 1, 2)):
            total += coefficient * shifted(c, ch, d, lane, G)
        results.append(total)
    return results


def y_coefficients_at(row, j):
    return coefficients(
        {d: row(V, j + d)[...] for d in (-2, -1, 0, 1)},
        {d: row(M, j + d)[...] for d in (-2, -1, 0, 1, 2)},
    )


def by_fours(start, stop, body):
    def four(i, carry):
        for k in range(4):
            body(start + 4 * i + k)
        return carry

    lax.fori_loop(0, (stop - start) // 4, four, 0)


def raw_levels(raw, j):
    return lambda f, q: (raw.at[f][strided(q, j, R, 1), :], raw.at[f][strided(q, j, R, -1), :])


def rolled_levels(load):
    after = [pltpu.roll(load(f), K - 1, 0) for f in range(4)]
    before = [pltpu.roll(load(f), 1, 0) for f in range(4)]
    return lambda f, q: (after[f][8 * q : 8 * q + 8], before[f][8 * q : 8 * q + 8])


def prepare(rows, raw, y_out, level_out, base_out):
    def levels(j):
        for k, value in enumerate(level_coefficients(rows[M, j])):
            level_out[j, k] = value

    by_fours(0, R, levels)

    def across(j):
        got = y_coefficients_at(lambda f, r: rows.at[f, r], j)
        for k in range(9):
            y_out[j - 2, k] = got[k]

    by_fours(2, R - 2, across)

    def first(j):
        def store(f, q, value):
            base_out.at[f, j - 2][chunk(q)] = value

        step_row(
            store,
            lambda f, d, q: rows.at[f, j + d][chunk(q)],
            y=y_out.at[j - 2],
            z=(level_out.at[j], raw_levels(raw, j)),
        )

    by_fours(2, R - 2, first)


def interior(*refs):
    rows, raw, left, right, merged, y_in, level_in, base_in = refs[:8]
    x_out, c1_out, part1_out, c2_out, part2_out, edge_out, merged1 = refs[8:]
    lane = lanes()
    west_half = lane % G < HALO
    def x_body(j):
        got = x_coefficients(
            rows[U, j], halo_columns(merged[U], j), rows[M, j], halo_columns(merged[M], j), lane
        )
        for k in range(9):
            x_out[j, k] = got[k]

    by_fours(0, R, x_body)

    both = []
    for side, edges in enumerate((left, right)):
        partial = edge_columns_and_levels(edges)
        across = edge_rows(edges, lambda f: edges[f])
        for f in range(4):
            edge_out[side, f] = partial[f]
        both.append([p + a for p, a in zip(partial, across)])
    for f in range(4):
        merged1[f] = jnp.where(west_half, both[0][f], both[1][f])

    def halo(source, j):
        halos = [halo_columns(source[f], j) for f in range(4)]
        return lambda f, q: halos[f][8 * q : 8 * q + 8]

    def first(j):
        def store(f, q, value):
            c1_out.at[f, j - 2][chunk(q)] = value

        step_row(
            store,
            lambda f, d, q: rows.at[f, j][chunk(q)],
            x=(x_out.at[j], halo(merged, j)),
            base=lambda f, q: base_in.at[f, j - 2][chunk(q)],
        )

    by_fours(2, R - 2, first)

    for i, j in enumerate((0, 1, R - 2, R - 1)):
        def store(f, q, value):
            part1_out.at[f, i][chunk(q)] = value

        step_row(
            store,
            lambda f, d, q: rows.at[f, j][chunk(q)],
            x=(x_out.at[j], halo(merged, j)),
            z=(level_in.at[j], raw_levels(raw, j)),
        )

    def second(j):
        def store(f, q, value):
            c2_out.at[f, j - 4][chunk(q)] = value

        step_row(
            store,
            lambda f, d, q: c1_out.at[f, j - 2 + d][chunk(q)],
            x=(x_out.at[j], halo(merged1, j)),
            y=y_in.at[j - 2],
            z=(level_in.at[j], rolled_levels(lambda f: c1_out[f, j - 2])),
        )

    by_fours(4, R - 4, second)

    for i, j in enumerate((2, 3, R - 4, R - 3)):
        def store(f, q, value):
            part2_out.at[f, i][chunk(q)] = value

        step_row(
            store,
            lambda f, d, q: c1_out.at[f, j - 2][chunk(q)],
            x=(x_out.at[j], halo(merged1, j)),
            z=(level_in.at[j], rolled_levels(lambda f: c1_out[f, j - 2])),
        )


def boundary(*refs):
    rows, left, right, merged, y_in, level_in, x_in, c1_in, part1_in, c2_in, part2_in, edge_in = refs[:12]
    second, first = refs[12:14]
    outs = refs[14:18]
    sides, x_new, y_new, level_new, c1_new, merged1, beyond = refs[18:]
    lane = lanes()
    west_half = lane % G < HALO
    place = lax.axis_index("ns")
    last = lax.axis_size("ns") - 1
    odd = place % 2
    inside = {SOUTH: place > 0, NORTH: place < last}
    near = (-2, -1, 0, 1, R - 2, R - 1, R, R + 1)
    new_at = {j: i for i, j in enumerate(near)}
    def unpack(b, carry):
        for message, side in ((second, odd), (first, 1 - odd)):
            here = jnp.where(side == NORTH, place < last, place > 0)
            sides[side, b] = jnp.where(here, message[b], 0.0)
        return carry

    lax.fori_loop(0, SIDE_BLOCKS, unpack, 0, unroll=2)

    def row(f, j):
        if j < 0:
            return sides.at[SOUTH, ROWS_AT[f] + j + (2 if f == U else HALO)]
        if j >= R:
            return sides.at[NORTH, ROWS_AT[f] + j - R]
        return rows.at[f, j]

    for s in range(2):
        for f in range(FIELDS):
            south = turn(sides[SOUTH, CORNERS_AT + s], W - 2 * G - 2 * G * f)
            north = turn(sides[NORTH, CORNERS_AT + s], -2 * G * f)
            beyond[s, f] = jnp.where(lane >= W // 2, south, north)

    both = []
    for s, edges in enumerate((left, right)):
        across = edge_rows(edges, lambda f: beyond[s, f])
        both.append([edge_in[s, f] + a for f, a in enumerate(across)])
    for f in range(4):
        merged1[f] = jnp.where(west_half, both[0][f], both[1][f])

    def halo_beyond(f, j):
        return halo_columns(jnp.where(west_half, beyond[0, f], beyond[1, f]), j % R)

    for j in near:
        got = y_coefficients_at(row, j)
        for k in range(9):
            y_new[new_at[j], k] = got[k]
        if not 0 <= j < R:
            got = x_coefficients(
                row(U, j)[...], halo_beyond(U, j), row(M, j)[...], halo_beyond(M, j), lane
            )
            for k in range(9):
                x_new[new_at[j], k] = got[k]
            for k, value in enumerate(level_coefficients(row(M, j)[...])):
                level_new[new_at[j], k] = value

    for j in near:
        side = SOUTH if j < R // 2 else NORTH

        def store(f, q, value):
            if f >= 2 and not 0 <= j < R:
                value = jnp.where(inside[side], value, 0.0)
            c1_new.at[f, new_at[j]][chunk(q)] = value

        def load(f, d, q):
            return row(f, j + d)[chunk(q)]

        if 0 <= j < R:
            i = (0, 1, R - 2, R - 1).index(j)
            step_row(
                store, load, y=y_new.at[new_at[j]], base=lambda f, q: part1_in.at[f, i][chunk(q)]
            )
        else:
            halos = [halo_beyond(f, j) for f in range(4)]
            step_row(
                store,
                load,
                x=(x_new.at[new_at[j]], lambda f, q: halos[f][8 * q : 8 * q + 8]),
                y=y_new.at[new_at[j]],
                z=(level_new.at[new_at[j]], rolled_levels(lambda f: row(f, j)[...])),
            )

    def load1(f, j, q):
        if j in new_at:
            return c1_new.at[f, new_at[j]][chunk(q)]
        return c1_in.at[f, j - 2][chunk(q)]

    for j in (0, 1, 2, 3, R - 4, R - 3, R - 2, R - 1):
        def store(f, q, value):
            outs[f][pl.ds(8 * q * R + j, 8, stride=R), :] = value

        def load(f, d, q):
            return load1(f, j + d, q)

        if j in new_at:
            halos = [halo_columns(merged1[f], j) for f in range(4)]
            step_row(
                store,
                load,
                x=(x_in.at[j], lambda f, q: halos[f][8 * q : 8 * q + 8]),
                y=y_new.at[new_at[j]],
                z=(level_in.at[j], rolled_levels(lambda f: c1_new[f, new_at[j]])),
            )
        else:
            i = (2, 3, R - 4, R - 3).index(j)
            step_row(
                store, load, y=y_in.at[j - 2], base=lambda f, q: part2_in.at[f, i][chunk(q)]
            )

    def copy(j, carry):
        for f in range(4):
            outs[f][pl.ds(j, K, stride=R), :] = c2_in[f, j - 4]
        return carry

    lax.fori_loop(4, R - 4, copy, 0, unroll=2)


def vmem():
    return pl.BlockSpec(memory_space=pltpu.VMEM)


def call(kernel, in_specs, out_shapes, scratch=(), limit=16 * MIB, cost=0.0):
    return pl.pallas_call(
        kernel,
        out_shape=[jax.ShapeDtypeStruct(shape, F32) for shape in out_shapes],
        in_specs=in_specs,
        out_specs=[vmem()] * len(out_shapes),
        scratch_shapes=list(scratch),
        compiler_params=pltpu.CompilerParams(vmem_limit_bytes=limit),
        cost_estimate=pl.CostEstimate(flops=0, bytes_accessed=int(cost * MIB), transcendentals=0),
    )


def partners(odd, n_ew, n_ns):
    pairs = []
    for e in range(n_ew):
        for s in range(n_ns):
            step = 1 if (s - odd) % 2 == 0 else -1
            if 0 <= s + step < n_ns:
                to = (e, s + step)
            else:
                to = (e ^ 1 if e ^ 1 < n_ew else e, s)
            pairs.append((e * n_ns + s, to[0] * n_ns + to[1]))
    return pairs


def local(temp, salt, u_east, v_north, wet, cot_temp, cot_salt):
    flat = [a.reshape(K * R, W) for a in (temp, salt, cot_temp, cot_salt, u_east, v_north, wet)]

    row = (K, W)
    padded = ((K + 2) * R, W)
    rows, raw, own, to_east, to_west = call(
        pack_edges,
        [pl.BlockSpec(memory_space=pltpu.HBM)] * FIELDS,
        [(FIELDS, R) + row, (4,) + padded, (FIELDS,) + row, (PAIRS,) + row, (PAIRS,) + row],
        [
            pltpu.VMEM((2, K * R, W), F32),
            pltpu.VMEM((K * R, W), jnp.int32),
            pltpu.SemaphoreType.DMA((FIELDS,)),
        ],
    )(*[pltpu.with_memory_space_constraint(a, pltpu.HBM) for a in flat])

    n_ew, n_ns = lax.axis_size("ew"), lax.axis_size("ns")
    from_west = lax.ppermute(to_east, "ew", [(i, (i + 1) % n_ew) for i in range(n_ew)])
    from_east = lax.ppermute(to_west, "ew", [((i + 1) % n_ew, i) for i in range(n_ew)])

    def swap(odd, message):
        return lax.ppermute(message, ("ew", "ns"), partners(odd, n_ew, n_ns))

    y_in, level, base = call(
        prepare,
        [vmem()] * 2,
        [(R - 4, 9) + row, (R, 3) + row, (4, R - 4) + row],
        cost=6,
    )(rows, raw)

    left, right, merged, second, first = call(
        pack_sides,
        [vmem()] * 4 + [pl.BlockSpec(memory_space=pl.ANY)],
        [(FIELDS,) + row] * 3 + [(SIDE_BLOCKS,) + row] * 2,
        cost=1,
    )(rows, own, from_west, from_east, level)
    second = swap(1, second)
    first = swap(0, first)

    x_in, c1, part1, c2, part2, edge = call(
        interior,
        [vmem()] * 8,
        [(R, 9) + row, (4, R - 4) + row, (4, 4) + row, (4, R - 8) + row, (4, 4) + row, (2, 4) + row],
        [pltpu.VMEM((4,) + row, F32)],
        cost=20,
    )(rows, raw, left, right, merged, y_in, level, base)

    outs = call(
        boundary,
        [vmem()] * 14,
        [(K * R, W)] * 4,
        [
            pltpu.VMEM((2, SIDE_BLOCKS) + row, F32),
            pltpu.VMEM((8, 9) + row, F32),
            pltpu.VMEM((8, 9) + row, F32),
            pltpu.VMEM((8, 3) + row, F32),
            pltpu.VMEM((4, 8) + row, F32),
            pltpu.VMEM((4,) + row, F32),
            pltpu.VMEM((2, FIELDS) + row, F32),
        ],
        cost=20,
    )(
        *(rows, left, right, merged, y_in, level, x_in, c1, part1, c2, part2, edge),
        *(second, first),
    )
    return tuple(a.reshape(K, R, W) for a in outs)


def solution(mesh):
    spec = P(None, "ns", "ew")
    return jax.shard_map(
        local, mesh=mesh, in_specs=(spec,) * 7, out_specs=(spec,) * 4, check_vma=False
    )
```

```python
import jax
import jax.numpy as jnp
from jax import lax
from jax.experimental import pallas as pl
from jax.experimental.pallas import tpu as pltpu
from jax.sharding import PartitionSpec as P

horizontal_mix = 0.05
vertical_mix = 0.2

F32 = jnp.float32
K = 32
R = 16
W = 128
G = W // R
HALO = 4
FIELDS = 7
U, V, M = 4, 5, 6
PAIRS = ((0, 1), (2, 3), (U, M))
EDGE_ROWS = len(PAIRS) * K + 8
SIDE_BLOCKS = 27
ROWS_AT = (0, 4, 8, 12, 24, 16, 20)
CORNERS_AT = 26
SOUTH, NORTH = 0, 1
MIB = 1 << 20


def lanes():
    return lax.broadcasted_iota(jnp.int32, (K, W), 1)


def turn(x, amount):
    return pltpu.roll(x, amount % W, 1)


def pack_edges(*refs):
    sources = refs[:FIELDS]
    rows, raw, own, to_east, to_west, raw_flow, raw_wet, arrived = refs[FIELDS:]
    copies = []
    for f in range(FIELDS):
        target = raw.at[f, pl.ds(R, K * R)] if f < 4 else raw_wet if f == M else raw_flow.at[f - U]
        copies.append(pltpu.make_async_copy(sources[f], target, arrived.at[f]))
        copies[-1].start()
    for f in range(4):
        raw[f, pl.ds(0, R)] = jnp.zeros((R, W), F32)
        raw[f, pl.ds((K + 1) * R, R)] = jnp.zeros((R, W), F32)
    lane = lanes()
    group = lane // G
    packed = []
    for f in range(FIELDS):
        copies[f].wait()
        source = raw.at[f] if f < 4 else raw_wet if f == M else raw_flow.at[f - U]
        edges = jnp.zeros((K, W), F32)
        for r in range(R):
            x = source[pl.ds(R + r if f < 4 else r, K, stride=R), :].astype(F32)
            rows[f, r] = x
            edges = jnp.where(group == r, turn(x, G * r + HALO), edges)
        own[f] = edges
        packed.append(edges)
    west_half = lane % G < HALO
    for p, (f, g) in enumerate(PAIRS):
        a, b = packed[f], packed[g]
        to_east[pl.ds(p * K, K)] = jnp.where(west_half, a, turn(b, HALO))
        to_west[pl.ds(p * K, K)] = jnp.where(west_half, turn(b, -HALO), a)
    part = lane[:8] % G // 2
    for target, column in ((to_east, HALO - 2), (to_west, HALO)):
        block = jnp.zeros((8, W), F32)
        for q in range(K // 8):
            moved = turn(packed[V][8 * q : 8 * q + 8], 2 * q - column)
            block = jnp.where(part == q, moved, block)
        target[pl.ds(len(PAIRS) * K, 8)] = block


def pack_sides(rows, own, from_west, from_east, _, left, right, merged, second, first):
    odd = lax.axis_index("ns") % 2
    lane = lanes()
    west_half = lane % G < HALO
    halos = {}
    for p, (f, g) in enumerate(PAIRS):
        a, b = from_west[pl.ds(p * K, K)], from_east[pl.ds(p * K, K)]
        halos[f], halos[g] = (a, b), (turn(a, -HALO), turn(b, HALO))
    a, b = from_west[pl.ds(len(PAIRS) * K, 8)], from_east[pl.ds(len(PAIRS) * K, 8)]
    halos[V] = [
        jnp.concatenate([turn(x, column - 2 * q) for q in range(K // 8)], axis=0)
        for x, column in ((a, HALO - 2), (b, HALO))
    ]
    for f in range(FIELDS):
        a, b = halos[f]
        left[f] = jnp.where(west_half, a, own[f])
        right[f] = jnp.where(west_half, own[f], b)
        merged[f] = jnp.where(west_half, a, b)
    for out, north in ((second, odd), (first, 1 - odd)):
        for f in range(FIELDS):
            count = 2 if f == U else HALO
            start = (R - count) * north
            for r in range(count):
                out[ROWS_AT[f] + r] = rows[f, start + r]
        block = jnp.zeros((K, W), F32)
        for f in range(FIELDS):
            amount = lax.rem(2 * G * f + W - (W - 2 * G) * north, W)
            moved = pltpu.roll(merged[f], amount, 1)
            block = jnp.where(lane // (2 * G) == f, moved, block)
        out[CORNERS_AT] = block


def coefficients(speed, mask):
    opened = {d: mask[d] * mask[d + 1] for d in (-2, -1, 0, 1)}
    return face_coefficients({d: scaled(speed[d], opened[d]) for d in opened}, opened)


def scaled(speed, opened):
    return speed * opened * (1.0 / 12.0)


def face_coefficients(s, opened):
    a = {d: jnp.abs(s[d]) for d in s}
    w0 = {d: -(s[d] + a[d]) for d in (-1, 0, 1)}
    w3 = {d: a[d] - s[d] for d in (-2, -1, 0)}
    w1, w2 = {}, {}
    for d in (-1, 0):
        even, odd = 7.0 * s[d], 3.0 * a[d] + horizontal_mix * opened[d]
        w1[d], w2[d] = even + odd, even - odd
    forward = [w0[-1], w1[-1] - w0[0], w3[-1] - w2[0], -w3[0]]
    transposed = [-w3[-2], w3[-2] - w2[-1], w1[0] - w0[1], w0[1]]
    return forward + transposed + [w2[-1] - w1[0]]


def shifted(c, h, d, lane, step=1):
    if d == 0:
        return c
    if d > 0:
        return turn(jnp.where(lane < step * d, h, c), -step * d)
    return turn(jnp.where(lane >= W + step * d, h, c), -step * d)


def x_coefficients(u, uh, m, mh, lane):
    return coefficients(
        {d: shifted(u, uh, d, lane) for d in (-2, -1, 0, 1)},
        {d: shifted(m, mh, d, lane) for d in (-2, -1, 0, 1, 2)},
    )


def level_coefficients(m):
    inner = lax.broadcasted_iota(jnp.int32, (K, W), 0) < K - 1
    after = jnp.where(inner, vertical_mix * m * pltpu.roll(m, K - 1, 0), 0.0)
    before = pltpu.roll(after, 1, 0)
    return after, before, 1.0 - after - before


def chunk(q):
    return pl.ds(8 * q, 8)


def strided(q, j, stride, shift=0):
    return pl.ds((8 * q + 1 + shift) * stride + j, 8, stride=stride)


def step_row(store, load, x=None, y=None, z=None, base=None):
    lane = lanes()[:8]
    results = []
    for q in range(K // 8):
        part = chunk(q)
        centre = None
        for term in (x and x[0].at[8], y and y.at[8], z and z[0].at[2]):
            if term is not None:
                centre = term[part] if centre is None else centre + term[part]
        if z:
            after, before = z[0].at[0][part], z[0].at[1][part]
        for direction in (0, 1):
            ks = range(4 * direction, 4 * direction + 4)
            xs = [x[0].at[k][part] for k in ks] if x else []
            ys = [y.at[k][part] for k in ks] if y else []
            for f in (2 * direction, 2 * direction + 1):
                c = load(f, 0, q)
                total = centre * c
                if base:
                    total += base(f, q)
                if x:
                    h = x[1](f, q)
                for coefficient, d in zip(xs, (-2, -1, 1, 2)):
                    total += coefficient * shifted(c, h, d, lane)
                for coefficient, d in zip(ys, (-2, -1, 1, 2)):
                    total += coefficient * load(f, d, q)
                if z:
                    c_after, c_before = z[1](f, q)
                    total += after * c_after + before * c_before
                results.append((f, q, total))
    for result in results:
        store(*result)


def halo_columns(merged, j):
    return pltpu.roll(merged, lax.rem(2 * W - HALO - G * j, W), 1)


def edge_faces(edges):
    opened = edges[M] * turn(edges[M], -1)
    return scaled(edges[U], opened), opened


def edge_columns_and_levels(edges, s, opened):
    m = edges[M]
    xs = face_coefficients(
        {d: turn(s, -d) if d else s for d in (-2, -1, 0, 1)}, {-1: turn(opened, 1), 0: opened}
    )
    after, before, centre = level_coefficients(m)
    results = []
    for f in range(4):
        c = edges[f]
        total = (centre + xs[8]) * c
        total += after * pltpu.roll(c, K - 1, 0) + before * pltpu.roll(c, 1, 0)
        for coefficient, d in zip(xs[4 * (f // 2) :], (-2, -1, 1, 2)):
            total += coefficient * turn(c, -d)
        results.append(total)
    return results


def edge_rows(edges, beyond):
    lane = lanes()
    v, m = edges[V], edges[M]
    vh, mh = beyond(V), beyond(M)
    ys = coefficients(
        {d: shifted(v, vh, d, lane, G) for d in (-2, -1, 0, 1)},
        {d: shifted(m, mh, d, lane, G) for d in (-2, -1, 0, 1, 2)},
    )
    results = []
    for f in range(4):
        c, ch = edges[f], beyond(f)
        total = ys[8] * c
        for coefficient, d in zip(ys[4 * (f // 2) :], (-2, -1, 1, 2)):
            total += coefficient * shifted(c, ch, d, lane, G)
        results.append(total)
    return results


def y_coefficients_at(row, j):
    return coefficients(
        {d: row(V, j + d)[...] for d in (-2, -1, 0, 1)},
        {d: row(M, j + d)[...] for d in (-2, -1, 0, 1, 2)},
    )


def by_fours(start, stop, body):
    def four(i, carry):
        for k in range(4):
            body(start + 4 * i + k)
        return carry

    lax.fori_loop(0, (stop - start) // 4, four, 0)


def raw_levels(raw, j):
    return lambda f, q: (raw.at[f][strided(q, j, R, 1), :], raw.at[f][strided(q, j, R, -1), :])


TALL = K + 16


def moved_chunk(q, shift=0):
    return pl.ds(8 + 8 * q + shift, 8)


def clear_ends(ref):
    ref[pl.ds(0, 8)] = jnp.zeros((8, W), F32)
    ref[pl.ds(8 + K, 8)] = jnp.zeros((8, W), F32)


def moved_levels(row):
    return lambda f, q: (row(f)[moved_chunk(q, 1)], row(f)[moved_chunk(q, -1)])


def rolled_levels(load):
    after = [pltpu.roll(load(f), K - 1, 0) for f in range(4)]
    before = [pltpu.roll(load(f), 1, 0) for f in range(4)]
    return lambda f, q: (after[f][8 * q : 8 * q + 8], before[f][8 * q : 8 * q + 8])


def prepare(rows, raw, y_out, level_out, base_out):
    def levels(j):
        for k, value in enumerate(level_coefficients(rows[M, j])):
            level_out[j, k] = value

    by_fours(0, R, levels)

    def across(j):
        got = y_coefficients_at(lambda f, r: rows.at[f, r], j)
        for k in range(9):
            y_out[j - 2, k] = got[k]

    by_fours(2, R - 2, across)

    def first(j):
        def store(f, q, value):
            base_out.at[f, j - 2][chunk(q)] = value

        step_row(
            store,
            lambda f, d, q: rows.at[f, j + d][chunk(q)],
            y=y_out.at[j - 2],
            z=(level_out.at[j], raw_levels(raw, j)),
        )

    by_fours(2, R - 2, first)


def interior(*refs):
    rows, raw, left, right, merged, y_in, level_in, base_in = refs[:8]
    x_out, c1_out, part1_out, c2_out, part2_out, edge_out, merged1, halo_s, halo_mixed = refs[8:]
    lane = lanes()
    west_half = lane % G < HALO
    for f in range(4):
        for r in range(R - 4):
            clear_ends(c1_out.at[f, r])
    faces = [edge_faces(edges) for edges in (left, right)]
    halo_s[...] = jnp.where(west_half, faces[0][0], faces[1][0])
    halo_mixed[...] = jnp.where(west_half, faces[0][1], right[M])

    def x_body(j):
        hs, hm = halo_columns(halo_s[...], j), halo_columns(halo_mixed[...], j)
        m = rows[M, j]
        opened = m * shifted(m, hm, 1, lane)
        s = scaled(rows[U, j], opened)
        got = face_coefficients(
            {d: shifted(s, hs, d, lane) for d in (-2, -1, 0, 1)},
            {-1: shifted(opened, hm, -1, lane), 0: opened},
        )
        for k in range(9):
            x_out[j, k] = got[k]

    by_fours(0, R, x_body)

    both = []
    for side, edges in enumerate((left, right)):
        partial = edge_columns_and_levels(edges, *faces[side])
        across = edge_rows(edges, lambda f: edges[f])
        for f in range(4):
            edge_out[side, f] = partial[f]
        both.append([p + a for p, a in zip(partial, across)])
    for f in range(4):
        merged1[f] = jnp.where(west_half, both[0][f], both[1][f])

    def halo(source, j):
        halos = [halo_columns(source[f], j) for f in range(4)]
        return lambda f, q: halos[f][8 * q : 8 * q + 8]

    def first(j):
        def store(f, q, value):
            c1_out.at[f, j - 2][moved_chunk(q)] = value

        step_row(
            store,
            lambda f, d, q: rows.at[f, j][chunk(q)],
            x=(x_out.at[j], halo(merged, j)),
            base=lambda f, q: base_in.at[f, j - 2][chunk(q)],
        )

    by_fours(2, R - 2, first)

    for i, j in enumerate((0, 1, R - 2, R - 1)):
        def store(f, q, value):
            part1_out.at[f, i][chunk(q)] = value

        step_row(
            store,
            lambda f, d, q: rows.at[f, j][chunk(q)],
            x=(x_out.at[j], halo(merged, j)),
            z=(level_in.at[j], raw_levels(raw, j)),
        )

    def second(j):
        def store(f, q, value):
            c2_out.at[f, j - 4][chunk(q)] = value

        step_row(
            store,
            lambda f, d, q: c1_out.at[f, j - 2 + d][moved_chunk(q)],
            x=(x_out.at[j], halo(merged1, j)),
            y=y_in.at[j - 2],
            z=(level_in.at[j], moved_levels(lambda f: c1_out.at[f, j - 2])),
        )

    by_fours(4, R - 4, second)

    for i, j in enumerate((2, 3, R - 4, R - 3)):
        def store(f, q, value):
            part2_out.at[f, i][chunk(q)] = value

        step_row(
            store,
            lambda f, d, q: c1_out.at[f, j - 2][moved_chunk(q)],
            x=(x_out.at[j], halo(merged1, j)),
            z=(level_in.at[j], moved_levels(lambda f: c1_out.at[f, j - 2])),
        )


def boundary(*refs):
    rows, left, right, merged, y_in, level_in, x_in, c1_in, part1_in, c2_in, part2_in, edge_in = refs[:12]
    second, first = refs[12:14]
    outs = refs[14:18]
    sides, x_new, y_new, level_new, c1_new, merged1, beyond = refs[18:]
    lane = lanes()
    west_half = lane % G < HALO
    place = lax.axis_index("ns")
    last = lax.axis_size("ns") - 1
    odd = place % 2
    inside = {SOUTH: place > 0, NORTH: place < last}
    near = (-2, -1, 0, 1, R - 2, R - 1, R, R + 1)
    new_at = {j: i for i, j in enumerate(near)}
    def unpack(b, carry):
        for message, side in ((second, odd), (first, 1 - odd)):
            here = jnp.where(side == NORTH, place < last, place > 0)
            sides[side, b] = jnp.where(here, message[b], 0.0)
        return carry

    lax.fori_loop(0, SIDE_BLOCKS, unpack, 0, unroll=2)

    def row(f, j):
        if j < 0:
            return sides.at[SOUTH, ROWS_AT[f] + j + (2 if f == U else HALO)]
        if j >= R:
            return sides.at[NORTH, ROWS_AT[f] + j - R]
        return rows.at[f, j]

    for f in range(FIELDS):
        south = turn(sides[SOUTH, CORNERS_AT], W - 2 * G - 2 * G * f)
        north = turn(sides[NORTH, CORNERS_AT], -2 * G * f)
        beyond[f] = jnp.where(lane >= W // 2, south, north)
    for f in range(4):
        for i in range(2, 6):
            clear_ends(c1_new.at[f, i])

    both = []
    for s, edges in enumerate((left, right)):
        across = edge_rows(edges, lambda f: beyond[f])
        both.append([edge_in[s, f] + a for f, a in enumerate(across)])
    for f in range(4):
        merged1[f] = jnp.where(west_half, both[0][f], both[1][f])

    def halo_beyond(f, j):
        return halo_columns(beyond[f], j % R)

    for j in near:
        got = y_coefficients_at(row, j)
        for k in range(9):
            y_new[new_at[j], k] = got[k]
        if not 0 <= j < R:
            got = x_coefficients(
                row(U, j)[...], halo_beyond(U, j), row(M, j)[...], halo_beyond(M, j), lane
            )
            for k in range(9):
                x_new[new_at[j], k] = got[k]
            for k, value in enumerate(level_coefficients(row(M, j)[...])):
                level_new[new_at[j], k] = value

    for j in near:
        side = SOUTH if j < R // 2 else NORTH

        def store(f, q, value):
            if f >= 2 and not 0 <= j < R:
                value = jnp.where(inside[side], value, 0.0)
            c1_new.at[f, new_at[j]][moved_chunk(q)] = value

        def load(f, d, q):
            return row(f, j + d)[chunk(q)]

        if 0 <= j < R:
            i = (0, 1, R - 2, R - 1).index(j)
            step_row(
                store, load, y=y_new.at[new_at[j]], base=lambda f, q: part1_in.at[f, i][chunk(q)]
            )
        else:
            halos = [halo_beyond(f, j) for f in range(4)]
            step_row(
                store,
                load,
                x=(x_new.at[new_at[j]], lambda f, q: halos[f][8 * q : 8 * q + 8]),
                y=y_new.at[new_at[j]],
                z=(level_new.at[new_at[j]], rolled_levels(lambda f: row(f, j)[...])),
            )

    def load1(f, j, q):
        if j in new_at:
            return c1_new.at[f, new_at[j]][moved_chunk(q)]
        return c1_in.at[f, j - 2][moved_chunk(q)]

    for j in (0, 1, 2, 3, R - 4, R - 3, R - 2, R - 1):
        def store(f, q, value):
            outs[f][pl.ds(8 * q * R + j, 8, stride=R), :] = value

        def load(f, d, q):
            return load1(f, j + d, q)

        if j in new_at:
            halos = [halo_columns(merged1[f], j) for f in range(4)]
            step_row(
                store,
                load,
                x=(x_in.at[j], lambda f, q: halos[f][8 * q : 8 * q + 8]),
                y=y_new.at[new_at[j]],
                z=(level_in.at[j], moved_levels(lambda f: c1_new.at[f, new_at[j]])),
            )
        else:
            i = (2, 3, R - 4, R - 3).index(j)
            step_row(
                store, load, y=y_in.at[j - 2], base=lambda f, q: part2_in.at[f, i][chunk(q)]
            )

    def copy(j, carry):
        for f in range(4):
            outs[f][pl.ds(j, K, stride=R), :] = c2_in[f, j - 4]
        return carry

    lax.fori_loop(4, R - 4, copy, 0, unroll=2)


def vmem():
    return pl.BlockSpec(memory_space=pltpu.VMEM)


def call(kernel, in_specs, out_shapes, scratch=(), limit=16 * MIB, cost=0.0):
    return pl.pallas_call(
        kernel,
        out_shape=[jax.ShapeDtypeStruct(shape, F32) for shape in out_shapes],
        in_specs=in_specs,
        out_specs=[vmem()] * len(out_shapes),
        scratch_shapes=list(scratch),
        compiler_params=pltpu.CompilerParams(vmem_limit_bytes=limit),
        cost_estimate=pl.CostEstimate(flops=0, bytes_accessed=int(cost * MIB), transcendentals=0),
    )


def partners(odd, n_ew, n_ns):
    pairs = []
    for e in range(n_ew):
        for s in range(n_ns):
            step = 1 if (s - odd) % 2 == 0 else -1
            if 0 <= s + step < n_ns:
                to = (e, s + step)
            else:
                to = (e ^ 1 if e ^ 1 < n_ew else e, s)
            pairs.append((e * n_ns + s, to[0] * n_ns + to[1]))
    return pairs


def local(temp, salt, u_east, v_north, wet, cot_temp, cot_salt):
    flat = [a.reshape(K * R, W) for a in (temp, salt, cot_temp, cot_salt, u_east, v_north, wet)]

    row = (K, W)
    padded = ((K + 2) * R, W)
    rows, raw, own, to_east, to_west = call(
        pack_edges,
        [pl.BlockSpec(memory_space=pltpu.HBM)] * FIELDS,
        [(FIELDS, R) + row, (4,) + padded, (FIELDS,) + row, (EDGE_ROWS, W), (EDGE_ROWS, W)],
        [
            pltpu.VMEM((2, K * R, W), F32),
            pltpu.VMEM((K * R, W), jnp.int32),
            pltpu.SemaphoreType.DMA((FIELDS,)),
        ],
    )(*[pltpu.with_memory_space_constraint(a, pltpu.HBM) for a in flat])

    n_ew, n_ns = lax.axis_size("ew"), lax.axis_size("ns")
    from_west = lax.ppermute(to_east, "ew", [(i, (i + 1) % n_ew) for i in range(n_ew)])
    from_east = lax.ppermute(to_west, "ew", [((i + 1) % n_ew, i) for i in range(n_ew)])

    def swap(odd, message):
        return lax.ppermute(message, ("ew", "ns"), partners(odd, n_ew, n_ns))

    y_in, level, base = call(
        prepare,
        [vmem()] * 2,
        [(R - 4, 9) + row, (R, 3) + row, (4, R - 4) + row],
        cost=6,
    )(rows, raw)

    left, right, merged, second, first = call(
        pack_sides,
        [vmem()] * 4 + [pl.BlockSpec(memory_space=pl.ANY)],
        [(FIELDS,) + row] * 3 + [(SIDE_BLOCKS,) + row] * 2,
        cost=1,
    )(rows, own, from_west, from_east, level)
    second = swap(1, second)
    first = swap(0, first)

    x_in, c1, part1, c2, part2, edge = call(
        interior,
        [vmem()] * 8,
        [(R, 9) + row, (4, R - 4, TALL, W), (4, 4) + row, (4, R - 8) + row, (4, 4) + row, (2, 4) + row],
        [pltpu.VMEM((4,) + row, F32), pltpu.VMEM(row, F32), pltpu.VMEM(row, F32)],
        cost=20,
    )(rows, raw, left, right, merged, y_in, level, base)

    outs = call(
        boundary,
        [vmem()] * 14,
        [(K * R, W)] * 4,
        [
            pltpu.VMEM((2, SIDE_BLOCKS) + row, F32),
            pltpu.VMEM((8, 9) + row, F32),
            pltpu.VMEM((8, 9) + row, F32),
            pltpu.VMEM((8, 3) + row, F32),
            pltpu.VMEM((4, 8, TALL, W), F32),
            pltpu.VMEM((4,) + row, F32),
            pltpu.VMEM((FIELDS,) + row, F32),
        ],
        cost=20,
    )(
        *(rows, left, right, merged, y_in, level, x_in, c1, part1, c2, part2, edge),
        *(second, first),
    )
    return tuple(a.reshape(K, R, W) for a in outs)


def solution(mesh):
    spec = P(None, "ns", "ew")
    return jax.shard_map(
        local, mesh=mesh, in_specs=(spec,) * 7, out_specs=(spec,) * 4, check_vma=False
    )
```

```python
import jax
import jax.numpy as jnp
from jax import lax
from jax.experimental import pallas as pl
from jax.experimental.pallas import tpu as pltpu
from jax.sharding import PartitionSpec as P

horizontal_mix = 0.05
vertical_mix = 0.2

F32 = jnp.float32
K = 32
R = 16
W = 128
G = W // R
HALO = 4
FIELDS = 7
U, V, M = 4, 5, 6
PAIRS = ((0, 1), (2, 3), (U, M))
EDGE_ROWS = len(PAIRS) * K + 8
SIDE_BLOCKS = 27
ROWS_AT = (0, 4, 8, 12, 24, 16, 20)
CORNERS_AT = 26
SOUTH, NORTH = 0, 1
MIB = 1 << 20


def lanes():
    return lax.broadcasted_iota(jnp.int32, (K, W), 1)


def turn(x, amount):
    return pltpu.roll(x, amount % W, 1)


def pack_edges(*refs):
    sources = refs[:FIELDS]
    rows, raw, own, to_east, to_west, raw_flow, raw_wet, arrived = refs[FIELDS:]
    copies = []
    for f in range(FIELDS):
        target = raw.at[f, pl.ds(R, K * R)] if f < 4 else raw_wet if f == M else raw_flow.at[f - U]
        copies.append(pltpu.make_async_copy(sources[f], target, arrived.at[f]))
        copies[-1].start()
    for f in range(4):
        raw[f, pl.ds(0, R)] = jnp.zeros((R, W), F32)
        raw[f, pl.ds((K + 1) * R, R)] = jnp.zeros((R, W), F32)
    lane = lanes()
    group = lane // G
    packed = []
    for f in range(FIELDS):
        copies[f].wait()
        source = raw.at[f] if f < 4 else raw_wet if f == M else raw_flow.at[f - U]
        edges = jnp.zeros((K, W), F32)
        for r in range(R):
            x = source[pl.ds(R + r if f < 4 else r, K, stride=R), :].astype(F32)
            rows[f, r] = x
            edges = jnp.where(group == r, turn(x, G * r + HALO), edges)
        own[f] = edges
        packed.append(edges)
    west_half = lane % G < HALO
    for p, (f, g) in enumerate(PAIRS):
        a, b = packed[f], packed[g]
        to_east[pl.ds(p * K, K)] = jnp.where(west_half, a, turn(b, HALO))
        to_west[pl.ds(p * K, K)] = jnp.where(west_half, turn(b, -HALO), a)
    part = lane[:8] % G // 2
    for target, column in ((to_east, HALO - 2), (to_west, HALO)):
        block = jnp.zeros((8, W), F32)
        for q in range(K // 8):
            moved = turn(packed[V][8 * q : 8 * q + 8], 2 * q - column)
            block = jnp.where(part == q, moved, block)
        target[pl.ds(len(PAIRS) * K, 8)] = block


def pack_sides(rows, own, from_west, from_east, _, left, right, merged, second, first):
    odd = lax.axis_index("ns") % 2
    lane = lanes()
    west_half = lane % G < HALO
    halos = {}
    for p, (f, g) in enumerate(PAIRS):
        a, b = from_west[pl.ds(p * K, K)], from_east[pl.ds(p * K, K)]
        halos[f], halos[g] = (a, b), (turn(a, -HALO), turn(b, HALO))
    a, b = from_west[pl.ds(len(PAIRS) * K, 8)], from_east[pl.ds(len(PAIRS) * K, 8)]
    halos[V] = [
        jnp.concatenate([turn(x, column - 2 * q) for q in range(K // 8)], axis=0)
        for x, column in ((a, HALO - 2), (b, HALO))
    ]
    for f in range(FIELDS):
        a, b = halos[f]
        left[f] = jnp.where(west_half, a, own[f])
        right[f] = jnp.where(west_half, own[f], b)
        merged[f] = jnp.where(west_half, a, b)
    for out, north in ((second, odd), (first, 1 - odd)):
        for f in range(FIELDS):
            count = 2 if f == U else HALO
            start = (R - count) * north
            for r in range(count):
                out[ROWS_AT[f] + r] = rows[f, start + r]
        block = jnp.zeros((K, W), F32)
        for f in range(FIELDS):
            amount = lax.rem(2 * G * f + W - (W - 2 * G) * north, W)
            moved = pltpu.roll(merged[f], amount, 1)
            block = jnp.where(lane // (2 * G) == f, moved, block)
        out[CORNERS_AT] = block


def coefficients(speed, mask):
    opened = {d: mask[d] * mask[d + 1] for d in (-2, -1, 0, 1)}
    return face_coefficients({d: scaled(speed[d], opened[d]) for d in opened}, opened)


def scaled(speed, opened):
    return speed * opened * (1.0 / 12.0)


def face_coefficients(s, opened):
    a = {d: jnp.abs(s[d]) for d in s}
    w0 = {d: -(s[d] + a[d]) for d in (-1, 0, 1)}
    w3 = {d: a[d] - s[d] for d in (-2, -1, 0)}
    w1, w2 = {}, {}
    for d in (-1, 0):
        even, odd = 7.0 * s[d], 3.0 * a[d] + horizontal_mix * opened[d]
        w1[d], w2[d] = even + odd, even - odd
    forward = [w0[-1], w1[-1] - w0[0], w3[-1] - w2[0], -w3[0]]
    transposed = [-w3[-2], w3[-2] - w2[-1], w1[0] - w0[1], w0[1]]
    return forward + transposed + [w2[-1] - w1[0]]


def shifted(c, h, d, lane, step=1):
    if d == 0:
        return c
    if d > 0:
        return turn(jnp.where(lane < step * d, h, c), -step * d)
    return turn(jnp.where(lane >= W + step * d, h, c), -step * d)


def x_coefficients(u, uh, m, mh, lane):
    return coefficients(
        {d: shifted(u, uh, d, lane) for d in (-2, -1, 0, 1)},
        {d: shifted(m, mh, d, lane) for d in (-2, -1, 0, 1, 2)},
    )


def level_coefficients(m):
    inner = lax.broadcasted_iota(jnp.int32, (K, W), 0) < K - 1
    after = jnp.where(inner, vertical_mix * m * pltpu.roll(m, K - 1, 0), 0.0)
    before = pltpu.roll(after, 1, 0)
    return after, before, 1.0 - after - before


def chunk(q):
    return pl.ds(8 * q, 8)


def strided(q, j, stride, shift=0):
    return pl.ds((8 * q + 1 + shift) * stride + j, 8, stride=stride)


def step_row(store, load, x=None, y=None, z=None, base=None, directions=(0, 1)):
    lane = lanes()[:8]
    results = []
    for q in range(K // 8):
        part = chunk(q)
        centre = None
        for term in (x and x[0].at[8], y and y.at[8], z and z[0].at[2]):
            if term is not None:
                centre = term[part] if centre is None else centre + term[part]
        if z:
            after, before = z[0].at[0][part], z[0].at[1][part]
        for direction in directions:
            ks = range(4 * direction, 4 * direction + 4)
            xs = [x[0].at[k][part] for k in ks] if x else []
            ys = [y.at[k][part] for k in ks] if y else []
            for f in (2 * direction, 2 * direction + 1):
                c = load(f, 0, q)
                total = centre * c
                if base:
                    total += base(f, q)
                if x:
                    h = x[1](f, q)
                for coefficient, d in zip(xs, (-2, -1, 1, 2)):
                    total += coefficient * shifted(c, h, d, lane)
                for coefficient, d in zip(ys, (-2, -1, 1, 2)):
                    total += coefficient * load(f, d, q)
                if z:
                    c_after, c_before = z[1](f, q)
                    total += after * c_after + before * c_before
                results.append((f, q, total))
    for result in results:
        store(*result)


def halo_columns(merged, j):
    return pltpu.roll(merged, lax.rem(2 * W - HALO - G * j, W), 1)


def edge_faces(edges):
    opened = edges[M] * turn(edges[M], -1)
    return scaled(edges[U], opened), opened


def edge_columns_and_levels(edges, s, opened):
    m = edges[M]
    xs = face_coefficients(
        {d: turn(s, -d) if d else s for d in (-2, -1, 0, 1)}, {-1: turn(opened, 1), 0: opened}
    )
    after, before, centre = level_coefficients(m)
    results = []
    for f in range(4):
        c = edges[f]
        total = (centre + xs[8]) * c
        total += after * pltpu.roll(c, K - 1, 0) + before * pltpu.roll(c, 1, 0)
        for coefficient, d in zip(xs[4 * (f // 2) :], (-2, -1, 1, 2)):
            total += coefficient * turn(c, -d)
        results.append(total)
    return results


def edge_rows(merged, beyond):
    lane = lanes()
    v, m = merged[V], merged[M]
    vh, mh = beyond(V), beyond(M)
    ys = coefficients(
        {d: shifted(v, vh, d, lane, G) for d in (-2, -1, 0, 1)},
        {d: shifted(m, mh, d, lane, G) for d in (-2, -1, 0, 1, 2)},
    )
    results = []
    for f in range(4):
        c, ch = merged[f], beyond(f)
        total = ys[8] * c
        for coefficient, d in zip(ys[4 * (f // 2) :], (-2, -1, 1, 2)):
            total += coefficient * shifted(c, ch, d, lane, G)
        results.append(total)
    return results


def y_coefficients_at(row, j):
    return coefficients(
        {d: row(V, j + d)[...] for d in (-2, -1, 0, 1)},
        {d: row(M, j + d)[...] for d in (-2, -1, 0, 1, 2)},
    )


def by_fours(start, stop, body):
    def four(i, carry):
        for k in range(4):
            body(start + 4 * i + k)
        return carry

    lax.fori_loop(0, (stop - start) // 4, four, 0)


def raw_levels(raw, j):
    return lambda f, q: (raw.at[f][strided(q, j, R, 1), :], raw.at[f][strided(q, j, R, -1), :])


TALL = K + 16


def moved_chunk(q, shift=0):
    return pl.ds(8 + 8 * q + shift, 8)


def clear_ends(ref):
    ref[pl.ds(0, 8)] = jnp.zeros((8, W), F32)
    ref[pl.ds(8 + K, 8)] = jnp.zeros((8, W), F32)


def moved_levels(row):
    return lambda f, q: (row(f)[moved_chunk(q, 1)], row(f)[moved_chunk(q, -1)])


def rolled_levels(load, fields):
    after = {f: pltpu.roll(load(f), K - 1, 0) for f in fields}
    before = {f: pltpu.roll(load(f), 1, 0) for f in fields}
    return lambda f, q: (after[f][8 * q : 8 * q + 8], before[f][8 * q : 8 * q + 8])


def prepare(rows, raw, y_out, level_out, base_out):
    def levels(j):
        for k, value in enumerate(level_coefficients(rows[M, j])):
            level_out[j, k] = value

    by_fours(0, R, levels)

    def across(j):
        got = y_coefficients_at(lambda f, r: rows.at[f, r], j)
        for k in range(9):
            y_out[j - 2, k] = got[k]

    by_fours(2, R - 2, across)

    def first(j):
        def store(f, q, value):
            base_out.at[f, j - 2][chunk(q)] = value

        step_row(
            store,
            lambda f, d, q: rows.at[f, j + d][chunk(q)],
            y=y_out.at[j - 2],
            z=(level_out.at[j], raw_levels(raw, j)),
        )

    by_fours(2, R - 2, first)


def interior(*refs):
    rows, raw, left, right, merged, y_in, level_in, base_in = refs[:8]
    x_out, c1_out, part1_out, c2_out, part2_out, edge_out, merged1, halo_s, halo_mixed = refs[8:]
    lane = lanes()
    west_half = lane % G < HALO
    for f in range(4):
        for r in range(R - 4):
            clear_ends(c1_out.at[f, r])
    faces = [edge_faces(edges) for edges in (left, right)]
    halo_s[...] = jnp.where(west_half, faces[0][0], faces[1][0])
    halo_mixed[...] = jnp.where(west_half, faces[0][1], right[M])

    def x_body(j):
        hs, hm = halo_columns(halo_s[...], j), halo_columns(halo_mixed[...], j)
        m = rows[M, j]
        opened = m * shifted(m, hm, 1, lane)
        s = scaled(rows[U, j], opened)
        got = face_coefficients(
            {d: shifted(s, hs, d, lane) for d in (-2, -1, 0, 1)},
            {-1: shifted(opened, hm, -1, lane), 0: opened},
        )
        for k in range(9):
            x_out[j, k] = got[k]

    by_fours(0, R, x_body)

    partial = [edge_columns_and_levels(e, *f) for e, f in zip((left, right), faces)]
    across = edge_rows(merged, lambda f: merged[f])
    for f in range(4):
        edge = jnp.where(west_half, partial[0][f], partial[1][f])
        edge_out[f] = edge
        merged1[f] = edge + across[f]

    def halo(source, j):
        halos = [halo_columns(source[f], j) for f in range(4)]
        return lambda f, q: halos[f][8 * q : 8 * q + 8]

    def first(j):
        def store(f, q, value):
            c1_out.at[f, j - 2][moved_chunk(q)] = value

        step_row(
            store,
            lambda f, d, q: rows.at[f, j][chunk(q)],
            x=(x_out.at[j], halo(merged, j)),
            base=lambda f, q: base_in.at[f, j - 2][chunk(q)],
        )

    by_fours(2, R - 2, first)

    for i, j in enumerate((0, 1, R - 2, R - 1)):
        def store(f, q, value):
            part1_out.at[f, i][chunk(q)] = value

        step_row(
            store,
            lambda f, d, q: rows.at[f, j][chunk(q)],
            x=(x_out.at[j], halo(merged, j)),
            z=(level_in.at[j], raw_levels(raw, j)),
        )

    def second(j):
        def store(f, q, value):
            c2_out.at[f, j - 4][chunk(q)] = value

        step_row(
            store,
            lambda f, d, q: c1_out.at[f, j - 2 + d][moved_chunk(q)],
            x=(x_out.at[j], halo(merged1, j)),
            y=y_in.at[j - 2],
            z=(level_in.at[j], moved_levels(lambda f: c1_out.at[f, j - 2])),
        )

    by_fours(4, R - 4, second)

    for i, j in enumerate((2, 3, R - 4, R - 3)):
        def store(f, q, value):
            part2_out.at[f, i][chunk(q)] = value

        step_row(
            store,
            lambda f, d, q: c1_out.at[f, j - 2][moved_chunk(q)],
            x=(x_out.at[j], halo(merged1, j)),
            z=(level_in.at[j], moved_levels(lambda f: c1_out.at[f, j - 2])),
        )


def boundary(*refs):
    rows, merged, y_in, level_in, x_in, c1_in, part1_in, c2_in, part2_in, edge_in = refs[:10]
    second, first = refs[10:12]
    outs = refs[12:16]
    sides, x_new, y_new, level_new, c1_new, merged1, beyond, final, left_by = refs[16:]
    lane = lanes()
    place = lax.axis_index("ns")
    last = lax.axis_size("ns") - 1
    odd = place % 2
    inside = {SOUTH: place > 0, NORTH: place < last}
    near = (-2, -1, 0, 1, R - 2, R - 1, R, R + 1)
    new_at = {j: i for i, j in enumerate(near)}
    def unpack(b, carry):
        for message, side in ((second, odd), (first, 1 - odd)):
            here = jnp.where(side == NORTH, place < last, place > 0)
            sides[side, b] = jnp.where(here, message[b], 0.0)
        return carry

    lax.fori_loop(0, SIDE_BLOCKS, unpack, 0, unroll=2)

    def row(f, j):
        if j < 0:
            return sides.at[SOUTH, ROWS_AT[f] + j + (2 if f == U else HALO)]
        if j >= R:
            return sides.at[NORTH, ROWS_AT[f] + j - R]
        return rows.at[f, j]

    for f in range(FIELDS):
        south = turn(sides[SOUTH, CORNERS_AT], W - 2 * G - 2 * G * f)
        north = turn(sides[NORTH, CORNERS_AT], -2 * G * f)
        beyond[f] = jnp.where(lane >= W // 2, south, north)
    for f in range(4):
        for i in range(2, 6):
            clear_ends(c1_new.at[f, i])

    for f, across in enumerate(edge_rows(merged, lambda f: beyond[f])):
        merged1[f] = edge_in[f] + across

    def halo_beyond(f, j):
        return halo_columns(beyond[f], j % R)

    for j in near:
        got = y_coefficients_at(row, j)
        for k in range(9):
            y_new[new_at[j], k] = got[k]
        if not 0 <= j < R:
            got = x_coefficients(
                row(U, j)[...], halo_beyond(U, j), row(M, j)[...], halo_beyond(M, j), lane
            )
            for k in range(9):
                x_new[new_at[j], k] = got[k]
            for k, value in enumerate(level_coefficients(row(M, j)[...])):
                level_new[new_at[j], k] = value

    def load1(f, j, q):
        if j in new_at:
            return c1_new.at[f, new_at[j]][moved_chunk(q)]
        return c1_in.at[f, j - 2][moved_chunk(q)]

    def copy(j, carry):
        for f in range(4):
            final[f, pl.ds(j, K, stride=R), :] = c2_in[f, j - 4]
        return carry

    lax.fori_loop(4, R - 4, copy, 0, unroll=2)

    copies = []
    for direction in (0, 1):
        directions = (direction,)
        here = (2 * direction, 2 * direction + 1)
        for j in near:
            side = SOUTH if j < R // 2 else NORTH

            def store(f, q, value):
                if f >= 2 and not 0 <= j < R:
                    value = jnp.where(inside[side], value, 0.0)
                c1_new.at[f, new_at[j]][moved_chunk(q)] = value

            def load(f, d, q):
                return row(f, j + d)[chunk(q)]

            if 0 <= j < R:
                i = (0, 1, R - 2, R - 1).index(j)
                step_row(
                    store, load, y=y_new.at[new_at[j]], base=lambda f, q: part1_in.at[f, i][chunk(q)],
                    directions=directions,
                )
            else:
                halos = {f: halo_beyond(f, j) for f in here}
                step_row(
                    store,
                    load,
                    x=(x_new.at[new_at[j]], lambda f, q: halos[f][8 * q : 8 * q + 8]),
                    y=y_new.at[new_at[j]],
                    z=(level_new.at[new_at[j]], rolled_levels(lambda f: row(f, j)[...], here)),
                    directions=directions,
                )

        for j in (0, 1, 2, 3, R - 4, R - 3, R - 2, R - 1):
            def store(f, q, value):
                final[f, pl.ds(8 * q * R + j, 8, stride=R), :] = value

            def load(f, d, q):
                return load1(f, j + d, q)

            if j in new_at:
                halos = {f: halo_columns(merged1[f], j) for f in here}
                step_row(
                    store,
                    load,
                    x=(x_in.at[j], lambda f, q: halos[f][8 * q : 8 * q + 8]),
                    y=y_new.at[new_at[j]],
                    z=(level_in.at[j], moved_levels(lambda f: c1_new.at[f, new_at[j]])),
                    directions=directions,
                )
            else:
                i = (2, 3, R - 4, R - 3).index(j)
                step_row(
                    store, load, y=y_in.at[j - 2], base=lambda f, q: part2_in.at[f, i][chunk(q)],
                    directions=directions,
                )

        for f in here:
            copies.append(pltpu.make_async_copy(final.at[f], outs[f], left_by.at[f]))
            copies[-1].start()
    for copy_out in copies:
        copy_out.wait()


def vmem():
    return pl.BlockSpec(memory_space=pltpu.VMEM)


def call(kernel, in_specs, out_shapes, scratch=(), out_space=pltpu.VMEM, limit=16 * MIB, cost=0.0):
    return pl.pallas_call(
        kernel,
        out_shape=[jax.ShapeDtypeStruct(shape, F32) for shape in out_shapes],
        in_specs=in_specs,
        out_specs=[pl.BlockSpec(memory_space=out_space)] * len(out_shapes),
        scratch_shapes=list(scratch),
        compiler_params=pltpu.CompilerParams(vmem_limit_bytes=limit),
        cost_estimate=pl.CostEstimate(flops=0, bytes_accessed=int(cost * MIB), transcendentals=0),
    )


def partners(odd, n_ew, n_ns):
    pairs = []
    for e in range(n_ew):
        for s in range(n_ns):
            step = 1 if (s - odd) % 2 == 0 else -1
            if 0 <= s + step < n_ns:
                to = (e, s + step)
            else:
                to = (e ^ 1 if e ^ 1 < n_ew else e, s)
            pairs.append((e * n_ns + s, to[0] * n_ns + to[1]))
    return pairs


def local(temp, salt, u_east, v_north, wet, cot_temp, cot_salt):
    flat = [a.reshape(K * R, W) for a in (temp, salt, cot_temp, cot_salt, u_east, v_north, wet)]

    row = (K, W)
    padded = ((K + 2) * R, W)
    rows, raw, own, to_east, to_west = call(
        pack_edges,
        [pl.BlockSpec(memory_space=pltpu.HBM)] * FIELDS,
        [(FIELDS, R) + row, (4,) + padded, (FIELDS,) + row, (EDGE_ROWS, W), (EDGE_ROWS, W)],
        [
            pltpu.VMEM((2, K * R, W), F32),
            pltpu.VMEM((K * R, W), jnp.int32),
            pltpu.SemaphoreType.DMA((FIELDS,)),
        ],
    )(*[pltpu.with_memory_space_constraint(a, pltpu.HBM) for a in flat])

    n_ew, n_ns = lax.axis_size("ew"), lax.axis_size("ns")
    from_west = lax.ppermute(to_east, "ew", [(i, (i + 1) % n_ew) for i in range(n_ew)])
    from_east = lax.ppermute(to_west, "ew", [((i + 1) % n_ew, i) for i in range(n_ew)])

    def swap(odd, message):
        return lax.ppermute(message, ("ew", "ns"), partners(odd, n_ew, n_ns))

    y_in, level, base = call(
        prepare,
        [vmem()] * 2,
        [(R - 4, 9) + row, (R, 3) + row, (4, R - 4) + row],
        cost=6,
    )(rows, raw)

    left, right, merged, second, first = call(
        pack_sides,
        [vmem()] * 4 + [pl.BlockSpec(memory_space=pl.ANY)],
        [(FIELDS,) + row] * 3 + [(SIDE_BLOCKS,) + row] * 2,
        cost=1,
    )(rows, own, from_west, from_east, level)
    second = swap(1, second)
    first = swap(0, first)

    x_in, c1, part1, c2, part2, edge = call(
        interior,
        [vmem()] * 8,
        [(R, 9) + row, (4, R - 4, TALL, W), (4, 4) + row, (4, R - 8) + row, (4, 4) + row, (4,) + row],
        [pltpu.VMEM((4,) + row, F32), pltpu.VMEM(row, F32), pltpu.VMEM(row, F32)],
        cost=20,
    )(rows, raw, left, right, merged, y_in, level, base)

    outs = call(
        boundary,
        [vmem()] * 12,
        [(K * R, W)] * 4,
        [
            pltpu.VMEM((2, SIDE_BLOCKS) + row, F32),
            pltpu.VMEM((8, 9) + row, F32),
            pltpu.VMEM((8, 9) + row, F32),
            pltpu.VMEM((8, 3) + row, F32),
            pltpu.VMEM((4, 8, TALL, W), F32),
            pltpu.VMEM((4,) + row, F32),
            pltpu.VMEM((FIELDS,) + row, F32),
            pltpu.VMEM((4, K * R, W), F32),
            pltpu.SemaphoreType.DMA((4,)),
        ],
        out_space=pltpu.HBM,
        cost=20,
    )(
        *(rows, merged, y_in, level, x_in, c1, part1, c2, part2, edge),
        *(second, first),
    )
    return tuple(a.reshape(K, R, W) for a in outs)


def solution(mesh):
    spec = P(None, "ns", "ew")
    return jax.shard_map(
        local, mesh=mesh, in_specs=(spec,) * 7, out_specs=(spec,) * 4, check_vma=False
    )
```

```python
import jax
import jax.numpy as jnp
from jax import lax
from jax.experimental import pallas as pl
from jax.experimental.pallas import tpu as pltpu
from jax.sharding import PartitionSpec as P

horizontal_mix = 0.05
vertical_mix = 0.2

F32 = jnp.float32
K = 32
R = 16
W = 128
G = W // R
HALO = 4
FIELDS = 7
U, V, M = 4, 5, 6
PAIRS = ((0, 1), (2, 3), (U, M))
EDGE_ROWS = len(PAIRS) * K + 8
SIDE_BLOCKS = 27
ROWS_AT = (0, 4, 8, 12, 24, 16, 20)
CORNERS_AT = 26
SOUTH, NORTH = 0, 1
MIB = 1 << 20


def lanes():
    return lax.broadcasted_iota(jnp.int32, (K, W), 1)


def turn(x, amount):
    return pltpu.roll(x, amount % W, 1)


def pack_edges(*refs):
    sources = refs[:FIELDS]
    rows, raw, own, first, second, raw_flow, raw_wet, arrived = refs[FIELDS:]
    odd = lax.axis_index("ew") % 2 == 1
    copies = []
    for f in range(FIELDS):
        target = raw.at[f, pl.ds(R, K * R)] if f < 4 else raw_wet if f == M else raw_flow.at[f - U]
        copies.append(pltpu.make_async_copy(sources[f], target, arrived.at[f]))
        copies[-1].start()
    for f in range(4):
        raw[f, pl.ds(0, R)] = jnp.zeros((R, W), F32)
        raw[f, pl.ds((K + 1) * R, R)] = jnp.zeros((R, W), F32)
    lane = lanes()
    group = lane // G
    packed = []
    for f in range(FIELDS):
        copies[f].wait()
        source = raw.at[f] if f < 4 else raw_wet if f == M else raw_flow.at[f - U]
        edges = jnp.zeros((K, W), F32)
        for r in range(R):
            x = source[pl.ds(R + r if f < 4 else r, K, stride=R), :].astype(F32)
            rows[f, r] = x
            edges = jnp.where(group == r, turn(x, G * r + HALO), edges)
        own[f] = edges
        packed.append(edges)
    west_half = lane % G < HALO
    for p, (f, g) in enumerate(PAIRS):
        a, b = packed[f], packed[g]
        to_east = jnp.where(west_half, a, turn(b, HALO))
        to_west = jnp.where(west_half, turn(b, -HALO), a)
        first[pl.ds(p * K, K)] = jnp.where(odd, to_west, to_east)
        second[pl.ds(p * K, K)] = jnp.where(odd, to_east, to_west)
    part = lane[:8] % G // 2
    to_east = to_west = jnp.zeros((8, W), F32)
    for q in range(K // 8):
        v = packed[V][8 * q : 8 * q + 8]
        to_east = jnp.where(part == q, turn(v, 2 * q - HALO + 2), to_east)
        to_west = jnp.where(part == q, turn(v, 2 * q - HALO), to_west)
    first[pl.ds(len(PAIRS) * K, 8)] = jnp.where(odd, to_west, to_east)
    second[pl.ds(len(PAIRS) * K, 8)] = jnp.where(odd, to_east, to_west)


def pack_sides(rows, own, from_first, from_second, _, left, right, merged, second, first):
    odd = lax.axis_index("ns") % 2
    lane = lanes()
    west_half = lane % G < HALO
    odd_ew = lax.axis_index("ew") % 2 == 1

    def from_sides(part):
        x, y = from_first[part], from_second[part]
        return jnp.where(odd_ew, x, y), jnp.where(odd_ew, y, x)

    halos = {}
    for p, (f, g) in enumerate(PAIRS):
        a, b = from_sides(pl.ds(p * K, K))
        halos[f], halos[g] = (a, b), (turn(a, -HALO), turn(b, HALO))
    a, b = from_sides(pl.ds(len(PAIRS) * K, 8))
    halos[V] = [
        jnp.concatenate([turn(x, column - 2 * q) for q in range(K // 8)], axis=0)
        for x, column in ((a, HALO - 2), (b, HALO))
    ]
    for f in range(FIELDS):
        a, b = halos[f]
        left[f] = jnp.where(west_half, a, own[f])
        right[f] = jnp.where(west_half, own[f], b)
        merged[f] = jnp.where(west_half, a, b)
    for out, north in ((second, odd), (first, 1 - odd)):
        for f in range(FIELDS):
            count = 2 if f == U else HALO
            start = (R - count) * north
            for r in range(count):
                out[ROWS_AT[f] + r] = rows[f, start + r]
        block = jnp.zeros((K, W), F32)
        for f in range(FIELDS):
            amount = lax.rem(2 * G * f + W - (W - 2 * G) * north, W)
            moved = pltpu.roll(merged[f], amount, 1)
            block = jnp.where(lane // (2 * G) == f, moved, block)
        out[CORNERS_AT] = block


def coefficients(speed, mask):
    opened = {d: mask[d] * mask[d + 1] for d in (-2, -1, 0, 1)}
    return face_coefficients({d: scaled(speed[d], opened[d]) for d in opened}, opened)


def scaled(speed, opened):
    return speed * opened * (1.0 / 12.0)


def face_coefficients(s, opened):
    a = {d: jnp.abs(s[d]) for d in s}
    w0 = {d: -(s[d] + a[d]) for d in (-1, 0, 1)}
    w3 = {d: a[d] - s[d] for d in (-2, -1, 0)}
    w1, w2 = {}, {}
    for d in (-1, 0):
        even, odd = 7.0 * s[d], 3.0 * a[d] + horizontal_mix * opened[d]
        w1[d], w2[d] = even + odd, even - odd
    forward = [w0[-1], w1[-1] - w0[0], w3[-1] - w2[0], -w3[0]]
    transposed = [-w3[-2], w3[-2] - w2[-1], w1[0] - w0[1], w0[1]]
    return forward + transposed + [w2[-1] - w1[0]]


def shifted(c, h, d, lane, step=1):
    if d == 0:
        return c
    if d > 0:
        return turn(jnp.where(lane < step * d, h, c), -step * d)
    return turn(jnp.where(lane >= W + step * d, h, c), -step * d)


def x_coefficients(u, uh, m, mh, lane):
    return coefficients(
        {d: shifted(u, uh, d, lane) for d in (-2, -1, 0, 1)},
        {d: shifted(m, mh, d, lane) for d in (-2, -1, 0, 1, 2)},
    )


def level_coefficients(m):
    inner = lax.broadcasted_iota(jnp.int32, (K, W), 0) < K - 1
    after = jnp.where(inner, vertical_mix * m * pltpu.roll(m, K - 1, 0), 0.0)
    before = pltpu.roll(after, 1, 0)
    return after, before, 1.0 - after - before


def chunk(q):
    return pl.ds(8 * q, 8)


def strided(q, j, stride, shift=0):
    return pl.ds((8 * q + 1 + shift) * stride + j, 8, stride=stride)


def step_row(store, load, x=None, y=None, z=None, base=None):
    lane = lanes()[:8]
    for q in range(K // 8):
        part = chunk(q)
        centre = None
        for term in (x and x[0].at[8], y and y.at[8], z and z[0].at[2]):
            if term is not None:
                centre = term[part] if centre is None else centre + term[part]
        if z:
            after, before = z[0].at[0][part], z[0].at[1][part]
        for direction in (0, 1):
            ks = range(4 * direction, 4 * direction + 4)
            xs = [x[0].at[k][part] for k in ks] if x else []
            ys = [y.at[k][part] for k in ks] if y else []
            for f in (2 * direction, 2 * direction + 1):
                c = load(f, 0, q)
                total = centre * c
                if base:
                    total += base(f, q)
                if x:
                    h = x[1](f, q)
                for coefficient, d in zip(xs, (-2, -1, 1, 2)):
                    total += coefficient * shifted(c, h, d, lane)
                for coefficient, d in zip(ys, (-2, -1, 1, 2)):
                    total += coefficient * load(f, d, q)
                if z:
                    c_after, c_before = z[1](f, q)
                    total += after * c_after + before * c_before
                store(f, q, total)


def halo_columns(merged, j):
    return pltpu.roll(merged, lax.rem(2 * W - HALO - G * j, W), 1)


def edge_faces(edges):
    opened = edges[M] * turn(edges[M], -1)
    return scaled(edges[U], opened), opened


def edge_columns_and_levels(edges, s, opened):
    m = edges[M]
    xs = face_coefficients(
        {d: turn(s, -d) if d else s for d in (-2, -1, 0, 1)}, {-1: turn(opened, 1), 0: opened}
    )
    after, before, centre = level_coefficients(m)
    results = []
    for f in range(4):
        c = edges[f]
        total = (centre + xs[8]) * c
        total += after * pltpu.roll(c, K - 1, 0) + before * pltpu.roll(c, 1, 0)
        for coefficient, d in zip(xs[4 * (f // 2) :], (-2, -1, 1, 2)):
            total += coefficient * turn(c, -d)
        results.append(total)
    return results


def edge_rows(merged, beyond):
    lane = lanes()
    v, m = merged[V], merged[M]
    vh, mh = beyond(V), beyond(M)
    ys = coefficients(
        {d: shifted(v, vh, d, lane, G) for d in (-2, -1, 0, 1)},
        {d: shifted(m, mh, d, lane, G) for d in (-2, -1, 0, 1, 2)},
    )
    results = []
    for f in range(4):
        c, ch = merged[f], beyond(f)
        total = ys[8] * c
        for coefficient, d in zip(ys[4 * (f // 2) :], (-2, -1, 1, 2)):
            total += coefficient * shifted(c, ch, d, lane, G)
        results.append(total)
    return results


def y_coefficients_at(row, j):
    return coefficients(
        {d: row(V, j + d)[...] for d in (-2, -1, 0, 1)},
        {d: row(M, j + d)[...] for d in (-2, -1, 0, 1, 2)},
    )


def by_fours(start, stop, body):
    def four(i, carry):
        for k in range(4):
            body(start + 4 * i + k)
        return carry

    lax.fori_loop(0, (stop - start) // 4, four, 0)


def raw_levels(raw, j):
    return lambda f, q: (raw.at[f][strided(q, j, R, 1), :], raw.at[f][strided(q, j, R, -1), :])


TALL = K + 16


def moved_chunk(q, shift=0):
    return pl.ds(8 + 8 * q + shift, 8)


def clear_ends(ref):
    ref[pl.ds(0, 8)] = jnp.zeros((8, W), F32)
    ref[pl.ds(8 + K, 8)] = jnp.zeros((8, W), F32)


def moved_levels(row):
    return lambda f, q: (row(f)[moved_chunk(q, 1)], row(f)[moved_chunk(q, -1)])


def rolled_levels(load, fields):
    after = {f: pltpu.roll(load(f), K - 1, 0) for f in fields}
    before = {f: pltpu.roll(load(f), 1, 0) for f in fields}
    return lambda f, q: (after[f][8 * q : 8 * q + 8], before[f][8 * q : 8 * q + 8])


def prepare(rows, raw, y_out, level_out, base_out):
    def levels(j):
        for k, value in enumerate(level_coefficients(rows[M, j])):
            level_out[j, k] = value

    by_fours(0, R, levels)

    def across(j):
        got = y_coefficients_at(lambda f, r: rows.at[f, r], j)
        for k in range(9):
            y_out[j - 2, k] = got[k]

    by_fours(2, R - 2, across)

    def first(j):
        def store(f, q, value):
            base_out.at[f, j - 2][chunk(q)] = value

        step_row(
            store,
            lambda f, d, q: rows.at[f, j + d][chunk(q)],
            y=y_out.at[j - 2],
            z=(level_out.at[j], raw_levels(raw, j)),
        )

    by_fours(2, R - 2, first)


def interior(*refs):
    rows, raw, left, right, merged, y_in, level_in, base_in = refs[:8]
    x_out, c1_out, part1_out, c2_out, part2_out, edge_out, merged1, halo_s, halo_mixed = refs[8:]
    lane = lanes()
    west_half = lane % G < HALO
    for f in range(4):
        for r in range(R - 4):
            clear_ends(c1_out.at[f, r])
    faces = [edge_faces(edges) for edges in (left, right)]
    halo_s[...] = jnp.where(west_half, faces[0][0], faces[1][0])
    halo_mixed[...] = jnp.where(west_half, faces[0][1], right[M])

    def x_body(j):
        hs, hm = halo_columns(halo_s[...], j), halo_columns(halo_mixed[...], j)
        m = rows[M, j]
        opened = m * shifted(m, hm, 1, lane)
        s = scaled(rows[U, j], opened)
        got = face_coefficients(
            {d: shifted(s, hs, d, lane) for d in (-2, -1, 0, 1)},
            {-1: shifted(opened, hm, -1, lane), 0: opened},
        )
        for k in range(9):
            x_out[j, k] = got[k]

    by_fours(0, R, x_body)

    partial = [edge_columns_and_levels(e, *f) for e, f in zip((left, right), faces)]
    across = edge_rows(merged, lambda f: merged[f])
    for f in range(4):
        edge = jnp.where(west_half, partial[0][f], partial[1][f])
        edge_out[f] = edge
        merged1[f] = edge + across[f]

    def halo(source, j):
        return lambda f, q: halo_columns(source.at[f][chunk(q)], j)

    def first(j):
        def store(f, q, value):
            c1_out.at[f, j - 2][moved_chunk(q)] = value

        step_row(
            store,
            lambda f, d, q: rows.at[f, j][chunk(q)],
            x=(x_out.at[j], halo(merged, j)),
            base=lambda f, q: base_in.at[f, j - 2][chunk(q)],
        )

    by_fours(2, R - 2, first)

    for i, j in enumerate((0, 1, R - 2, R - 1)):
        def store(f, q, value):
            part1_out.at[f, i][chunk(q)] = value

        step_row(
            store,
            lambda f, d, q: rows.at[f, j][chunk(q)],
            x=(x_out.at[j], halo(merged, j)),
            z=(level_in.at[j], raw_levels(raw, j)),
        )

    def second(j):
        def store(f, q, value):
            c2_out.at[f, j - 4][chunk(q)] = value

        step_row(
            store,
            lambda f, d, q: c1_out.at[f, j - 2 + d][moved_chunk(q)],
            x=(x_out.at[j], halo(merged1, j)),
            y=y_in.at[j - 2],
            z=(level_in.at[j], moved_levels(lambda f: c1_out.at[f, j - 2])),
        )

    by_fours(4, R - 4, second)

    for i, j in enumerate((2, 3, R - 4, R - 3)):
        def store(f, q, value):
            part2_out.at[f, i][chunk(q)] = value

        step_row(
            store,
            lambda f, d, q: c1_out.at[f, j - 2][moved_chunk(q)],
            x=(x_out.at[j], halo(merged1, j)),
            z=(level_in.at[j], moved_levels(lambda f: c1_out.at[f, j - 2])),
        )


def boundary(*refs):
    rows, merged, y_in, level_in, x_in, c1_in, part1_in, c2_in, part2_in, edge_in = refs[:10]
    second, first = refs[10:12]
    outs = refs[12:16]
    sides, x_new, y_new, level_new, c1_new, merged1, beyond = refs[16:]
    lane = lanes()
    place = lax.axis_index("ns")
    last = lax.axis_size("ns") - 1
    odd = place % 2
    inside = {SOUTH: place > 0, NORTH: place < last}
    near = (-2, -1, 0, 1, R - 2, R - 1, R, R + 1)
    new_at = {j: i for i, j in enumerate(near)}
    def unpack(b, carry):
        for message, side in ((second, odd), (first, 1 - odd)):
            here = jnp.where(side == NORTH, place < last, place > 0)
            sides[side, b] = jnp.where(here, message[b], 0.0)
        return carry

    lax.fori_loop(0, SIDE_BLOCKS, unpack, 0, unroll=2)

    def row(f, j):
        if j < 0:
            return sides.at[SOUTH, ROWS_AT[f] + j + (2 if f == U else HALO)]
        if j >= R:
            return sides.at[NORTH, ROWS_AT[f] + j - R]
        return rows.at[f, j]

    for f in range(FIELDS):
        south = turn(sides[SOUTH, CORNERS_AT], W - 2 * G - 2 * G * f)
        north = turn(sides[NORTH, CORNERS_AT], -2 * G * f)
        beyond[f] = jnp.where(lane >= W // 2, south, north)
    for f in range(4):
        for i in range(2, 6):
            clear_ends(c1_new.at[f, i])

    for f, across in enumerate(edge_rows(merged, lambda f: beyond[f])):
        merged1[f] = edge_in[f] + across

    def halo_beyond(f, j):
        return halo_columns(beyond[f], j % R)

    for j in near:
        got = y_coefficients_at(row, j)
        for k in range(9):
            y_new[new_at[j], k] = got[k]
        if not 0 <= j < R:
            got = x_coefficients(
                row(U, j)[...], halo_beyond(U, j), row(M, j)[...], halo_beyond(M, j), lane
            )
            for k in range(9):
                x_new[new_at[j], k] = got[k]
            for k, value in enumerate(level_coefficients(row(M, j)[...])):
                level_new[new_at[j], k] = value

    for j in near:
        side = SOUTH if j < R // 2 else NORTH

        def store(f, q, value):
            if f >= 2 and not 0 <= j < R:
                value = jnp.where(inside[side], value, 0.0)
            c1_new.at[f, new_at[j]][moved_chunk(q)] = value

        def load(f, d, q):
            return row(f, j + d)[chunk(q)]

        if 0 <= j < R:
            i = (0, 1, R - 2, R - 1).index(j)
            step_row(
                store, load, y=y_new.at[new_at[j]], base=lambda f, q: part1_in.at[f, i][chunk(q)]
            )
        else:
            halos = [halo_beyond(f, j) for f in range(4)]
            step_row(
                store,
                load,
                x=(x_new.at[new_at[j]], lambda f, q: halos[f][8 * q : 8 * q + 8]),
                y=y_new.at[new_at[j]],
                z=(level_new.at[new_at[j]], rolled_levels(lambda f: row(f, j)[...], range(4))),
            )

    def load1(f, j, q):
        if j in new_at:
            return c1_new.at[f, new_at[j]][moved_chunk(q)]
        return c1_in.at[f, j - 2][moved_chunk(q)]

    for j in (0, 1, 2, 3, R - 4, R - 3, R - 2, R - 1):
        def store(f, q, value):
            outs[f][pl.ds(8 * q * R + j, 8, stride=R), :] = value

        def load(f, d, q):
            return load1(f, j + d, q)

        if j in new_at:
            halos = [halo_columns(merged1[f], j) for f in range(4)]
            step_row(
                store,
                load,
                x=(x_in.at[j], lambda f, q: halos[f][8 * q : 8 * q + 8]),
                y=y_new.at[new_at[j]],
                z=(level_in.at[j], moved_levels(lambda f: c1_new.at[f, new_at[j]])),
            )
        else:
            i = (2, 3, R - 4, R - 3).index(j)
            step_row(
                store, load, y=y_in.at[j - 2], base=lambda f, q: part2_in.at[f, i][chunk(q)]
            )

    def copy(j, carry):
        for f in range(4):
            outs[f][pl.ds(j, K, stride=R), :] = c2_in[f, j - 4]
        return carry

    lax.fori_loop(4, R - 4, copy, 0, unroll=2)


def vmem():
    return pl.BlockSpec(memory_space=pltpu.VMEM)


def call(kernel, in_specs, out_shapes, scratch=(), limit=16 * MIB, cost=0.0):
    return pl.pallas_call(
        kernel,
        out_shape=[jax.ShapeDtypeStruct(shape, F32) for shape in out_shapes],
        in_specs=in_specs,
        out_specs=[vmem()] * len(out_shapes),
        scratch_shapes=list(scratch),
        compiler_params=pltpu.CompilerParams(vmem_limit_bytes=limit),
        cost_estimate=pl.CostEstimate(flops=0, bytes_accessed=int(cost * MIB), transcendentals=0),
    )


def partners(odd, n_ew, n_ns):
    pairs = []
    for e in range(n_ew):
        for s in range(n_ns):
            step = 1 if (s - odd) % 2 == 0 else -1
            if 0 <= s + step < n_ns:
                to = (e, s + step)
            else:
                to = (e ^ 1 if e ^ 1 < n_ew else e, s)
            pairs.append((e * n_ns + s, to[0] * n_ns + to[1]))
    return pairs


def local(temp, salt, u_east, v_north, wet, cot_temp, cot_salt):
    flat = [a.reshape(K * R, W) for a in (temp, salt, cot_temp, cot_salt, u_east, v_north, wet)]

    row = (K, W)
    padded = ((K + 2) * R, W)
    rows, raw, own, ew_first, ew_second = call(
        pack_edges,
        [pl.BlockSpec(memory_space=pltpu.HBM)] * FIELDS,
        [(FIELDS, R) + row, (4,) + padded, (FIELDS,) + row, (EDGE_ROWS, W), (EDGE_ROWS, W)],
        [
            pltpu.VMEM((2, K * R, W), F32),
            pltpu.VMEM((K * R, W), jnp.int32),
            pltpu.SemaphoreType.DMA((FIELDS,)),
        ],
    )(*[pltpu.with_memory_space_constraint(a, pltpu.HBM) for a in flat])

    n_ew, n_ns = lax.axis_size("ew"), lax.axis_size("ns")
    assert n_ew % 2 == 0
    ew_first = lax.ppermute(ew_first, "ew", [(i, i ^ 1) for i in range(n_ew)])
    ew_second = lax.ppermute(
        ew_second, "ew", [(i, (((i + 1) ^ 1) - 1) % n_ew) for i in range(n_ew)]
    )

    def swap(odd, message):
        return lax.ppermute(message, ("ew", "ns"), partners(odd, n_ew, n_ns))

    y_in, level, base = call(
        prepare,
        [vmem()] * 2,
        [(R - 4, 9) + row, (R, 3) + row, (4, R - 4) + row],
        cost=6,
    )(rows, raw)

    left, right, merged, second, first = call(
        pack_sides,
        [vmem()] * 4 + [pl.BlockSpec(memory_space=pl.ANY)],
        [(FIELDS,) + row] * 3 + [(SIDE_BLOCKS,) + row] * 2,
        cost=1,
    )(rows, own, ew_first, ew_second, level)
    second = swap(1, second)
    first = swap(0, first)

    x_in, c1, part1, c2, part2, edge = call(
        interior,
        [vmem()] * 8,
        [(R, 9) + row, (4, R - 4, TALL, W), (4, 4) + row, (4, R - 8) + row, (4, 4) + row, (4,) + row],
        [pltpu.VMEM((4,) + row, F32), pltpu.VMEM(row, F32), pltpu.VMEM(row, F32)],
        cost=20,
    )(rows, raw, left, right, merged, y_in, level, base)

    outs = call(
        boundary,
        [vmem()] * 12,
        [(K * R, W)] * 4,
        [
            pltpu.VMEM((2, SIDE_BLOCKS) + row, F32),
            pltpu.VMEM((8, 9) + row, F32),
            pltpu.VMEM((8, 9) + row, F32),
            pltpu.VMEM((8, 3) + row, F32),
            pltpu.VMEM((4, 8, TALL, W), F32),
            pltpu.VMEM((4,) + row, F32),
            pltpu.VMEM((FIELDS,) + row, F32),
        ],
        cost=20,
    )(
        *(rows, merged, y_in, level, x_in, c1, part1, c2, part2, edge),
        *(second, first),
    )
    return tuple(a.reshape(K, R, W) for a in outs)


def solution(mesh):
    spec = P(None, "ns", "ew")
    return jax.shard_map(
        local, mesh=mesh, in_specs=(spec,) * 7, out_specs=(spec,) * 4, check_vma=False
    )
```

```python
import jax
import jax.numpy as jnp
from jax import lax
from jax.experimental import pallas as pl
from jax.experimental.pallas import tpu as pltpu
from jax.sharding import PartitionSpec as P

horizontal_mix = 0.05
vertical_mix = 0.2

F32 = jnp.float32
K = 32
R = 16
W = 128
G = W // R
HALO = 4
FIELDS = 7
U, V, M = 4, 5, 6
PAIRS = ((0, 1), (2, 3), (U, M))
EDGE_ROWS = len(PAIRS) * K + 8
SIDE_BLOCKS = 27
ROWS_AT = (0, 4, 8, 12, 24, 16, 20)
CORNERS_AT = 26
SOUTH, NORTH = 0, 1
MIB = 1 << 20


def lanes():
    return lax.broadcasted_iota(jnp.int32, (K, W), 1)


def turn(x, amount):
    return pltpu.roll(x, amount % W, 1)


def pack_edges(*refs):
    sources = refs[:FIELDS]
    rows, raw, own, to_east, to_west, raw_flow, raw_wet, arrived = refs[FIELDS:]
    copies = []
    for f in range(FIELDS):
        target = raw.at[f, pl.ds(R, K * R)] if f < 4 else raw_wet if f == M else raw_flow.at[f - U]
        copies.append(pltpu.make_async_copy(sources[f], target, arrived.at[f]))
        copies[-1].start()
    for f in range(4):
        raw[f, pl.ds(0, R)] = jnp.zeros((R, W), F32)
        raw[f, pl.ds((K + 1) * R, R)] = jnp.zeros((R, W), F32)
    lane = lanes()
    group = lane // G
    packed = []
    for f in range(FIELDS):
        copies[f].wait()
        source = raw.at[f] if f < 4 else raw_wet if f == M else raw_flow.at[f - U]
        edges = jnp.zeros((K, W), F32)
        for r in range(R):
            x = source[pl.ds(R + r if f < 4 else r, K, stride=R), :].astype(F32)
            rows[f, r] = x
            edges = jnp.where(group == r, turn(x, G * r + HALO), edges)
        own[f] = edges
        packed.append(edges)
    west_half = lane % G < HALO
    for p, (f, g) in enumerate(PAIRS):
        a, b = packed[f], packed[g]
        to_east[pl.ds(p * K, K)] = jnp.where(west_half, a, turn(b, HALO))
        to_west[pl.ds(p * K, K)] = jnp.where(west_half, turn(b, -HALO), a)
    part = lane[:8] % G // 2
    for target, column in ((to_east, HALO - 2), (to_west, HALO)):
        block = jnp.zeros((8, W), F32)
        for q in range(K // 8):
            moved = turn(packed[V][8 * q : 8 * q + 8], 2 * q - column)
            block = jnp.where(part == q, moved, block)
        target[pl.ds(len(PAIRS) * K, 8)] = block


def pack_sides(rows, own, from_west, from_east, _, left, right, merged, second, first):
    odd = lax.axis_index("ns") % 2
    lane = lanes()
    west_half = lane % G < HALO
    halos = {}
    for p, (f, g) in enumerate(PAIRS):
        a, b = from_west[pl.ds(p * K, K)], from_east[pl.ds(p * K, K)]
        halos[f], halos[g] = (a, b), (turn(a, -HALO), turn(b, HALO))
    a, b = from_west[pl.ds(len(PAIRS) * K, 8)], from_east[pl.ds(len(PAIRS) * K, 8)]
    halos[V] = [
        jnp.concatenate([turn(x, column - 2 * q) for q in range(K // 8)], axis=0)
        for x, column in ((a, HALO - 2), (b, HALO))
    ]
    for f in range(FIELDS):
        a, b = halos[f]
        left[f] = jnp.where(west_half, a, own[f])
        right[f] = jnp.where(west_half, own[f], b)
        merged[f] = jnp.where(west_half, a, b)
    for out, north in ((second, odd), (first, 1 - odd)):
        for f in range(FIELDS):
            count = 2 if f == U else HALO
            start = (R - count) * north
            for r in range(count):
                out[ROWS_AT[f] + r] = rows[f, start + r]
        block = jnp.zeros((K, W), F32)
        for f in range(FIELDS):
            amount = lax.rem(2 * G * f + W - (W - 2 * G) * north, W)
            moved = pltpu.roll(merged[f], amount, 1)
            block = jnp.where(lane // (2 * G) == f, moved, block)
        out[CORNERS_AT] = block


def coefficients(speed, mask):
    opened = {d: mask[d] * mask[d + 1] for d in (-2, -1, 0, 1)}
    return face_coefficients({d: scaled(speed[d], opened[d]) for d in opened}, opened)


def scaled(speed, opened):
    return speed * opened * (1.0 / 12.0)


def face_coefficients(s, opened):
    a = {d: jnp.abs(s[d]) for d in s}
    w0 = {d: -(s[d] + a[d]) for d in (-1, 0, 1)}
    w3 = {d: a[d] - s[d] for d in (-2, -1, 0)}
    w1, w2 = {}, {}
    for d in (-1, 0):
        even, odd = 7.0 * s[d], 3.0 * a[d] + horizontal_mix * opened[d]
        w1[d], w2[d] = even + odd, even - odd
    forward = [w0[-1], w1[-1] - w0[0], w3[-1] - w2[0], -w3[0]]
    transposed = [-w3[-2], w3[-2] - w2[-1], w1[0] - w0[1], w0[1]]
    return forward + transposed + [w2[-1] - w1[0]]


def shifted(c, h, d, lane, step=1):
    if d == 0:
        return c
    if d > 0:
        return turn(jnp.where(lane < step * d, h, c), -step * d)
    return turn(jnp.where(lane >= W + step * d, h, c), -step * d)


def x_coefficients(u, uh, m, mh, lane):
    return coefficients(
        {d: shifted(u, uh, d, lane) for d in (-2, -1, 0, 1)},
        {d: shifted(m, mh, d, lane) for d in (-2, -1, 0, 1, 2)},
    )


def level_coefficients(m):
    inner = lax.broadcasted_iota(jnp.int32, (K, W), 0) < K - 1
    after = jnp.where(inner, vertical_mix * m * pltpu.roll(m, K - 1, 0), 0.0)
    before = pltpu.roll(after, 1, 0)
    return after, before, 1.0 - after - before


def chunk(q):
    return pl.ds(8 * q, 8)


def strided(q, j, stride, shift=0):
    return pl.ds((8 * q + 1 + shift) * stride + j, 8, stride=stride)


def step_row(store, load, x=None, y=None, z=None, base=None):
    lane = lanes()[:8]
    for q in range(K // 8):
        part = chunk(q)
        centre = None
        for term in (x and x[0].at[8], y and y.at[8], z and z[0].at[2]):
            if term is not None:
                centre = term[part] if centre is None else centre + term[part]
        if z:
            after, before = z[0].at[0][part], z[0].at[1][part]
        for direction in (0, 1):
            ks = range(4 * direction, 4 * direction + 4)
            xs = [x[0].at[k][part] for k in ks] if x else []
            ys = [y.at[k][part] for k in ks] if y else []
            for f in (2 * direction, 2 * direction + 1):
                c = load(f, 0, q)
                total = centre * c
                if base:
                    total += base(f, q)
                if x:
                    h = x[1](f, q)
                for coefficient, d in zip(xs, (-2, -1, 1, 2)):
                    total += coefficient * shifted(c, h, d, lane)
                for coefficient, d in zip(ys, (-2, -1, 1, 2)):
                    total += coefficient * load(f, d, q)
                if z:
                    c_after, c_before = z[1](f, q)
                    total += after * c_after + before * c_before
                store(f, q, total)


def halo_columns(merged, j):
    return turn(merged, -HALO - G * j)


def edge_faces(edges):
    opened = edges[M] * turn(edges[M], -1)
    return scaled(edges[U], opened), opened


def edge_columns_and_levels(edges, s, opened):
    m = edges[M]
    xs = face_coefficients(
        {d: turn(s, -d) if d else s for d in (-2, -1, 0, 1)}, {-1: turn(opened, 1), 0: opened}
    )
    after, before, centre = level_coefficients(m)
    results = []
    for f in range(4):
        c = edges[f]
        total = (centre + xs[8]) * c
        total += after * pltpu.roll(c, K - 1, 0) + before * pltpu.roll(c, 1, 0)
        for coefficient, d in zip(xs[4 * (f // 2) :], (-2, -1, 1, 2)):
            total += coefficient * turn(c, -d)
        results.append(total)
    return results


def edge_rows(merged, beyond):
    lane = lanes()
    v, m = merged[V], merged[M]
    vh, mh = beyond(V), beyond(M)
    ys = coefficients(
        {d: shifted(v, vh, d, lane, G) for d in (-2, -1, 0, 1)},
        {d: shifted(m, mh, d, lane, G) for d in (-2, -1, 0, 1, 2)},
    )
    results = []
    for f in range(4):
        c, ch = merged[f], beyond(f)
        total = ys[8] * c
        for coefficient, d in zip(ys[4 * (f // 2) :], (-2, -1, 1, 2)):
            total += coefficient * shifted(c, ch, d, lane, G)
        results.append(total)
    return results


def y_coefficients_at(row, j):
    return coefficients(
        {d: row(V, j + d)[...] for d in (-2, -1, 0, 1)},
        {d: row(M, j + d)[...] for d in (-2, -1, 0, 1, 2)},
    )


def by_fours(start, stop, body):
    def four(i, carry):
        for k in range(4):
            body(start + 4 * i + k)
        return carry

    lax.fori_loop(0, (stop - start) // 4, four, 0)


def by_fours_packed(start, stop, body, packed, turned):
    for f, source in enumerate(packed):
        turned[f] = turn(source, -G * start)

    def four(i, carry):
        for k in range(4):
            body(
                start + 4 * i + k,
                lambda f, part: turn(turned.at[f][part], W - HALO - G * k),
            )
        for f in range(len(packed)):
            turned[f] = turn(turned[f], -4 * G)
        return carry

    lax.fori_loop(0, (stop - start) // 4, four, 0)


def raw_levels(raw, j):
    return lambda f, q: (raw.at[f][strided(q, j, R, 1), :], raw.at[f][strided(q, j, R, -1), :])


TALL = K + 16


def moved_chunk(q, shift=0):
    return pl.ds(8 + 8 * q + shift, 8)


def clear_ends(ref):
    ref[pl.ds(0, 8)] = jnp.zeros((8, W), F32)
    ref[pl.ds(8 + K, 8)] = jnp.zeros((8, W), F32)


def moved_levels(row):
    return lambda f, q: (row(f)[moved_chunk(q, 1)], row(f)[moved_chunk(q, -1)])


def rolled_levels(load, fields):
    after = {f: pltpu.roll(load(f), K - 1, 0) for f in fields}
    before = {f: pltpu.roll(load(f), 1, 0) for f in fields}
    return lambda f, q: (after[f][8 * q : 8 * q + 8], before[f][8 * q : 8 * q + 8])


def prepare(rows, raw, y_out, level_out, base_out):
    def levels(j):
        for k, value in enumerate(level_coefficients(rows[M, j])):
            level_out[j, k] = value

    by_fours(0, R, levels)

    def across(j):
        got = y_coefficients_at(lambda f, r: rows.at[f, r], j)
        for k in range(9):
            y_out[j - 2, k] = got[k]

    by_fours(2, R - 2, across)

    def first(j):
        def store(f, q, value):
            base_out.at[f, j - 2][chunk(q)] = value

        step_row(
            store,
            lambda f, d, q: rows.at[f, j + d][chunk(q)],
            y=y_out.at[j - 2],
            z=(level_out.at[j], raw_levels(raw, j)),
        )

    by_fours(2, R - 2, first)


def interior(*refs):
    rows, raw, left, right, merged, y_in, level_in, base_in = refs[:8]
    x_out, c1_out, part1_out, c2_out, part2_out, edge_out, merged1, turned = refs[8:]
    lane = lanes()
    west_half = lane % G < HALO
    for f in range(4):
        for r in range(R - 4):
            clear_ends(c1_out.at[f, r])
    faces = [edge_faces(edges) for edges in (left, right)]
    halo_s = jnp.where(west_half, faces[0][0], faces[1][0])
    halo_mixed = jnp.where(west_half, faces[0][1], right[M])

    def x_body(j, halo):
        hs, hm = halo(0, pl.ds(0, K)), halo(1, pl.ds(0, K))
        m = rows[M, j]
        opened = m * shifted(m, hm, 1, lane)
        s = scaled(rows[U, j], opened)
        got = face_coefficients(
            {d: shifted(s, hs, d, lane) for d in (-2, -1, 0, 1)},
            {-1: shifted(opened, hm, -1, lane), 0: opened},
        )
        for k in range(9):
            x_out[j, k] = got[k]

    by_fours_packed(0, R, x_body, (halo_s, halo_mixed), turned)

    partial = [edge_columns_and_levels(e, *f) for e, f in zip((left, right), faces)]
    across = edge_rows(merged, lambda f: merged[f])
    for f in range(4):
        edge = jnp.where(west_half, partial[0][f], partial[1][f])
        edge_out[f] = edge
        merged1[f] = edge + across[f]

    def halo_at(source, j):
        return lambda f, q: halo_columns(source.at[f][chunk(q)], j)

    def first(j, halo):
        def store(f, q, value):
            c1_out.at[f, j - 2][moved_chunk(q)] = value

        step_row(
            store,
            lambda f, d, q: rows.at[f, j][chunk(q)],
            x=(x_out.at[j], lambda f, q: halo(f, chunk(q))),
            base=lambda f, q: base_in.at[f, j - 2][chunk(q)],
        )

    by_fours_packed(2, R - 2, first, [merged[f] for f in range(4)], turned)

    for i, j in enumerate((0, 1, R - 2, R - 1)):
        def store(f, q, value):
            part1_out.at[f, i][chunk(q)] = value

        step_row(
            store,
            lambda f, d, q: rows.at[f, j][chunk(q)],
            x=(x_out.at[j], halo_at(merged, j)),
            z=(level_in.at[j], raw_levels(raw, j)),
        )

    def second(j, halo):
        def store(f, q, value):
            c2_out.at[f, j - 4][chunk(q)] = value

        step_row(
            store,
            lambda f, d, q: c1_out.at[f, j - 2 + d][moved_chunk(q)],
            x=(x_out.at[j], lambda f, q: halo(f, chunk(q))),
            y=y_in.at[j - 2],
            z=(level_in.at[j], moved_levels(lambda f: c1_out.at[f, j - 2])),
        )

    by_fours_packed(4, R - 4, second, [merged1[f] for f in range(4)], turned)

    for i, j in enumerate((2, 3, R - 4, R - 3)):
        def store(f, q, value):
            part2_out.at[f, i][chunk(q)] = value

        step_row(
            store,
            lambda f, d, q: c1_out.at[f, j - 2][moved_chunk(q)],
            x=(x_out.at[j], halo_at(merged1, j)),
            z=(level_in.at[j], moved_levels(lambda f: c1_out.at[f, j - 2])),
        )


def boundary(*refs):
    rows, merged, y_in, level_in, x_in, c1_in, part1_in, c2_in, part2_in, edge_in = refs[:10]
    second, first = refs[10:12]
    outs = refs[12:16]
    sides, x_new, y_new, level_new, c1_new, merged1, beyond = refs[16:]
    lane = lanes()
    place = lax.axis_index("ns")
    last = lax.axis_size("ns") - 1
    odd = place % 2
    inside = {SOUTH: place > 0, NORTH: place < last}
    near = (-2, -1, 0, 1, R - 2, R - 1, R, R + 1)
    new_at = {j: i for i, j in enumerate(near)}
    def unpack(b, carry):
        for message, side in ((second, odd), (first, 1 - odd)):
            here = jnp.where(side == NORTH, place < last, place > 0)
            sides[side, b] = jnp.where(here, message[b], 0.0)
        return carry

    lax.fori_loop(0, SIDE_BLOCKS, unpack, 0, unroll=2)

    def row(f, j):
        if j < 0:
            return sides.at[SOUTH, ROWS_AT[f] + j + (2 if f == U else HALO)]
        if j >= R:
            return sides.at[NORTH, ROWS_AT[f] + j - R]
        return rows.at[f, j]

    for f in range(FIELDS):
        south = turn(sides[SOUTH, CORNERS_AT], W - 2 * G - 2 * G * f)
        north = turn(sides[NORTH, CORNERS_AT], -2 * G * f)
        beyond[f] = jnp.where(lane >= W // 2, south, north)
    for f in range(4):
        for i in range(2, 6):
            clear_ends(c1_new.at[f, i])

    for f, across in enumerate(edge_rows(merged, lambda f: beyond[f])):
        merged1[f] = edge_in[f] + across

    def halo_beyond(f, j):
        return halo_columns(beyond[f], j % R)

    for j in near:
        got = y_coefficients_at(row, j)
        for k in range(9):
            y_new[new_at[j], k] = got[k]
        if not 0 <= j < R:
            got = x_coefficients(
                row(U, j)[...], halo_beyond(U, j), row(M, j)[...], halo_beyond(M, j), lane
            )
            for k in range(9):
                x_new[new_at[j], k] = got[k]
            for k, value in enumerate(level_coefficients(row(M, j)[...])):
                level_new[new_at[j], k] = value

    for j in near:
        side = SOUTH if j < R // 2 else NORTH

        def store(f, q, value):
            if f >= 2 and not 0 <= j < R:
                value = jnp.where(inside[side], value, 0.0)
            c1_new.at[f, new_at[j]][moved_chunk(q)] = value

        def load(f, d, q):
            return row(f, j + d)[chunk(q)]

        if 0 <= j < R:
            i = (0, 1, R - 2, R - 1).index(j)
            step_row(
                store, load, y=y_new.at[new_at[j]], base=lambda f, q: part1_in.at[f, i][chunk(q)]
            )
        else:
            halos = [halo_beyond(f, j) for f in range(4)]
            step_row(
                store,
                load,
                x=(x_new.at[new_at[j]], lambda f, q: halos[f][8 * q : 8 * q + 8]),
                y=y_new.at[new_at[j]],
                z=(level_new.at[new_at[j]], rolled_levels(lambda f: row(f, j)[...], range(4))),
            )

    def load1(f, j, q):
        if j in new_at:
            return c1_new.at[f, new_at[j]][moved_chunk(q)]
        return c1_in.at[f, j - 2][moved_chunk(q)]

    for j in (0, 1, 2, 3, R - 4, R - 3, R - 2, R - 1):
        def store(f, q, value):
            outs[f][pl.ds(8 * q * R + j, 8, stride=R), :] = value

        def load(f, d, q):
            return load1(f, j + d, q)

        if j in new_at:
            halos = [halo_columns(merged1[f], j) for f in range(4)]
            step_row(
                store,
                load,
                x=(x_in.at[j], lambda f, q: halos[f][8 * q : 8 * q + 8]),
                y=y_new.at[new_at[j]],
                z=(level_in.at[j], moved_levels(lambda f: c1_new.at[f, new_at[j]])),
            )
        else:
            i = (2, 3, R - 4, R - 3).index(j)
            step_row(
                store, load, y=y_in.at[j - 2], base=lambda f, q: part2_in.at[f, i][chunk(q)]
            )

    def copy(j, carry):
        for f in range(4):
            outs[f][pl.ds(j, K, stride=R), :] = c2_in[f, j - 4]
        return carry

    lax.fori_loop(4, R - 4, copy, 0, unroll=2)


def vmem():
    return pl.BlockSpec(memory_space=pltpu.VMEM)


def call(kernel, in_specs, out_shapes, scratch=(), limit=16 * MIB, cost=0.0):
    return pl.pallas_call(
        kernel,
        out_shape=[jax.ShapeDtypeStruct(shape, F32) for shape in out_shapes],
        in_specs=in_specs,
        out_specs=[vmem()] * len(out_shapes),
        scratch_shapes=list(scratch),
        compiler_params=pltpu.CompilerParams(vmem_limit_bytes=limit),
        cost_estimate=pl.CostEstimate(flops=0, bytes_accessed=int(cost * MIB), transcendentals=0),
    )


def partners(odd, n_ew, n_ns):
    pairs = []
    for e in range(n_ew):
        for s in range(n_ns):
            step = 1 if (s - odd) % 2 == 0 else -1
            if 0 <= s + step < n_ns:
                to = (e, s + step)
            else:
                to = (e ^ 1 if e ^ 1 < n_ew else e, s)
            pairs.append((e * n_ns + s, to[0] * n_ns + to[1]))
    return pairs


def local(temp, salt, u_east, v_north, wet, cot_temp, cot_salt):
    flat = [a.reshape(K * R, W) for a in (temp, salt, cot_temp, cot_salt, u_east, v_north, wet)]

    row = (K, W)
    padded = ((K + 2) * R, W)
    rows, raw, own, to_east, to_west = call(
        pack_edges,
        [pl.BlockSpec(memory_space=pltpu.HBM)] * FIELDS,
        [(FIELDS, R) + row, (4,) + padded, (FIELDS,) + row, (EDGE_ROWS, W), (EDGE_ROWS, W)],
        [
            pltpu.VMEM((2, K * R, W), F32),
            pltpu.VMEM((K * R, W), jnp.int32),
            pltpu.SemaphoreType.DMA((FIELDS,)),
        ],
    )(*[pltpu.with_memory_space_constraint(a, pltpu.HBM) for a in flat])

    n_ew, n_ns = lax.axis_size("ew"), lax.axis_size("ns")
    from_west = lax.ppermute(to_east, "ew", [(i, (i + 1) % n_ew) for i in range(n_ew)])
    from_east = lax.ppermute(to_west, "ew", [((i + 1) % n_ew, i) for i in range(n_ew)])

    def swap(odd, message):
        return lax.ppermute(message, ("ew", "ns"), partners(odd, n_ew, n_ns))

    y_in, level, base = call(
        prepare,
        [vmem()] * 2,
        [(R - 4, 9) + row, (R, 3) + row, (4, R - 4) + row],
        cost=6,
    )(rows, raw)

    left, right, merged, second, first = call(
        pack_sides,
        [vmem()] * 4 + [pl.BlockSpec(memory_space=pl.ANY)],
        [(FIELDS,) + row] * 3 + [(SIDE_BLOCKS,) + row] * 2,
        cost=1,
    )(rows, own, from_west, from_east, level)
    second = swap(1, second)
    first = swap(0, first)

    x_in, c1, part1, c2, part2, edge = call(
        interior,
        [vmem()] * 8,
        [(R, 9) + row, (4, R - 4, TALL, W), (4, 4) + row, (4, R - 8) + row, (4, 4) + row, (4,) + row],
        [pltpu.VMEM((4,) + row, F32), pltpu.VMEM((4,) + row, F32)],
        cost=20,
    )(rows, raw, left, right, merged, y_in, level, base)

    outs = call(
        boundary,
        [vmem()] * 12,
        [(K * R, W)] * 4,
        [
            pltpu.VMEM((2, SIDE_BLOCKS) + row, F32),
            pltpu.VMEM((8, 9) + row, F32),
            pltpu.VMEM((8, 9) + row, F32),
            pltpu.VMEM((8, 3) + row, F32),
            pltpu.VMEM((4, 8, TALL, W), F32),
            pltpu.VMEM((4,) + row, F32),
            pltpu.VMEM((FIELDS,) + row, F32),
        ],
        cost=20,
    )(
        *(rows, merged, y_in, level, x_in, c1, part1, c2, part2, edge),
        *(second, first),
    )
    return tuple(a.reshape(K, R, W) for a in outs)


def solution(mesh):
    spec = P(None, "ns", "ew")
    return jax.shard_map(
        local, mesh=mesh, in_specs=(spec,) * 7, out_specs=(spec,) * 4, check_vma=False
    )
```

```python
import jax
import jax.numpy as jnp
from jax import lax
from jax.experimental import pallas as pl
from jax.experimental.pallas import tpu as pltpu
from jax.sharding import PartitionSpec as P

horizontal_mix = 0.05
vertical_mix = 0.2

F32 = jnp.float32
K = 32
R = 16
W = 128
G = W // R
HALO = 4
FIELDS = 7
U, V, M = 4, 5, 6
PAIRS = ((0, 1), (2, 3), (U, M))
EDGE_ROWS = len(PAIRS) * K + 8
SIDE_BLOCKS = 27
ROWS_AT = (0, 4, 8, 12, 24, 16, 20)
CORNERS_AT = 26
SOUTH, NORTH = 0, 1
MIB = 1 << 20


def lanes():
    return lax.broadcasted_iota(jnp.int32, (K, W), 1)


def turn(x, amount):
    return pltpu.roll(x, amount % W, 1)


def pack_edges(*refs):
    sources = refs[:FIELDS]
    rows, raw, own, to_east, to_west, raw_flow, raw_wet, arrived = refs[FIELDS:]
    copies = []
    for f in range(FIELDS):
        target = raw.at[f, pl.ds(R, K * R)] if f < 4 else raw_wet if f == M else raw_flow.at[f - U]
        copies.append(pltpu.make_async_copy(sources[f], target, arrived.at[f]))
        copies[-1].start()
    for f in range(4):
        raw[f, pl.ds(0, R)] = jnp.zeros((R, W), F32)
        raw[f, pl.ds((K + 1) * R, R)] = jnp.zeros((R, W), F32)
    lane = lanes()
    group = lane // G
    packed = []
    for f in range(FIELDS):
        copies[f].wait()
        source = raw.at[f] if f < 4 else raw_wet if f == M else raw_flow.at[f - U]
        edges = jnp.zeros((K, W), F32)
        for r in range(R):
            x = source[pl.ds(R + r if f < 4 else r, K, stride=R), :].astype(F32)
            rows[f, r] = x
            edges = jnp.where(group == r, turn(x, G * r + HALO), edges)
        own[f] = edges
        packed.append(edges)
    west_half = lane % G < HALO
    for p, (f, g) in enumerate(PAIRS):
        a, b = packed[f], packed[g]
        to_east[pl.ds(p * K, K)] = jnp.where(west_half, a, turn(b, HALO))
        to_west[pl.ds(p * K, K)] = jnp.where(west_half, turn(b, -HALO), a)
    part = lane[:8] % G // 2
    for target, column in ((to_east, HALO - 2), (to_west, HALO)):
        block = jnp.zeros((8, W), F32)
        for q in range(K // 8):
            moved = turn(packed[V][8 * q : 8 * q + 8], 2 * q - column)
            block = jnp.where(part == q, moved, block)
        target[pl.ds(len(PAIRS) * K, 8)] = block


def pack_sides(rows, own, from_west, from_east, _, left, right, merged, second, first):
    odd = lax.axis_index("ns") % 2
    lane = lanes()
    west_half = lane % G < HALO
    halos = {}
    for p, (f, g) in enumerate(PAIRS):
        a, b = from_west[pl.ds(p * K, K)], from_east[pl.ds(p * K, K)]
        halos[f], halos[g] = (a, b), (turn(a, -HALO), turn(b, HALO))
    a, b = from_west[pl.ds(len(PAIRS) * K, 8)], from_east[pl.ds(len(PAIRS) * K, 8)]
    halos[V] = [
        jnp.concatenate([turn(x, column - 2 * q) for q in range(K // 8)], axis=0)
        for x, column in ((a, HALO - 2), (b, HALO))
    ]
    for f in range(FIELDS):
        a, b = halos[f]
        left[f] = jnp.where(west_half, a, own[f])
        right[f] = jnp.where(west_half, own[f], b)
        merged[f] = jnp.where(west_half, a, b)
    for out, north in ((second, odd), (first, 1 - odd)):
        for f in range(FIELDS):
            count = 2 if f == U else HALO
            start = (R - count) * north
            for r in range(count):
                out[ROWS_AT[f] + r] = rows[f, start + r]
        block = jnp.zeros((K, W), F32)
        for f in range(FIELDS):
            amount = lax.rem(2 * G * f + W - (W - 2 * G) * north, W)
            moved = pltpu.roll(merged[f], amount, 1)
            block = jnp.where(lane // (2 * G) == f, moved, block)
        out[CORNERS_AT] = block


def coefficients(speed, mask):
    opened = {d: mask[d] * mask[d + 1] for d in (-2, -1, 0, 1)}
    return face_coefficients({d: scaled(speed[d], opened[d]) for d in opened}, opened)


def scaled(speed, opened):
    return speed * opened * (1.0 / 12.0)


def face_coefficients(s, opened):
    a = {d: jnp.abs(s[d]) for d in s}
    w0 = {d: -(s[d] + a[d]) for d in (-1, 0, 1)}
    w3 = {d: a[d] - s[d] for d in (-2, -1, 0)}
    w1, w2 = {}, {}
    for d in (-1, 0):
        even, odd = 7.0 * s[d], 3.0 * a[d] + horizontal_mix * opened[d]
        w1[d], w2[d] = even + odd, even - odd
    forward = [w0[-1], w1[-1] - w0[0], w3[-1] - w2[0], -w3[0]]
    transposed = [-w3[-2], w3[-2] - w2[-1], w1[0] - w0[1], w0[1]]
    return forward + transposed + [w2[-1] - w1[0]]


def shifted(c, h, d, lane, step=1):
    if d == 0:
        return c
    if d > 0:
        return turn(jnp.where(lane < step * d, h, c), -step * d)
    return turn(jnp.where(lane >= W + step * d, h, c), -step * d)


def x_coefficients(u, uh, m, mh, lane):
    return coefficients(
        {d: shifted(u, uh, d, lane) for d in (-2, -1, 0, 1)},
        {d: shifted(m, mh, d, lane) for d in (-2, -1, 0, 1, 2)},
    )


def level_coefficients(m):
    inner = lax.broadcasted_iota(jnp.int32, (K, W), 0) < K - 1
    after = jnp.where(inner, vertical_mix * m * pltpu.roll(m, K - 1, 0), 0.0)
    before = pltpu.roll(after, 1, 0)
    return after, before, 1.0 - after - before


def chunk(q):
    return pl.ds(8 * q, 8)


def strided(q, j, stride, shift=0):
    return pl.ds((8 * q + 1 + shift) * stride + j, 8, stride=stride)


def pipeline(items, issue, finish, depth=1):
    pending = []
    for item in items:
        pending.append((item, issue(item)))
        if len(pending) > depth:
            finish(*pending.pop(0))
    for late in pending:
        finish(*late)


def step_rows(jobs):
    lane = lanes()[:8]

    def issue(item):
        job, q = item
        if "x" not in job:
            return None
        halo = job["x"][1]
        rolled = []
        for f in range(4):
            c, h = job["load"](f, 0, q), halo(f, q)
            rolled.append([shifted(c, h, d, lane) for d in (-2, -1, 1, 2)])
        return rolled

    def finish(item, rolled):
        job, q = item
        x, y, z = job.get("x"), job.get("y"), job.get("z")
        load, part = job["load"], chunk(q)
        centre = None
        for term in (x and x[0].at[8], y and y.at[8], z and z[0].at[2]):
            if term is not None:
                centre = term[part] if centre is None else centre + term[part]
        if z:
            after, before = z[0].at[0][part], z[0].at[1][part]
        totals = []
        for f in range(4):
            total = centre * load(f, 0, q)
            if "base" in job:
                total += job["base"](f, q)
            if z:
                c_after, c_before = z[1](f, q)
                total += after * c_after + before * c_before
            totals.append(total)
        for coefficients_at, values in (
            (y, lambda f, i: load(f, (-2, -1, 1, 2)[i], q)),
            (x and x[0], lambda f, i: rolled[f][i]),
        ):
            if coefficients_at is None:
                continue
            for i in range(4):
                for direction in (0, 1):
                    coefficient = coefficients_at.at[4 * direction + i][part]
                    for f in (2 * direction, 2 * direction + 1):
                        totals[f] += coefficient * values(f, i)
        for f in range(4):
            job["store"](f, q, totals[f])

    pipeline([(job, q) for job in jobs for q in range(K // 8)], issue, finish)


def halo_columns(merged, j):
    return turn(merged, -HALO - G * j)


def edge_faces(edges):
    opened = edges[M] * turn(edges[M], -1)
    return scaled(edges[U], opened), opened


def edge_columns_and_levels(edges, s, opened):
    m = edges[M]
    xs = face_coefficients(
        {d: turn(s, -d) if d else s for d in (-2, -1, 0, 1)}, {-1: turn(opened, 1), 0: opened}
    )
    after, before, centre = level_coefficients(m)
    results = []
    for f in range(4):
        c = edges[f]
        total = (centre + xs[8]) * c
        total += after * pltpu.roll(c, K - 1, 0) + before * pltpu.roll(c, 1, 0)
        for coefficient, d in zip(xs[4 * (f // 2) :], (-2, -1, 1, 2)):
            total += coefficient * turn(c, -d)
        results.append(total)
    return results


def edge_rows(merged, beyond):
    lane = lanes()
    v, m = merged[V], merged[M]
    vh, mh = beyond(V), beyond(M)
    ys = coefficients(
        {d: shifted(v, vh, d, lane, G) for d in (-2, -1, 0, 1)},
        {d: shifted(m, mh, d, lane, G) for d in (-2, -1, 0, 1, 2)},
    )
    results = []
    for f in range(4):
        c, ch = merged[f], beyond(f)
        total = ys[8] * c
        for coefficient, d in zip(ys[4 * (f // 2) :], (-2, -1, 1, 2)):
            total += coefficient * shifted(c, ch, d, lane, G)
        results.append(total)
    return results


def y_coefficients_at(row, j):
    return coefficients(
        {d: row(V, j + d)[...] for d in (-2, -1, 0, 1)},
        {d: row(M, j + d)[...] for d in (-2, -1, 0, 1, 2)},
    )


def by_fours(start, stop, body):
    def four(i, carry):
        body([start + 4 * i + k for k in range(4)])
        return carry

    lax.fori_loop(0, (stop - start) // 4, four, 0)


def by_fours_packed(start, stop, body, packed, turned, halos):
    for f, source in enumerate(packed):
        turned[f] = turn(source, -G * start)

    def four(i, carry):
        for f in range(len(packed)):
            for k in range(4):
                halos[k, f] = turn(turned[f], -HALO - G * k)
        for f in range(len(packed)):
            turned[f] = turn(turned[f], -4 * G)
        body([start + 4 * i + k for k in range(4)])
        return carry

    lax.fori_loop(0, (stop - start) // 4, four, 0)


def raw_levels(raw, j):
    return lambda f, q: (raw.at[f][strided(q, j, R, 1), :], raw.at[f][strided(q, j, R, -1), :])


TALL = K + 16


def moved_chunk(q, shift=0):
    return pl.ds(8 + 8 * q + shift, 8)


def clear_ends(ref):
    ref[pl.ds(0, 8)] = jnp.zeros((8, W), F32)
    ref[pl.ds(8 + K, 8)] = jnp.zeros((8, W), F32)


def moved_levels(row):
    return lambda f, q: (row(f)[moved_chunk(q, 1)], row(f)[moved_chunk(q, -1)])


def rolled_levels(load, fields):
    after = {f: pltpu.roll(load(f), K - 1, 0) for f in fields}
    before = {f: pltpu.roll(load(f), 1, 0) for f in fields}
    return lambda f, q: (after[f][8 * q : 8 * q + 8], before[f][8 * q : 8 * q + 8])


def prepare(rows, raw, y_out, level_out, base_out):
    def levels(js):
        for j in js:
            for k, value in enumerate(level_coefficients(rows[M, j])):
                level_out[j, k] = value

    by_fours(0, R, levels)

    def across(js):
        for j in js:
            got = y_coefficients_at(lambda f, r: rows.at[f, r], j)
            for k in range(9):
                y_out[j - 2, k] = got[k]

    by_fours(2, R - 2, across)

    def first(js):
        def job(j):
            def store(f, q, value):
                base_out.at[f, j - 2][chunk(q)] = value

            return dict(
                store=store,
                load=lambda f, d, q: rows.at[f, j + d][chunk(q)],
                y=y_out.at[j - 2],
                z=(level_out.at[j], raw_levels(raw, j)),
            )

        step_rows([job(j) for j in js])

    by_fours(2, R - 2, first)


def interior(*refs):
    rows, raw, left, right, merged, y_in, level_in, base_in = refs[:8]
    x_out, c1_out, part1_out, c2_out, part2_out, edge_out, merged1, turned, halos, faces_now = refs[8:]
    lane = lanes()
    west_half = lane % G < HALO
    for f in range(4):
        for r in range(R - 4):
            clear_ends(c1_out.at[f, r])
    faces = [edge_faces(edges) for edges in (left, right)]
    halo_s = jnp.where(west_half, faces[0][0], faces[1][0])
    halo_mixed = jnp.where(west_half, faces[0][1], right[M])

    def x_body(js):
        for k, j in enumerate(js):
            m = rows[M, j]
            opened = m * shifted(m, halos[k, 1], 1, lane)
            faces_now[k, 0] = scaled(rows[U, j], opened)
            faces_now[k, 1] = opened

        def issue(item):
            k, q = item
            s, opened = faces_now.at[k, 0][chunk(q)], faces_now.at[k, 1][chunk(q)]
            hs, hm = halos.at[k, 0][chunk(q)], halos.at[k, 1][chunk(q)]
            return (
                {d: shifted(s, hs, d, lane[:8]) for d in (-2, -1, 0, 1)},
                {-1: shifted(opened, hm, -1, lane[:8]), 0: opened},
            )

        def finish(item, faces_here):
            k, q = item
            for i, value in enumerate(face_coefficients(*faces_here)):
                x_out.at[js[k], i][chunk(q)] = value

        pipeline([(k, q) for k in range(4) for q in range(K // 8)], issue, finish, 2)

    by_fours_packed(0, R, x_body, (halo_s, halo_mixed), turned, halos)

    partial = [edge_columns_and_levels(e, *f) for e, f in zip((left, right), faces)]
    across = edge_rows(merged, lambda f: merged[f])
    for f in range(4):
        edge = jnp.where(west_half, partial[0][f], partial[1][f])
        edge_out[f] = edge
        merged1[f] = edge + across[f]

    def kept(k):
        return lambda f, q: halos.at[k, f][chunk(q)]

    def keep(rows_now, source):
        for f in range(4):
            for k, j in enumerate(rows_now):
                halos[k, f] = halo_columns(source[f], j)

    def first(js):
        def job(k, j):
            def store(f, q, value):
                c1_out.at[f, j - 2][moved_chunk(q)] = value

            return dict(
                store=store,
                load=lambda f, d, q: rows.at[f, j][chunk(q)],
                x=(x_out.at[j], kept(k)),
                base=lambda f, q: base_in.at[f, j - 2][chunk(q)],
            )

        step_rows([job(k, j) for k, j in enumerate(js)])

    by_fours_packed(2, R - 2, first, [merged[f] for f in range(4)], turned, halos)

    def first_part(i, j):
        def store(f, q, value):
            part1_out.at[f, i][chunk(q)] = value

        return dict(
            store=store,
            load=lambda f, d, q: rows.at[f, j][chunk(q)],
            x=(x_out.at[j], kept(i)),
            z=(level_in.at[j], raw_levels(raw, j)),
        )

    ends = (0, 1, R - 2, R - 1)
    keep(ends, merged)
    step_rows([first_part(i, j) for i, j in enumerate(ends)])

    def second(js):
        def job(k, j):
            def store(f, q, value):
                c2_out.at[f, j - 4][chunk(q)] = value

            return dict(
                store=store,
                load=lambda f, d, q: c1_out.at[f, j - 2 + d][moved_chunk(q)],
                x=(x_out.at[j], kept(k)),
                y=y_in.at[j - 2],
                z=(level_in.at[j], moved_levels(lambda f: c1_out.at[f, j - 2])),
            )

        step_rows([job(k, j) for k, j in enumerate(js)])

    by_fours_packed(4, R - 4, second, [merged1[f] for f in range(4)], turned, halos)

    def second_part(i, j):
        def store(f, q, value):
            part2_out.at[f, i][chunk(q)] = value

        return dict(
            store=store,
            load=lambda f, d, q: c1_out.at[f, j - 2][moved_chunk(q)],
            x=(x_out.at[j], kept(i)),
            z=(level_in.at[j], moved_levels(lambda f: c1_out.at[f, j - 2])),
        )

    ends = (2, 3, R - 4, R - 3)
    keep(ends, merged1)
    step_rows([second_part(i, j) for i, j in enumerate(ends)])


def boundary(*refs):
    rows, merged, y_in, level_in, x_in, c1_in, part1_in, c2_in, part2_in, edge_in = refs[:10]
    second, first = refs[10:12]
    outs = refs[12:16]
    sides, x_new, y_new, level_new, c1_new, merged1, beyond, halos = refs[16:]
    lane = lanes()
    place = lax.axis_index("ns")
    last = lax.axis_size("ns") - 1
    odd = place % 2
    inside = {SOUTH: place > 0, NORTH: place < last}
    near = (-2, -1, 0, 1, R - 2, R - 1, R, R + 1)
    new_at = {j: i for i, j in enumerate(near)}
    def unpack(b, carry):
        for message, side in ((second, odd), (first, 1 - odd)):
            here = jnp.where(side == NORTH, place < last, place > 0)
            sides[side, b] = jnp.where(here, message[b], 0.0)
        return carry

    lax.fori_loop(0, SIDE_BLOCKS, unpack, 0, unroll=2)

    def row(f, j):
        if j < 0:
            return sides.at[SOUTH, ROWS_AT[f] + j + (2 if f == U else HALO)]
        if j >= R:
            return sides.at[NORTH, ROWS_AT[f] + j - R]
        return rows.at[f, j]

    for f in range(FIELDS):
        south = turn(sides[SOUTH, CORNERS_AT], W - 2 * G - 2 * G * f)
        north = turn(sides[NORTH, CORNERS_AT], -2 * G * f)
        beyond[f] = jnp.where(lane >= W // 2, south, north)
    for f in range(4):
        for i in range(2, 6):
            clear_ends(c1_new.at[f, i])

    for f, across in enumerate(edge_rows(merged, lambda f: beyond[f])):
        merged1[f] = edge_in[f] + across

    def halo_beyond(f, j):
        return halo_columns(beyond[f], j % R)

    for j in near:
        got = y_coefficients_at(row, j)
        for k in range(9):
            y_new[new_at[j], k] = got[k]
        if not 0 <= j < R:
            got = x_coefficients(
                row(U, j)[...], halo_beyond(U, j), row(M, j)[...], halo_beyond(M, j), lane
            )
            for k in range(9):
                x_new[new_at[j], k] = got[k]
            for k, value in enumerate(level_coefficients(row(M, j)[...])):
                level_new[new_at[j], k] = value

    out_rows = [j for j in near if not 0 <= j < R]
    for f in range(4):
        for i, j in enumerate(out_rows):
            halos[i, f] = halo_beyond(f, j)

    def kept(k):
        return lambda f, q: halos.at[k, f][chunk(q)]

    def first_job(j):
        side = SOUTH if j < R // 2 else NORTH

        def store(f, q, value):
            if f >= 2 and not 0 <= j < R:
                value = jnp.where(inside[side], value, 0.0)
            c1_new.at[f, new_at[j]][moved_chunk(q)] = value

        job = dict(
            store=store, load=lambda f, d, q: row(f, j + d)[chunk(q)], y=y_new.at[new_at[j]]
        )
        if 0 <= j < R:
            i = (0, 1, R - 2, R - 1).index(j)
            return job | dict(base=lambda f, q: part1_in.at[f, i][chunk(q)])
        return job | dict(
            x=(x_new.at[new_at[j]], kept(out_rows.index(j))),
            z=(level_new.at[new_at[j]], rolled_levels(lambda f: row(f, j)[...], range(4))),
        )

    step_rows([first_job(j) for j in (-2, 0, -1, 1, R, R - 2, R + 1, R - 1)])

    def load1(f, j, q):
        if j in new_at:
            return c1_new.at[f, new_at[j]][moved_chunk(q)]
        return c1_in.at[f, j - 2][moved_chunk(q)]

    ends = (0, 1, R - 2, R - 1)
    for f in range(4):
        for i, j in enumerate(ends):
            halos[i, f] = halo_columns(merged1[f], j)

    def second_job(j):
        def store(f, q, value):
            outs[f][pl.ds(8 * q * R + j, 8, stride=R), :] = value

        job = dict(store=store, load=lambda f, d, q: load1(f, j + d, q))
        if j in ends:
            return job | dict(
                x=(x_in.at[j], kept(ends.index(j))),
                y=y_new.at[new_at[j]],
                z=(level_in.at[j], moved_levels(lambda f: c1_new.at[f, new_at[j]])),
            )
        i = (2, 3, R - 4, R - 3).index(j)
        return job | dict(y=y_in.at[j - 2], base=lambda f, q: part2_in.at[f, i][chunk(q)])

    step_rows([second_job(j) for j in (0, 2, 1, 3, R - 2, R - 4, R - 1, R - 3)])

    def copy(j, carry):
        for f in range(4):
            outs[f][pl.ds(j, K, stride=R), :] = c2_in[f, j - 4]
        return carry

    lax.fori_loop(4, R - 4, copy, 0, unroll=2)


def vmem():
    return pl.BlockSpec(memory_space=pltpu.VMEM)


def call(kernel, in_specs, out_shapes, scratch=(), limit=16 * MIB, cost=0.0):
    return pl.pallas_call(
        kernel,
        out_shape=[jax.ShapeDtypeStruct(shape, F32) for shape in out_shapes],
        in_specs=in_specs,
        out_specs=[vmem()] * len(out_shapes),
        scratch_shapes=list(scratch),
        compiler_params=pltpu.CompilerParams(vmem_limit_bytes=limit),
        cost_estimate=pl.CostEstimate(flops=0, bytes_accessed=int(cost * MIB), transcendentals=0),
    )


def partners(odd, n_ew, n_ns):
    pairs = []
    for e in range(n_ew):
        for s in range(n_ns):
            step = 1 if (s - odd) % 2 == 0 else -1
            if 0 <= s + step < n_ns:
                to = (e, s + step)
            else:
                to = (e ^ 1 if e ^ 1 < n_ew else e, s)
            pairs.append((e * n_ns + s, to[0] * n_ns + to[1]))
    return pairs


def local(temp, salt, u_east, v_north, wet, cot_temp, cot_salt):
    flat = [a.reshape(K * R, W) for a in (temp, salt, cot_temp, cot_salt, u_east, v_north, wet)]

    row = (K, W)
    padded = ((K + 2) * R, W)
    rows, raw, own, to_east, to_west = call(
        pack_edges,
        [pl.BlockSpec(memory_space=pltpu.HBM)] * FIELDS,
        [(FIELDS, R) + row, (4,) + padded, (FIELDS,) + row, (EDGE_ROWS, W), (EDGE_ROWS, W)],
        [
            pltpu.VMEM((2, K * R, W), F32),
            pltpu.VMEM((K * R, W), jnp.int32),
            pltpu.SemaphoreType.DMA((FIELDS,)),
        ],
    )(*[pltpu.with_memory_space_constraint(a, pltpu.HBM) for a in flat])

    n_ew, n_ns = lax.axis_size("ew"), lax.axis_size("ns")
    from_west = lax.ppermute(to_east, "ew", [(i, (i + 1) % n_ew) for i in range(n_ew)])
    from_east = lax.ppermute(to_west, "ew", [((i + 1) % n_ew, i) for i in range(n_ew)])

    def swap(odd, message):
        return lax.ppermute(message, ("ew", "ns"), partners(odd, n_ew, n_ns))

    y_in, level, base = call(
        prepare,
        [vmem()] * 2,
        [(R - 4, 9) + row, (R, 3) + row, (4, R - 4) + row],
        cost=6,
    )(rows, raw)

    left, right, merged, second, first = call(
        pack_sides,
        [vmem()] * 4 + [pl.BlockSpec(memory_space=pl.ANY)],
        [(FIELDS,) + row] * 3 + [(SIDE_BLOCKS,) + row] * 2,
        cost=1,
    )(rows, own, from_west, from_east, level)
    second = swap(1, second)
    first = swap(0, first)

    x_in, c1, part1, c2, part2, edge = call(
        interior,
        [vmem()] * 8,
        [(R, 9) + row, (4, R - 4, TALL, W), (4, 4) + row, (4, R - 8) + row, (4, 4) + row, (4,) + row],
        [
            pltpu.VMEM((4,) + row, F32),
            pltpu.VMEM((4,) + row, F32),
            pltpu.VMEM((4, 4) + row, F32),
            pltpu.VMEM((4, 2) + row, F32),
        ],
        cost=20,
    )(rows, raw, left, right, merged, y_in, level, base)

    outs = call(
        boundary,
        [vmem()] * 12,
        [(K * R, W)] * 4,
        [
            pltpu.VMEM((2, SIDE_BLOCKS) + row, F32),
            pltpu.VMEM((8, 9) + row, F32),
            pltpu.VMEM((8, 9) + row, F32),
            pltpu.VMEM((8, 3) + row, F32),
            pltpu.VMEM((4, 8, TALL, W), F32),
            pltpu.VMEM((4,) + row, F32),
            pltpu.VMEM((FIELDS,) + row, F32),
            pltpu.VMEM((4, 4) + row, F32),
        ],
        cost=20,
    )(
        *(rows, merged, y_in, level, x_in, c1, part1, c2, part2, edge),
        *(second, first),
    )
    return tuple(a.reshape(K, R, W) for a in outs)


def solution(mesh):
    spec = P(None, "ns", "ew")
    return jax.shard_map(
        local, mesh=mesh, in_specs=(spec,) * 7, out_specs=(spec,) * 4, check_vma=False
    )
```

```python
import jax
import jax.numpy as jnp
from jax import lax
from jax.experimental import pallas as pl
from jax.experimental.pallas import tpu as pltpu
from jax.sharding import PartitionSpec as P

horizontal_mix = 0.05
vertical_mix = 0.2

F32 = jnp.float32
K = 32
R = 16
W = 128
G = W // R
HALO = 4
FIELDS = 7
U, V, M = 4, 5, 6
PAIRS = ((0, 1), (2, 3), (U, M))
EDGE_ROWS = len(PAIRS) * K + 8
SIDE_BLOCKS = 26
ROWS_AT = (0, 4, 8, 12, 24, 16, 20)
SOUTH, NORTH = 0, 1
MIB = 1 << 20
FLOPS_PER_US = 1.15e9


def lanes():
    return lax.broadcasted_iota(jnp.int32, (K, W), 1)


def turn(x, amount):
    return pltpu.roll(x, amount % W, 1)


def pack_edges(*refs):
    sources = refs[:FIELDS]
    rows, raw, own, to_east, to_west, raw_flow, raw_wet, arrived = refs[FIELDS:]
    copies = []
    for f in range(FIELDS):
        target = raw.at[f, pl.ds(R, K * R)] if f < 4 else raw_wet if f == M else raw_flow.at[f - U]
        copies.append(pltpu.make_async_copy(sources[f], target, arrived.at[f]))
        copies[-1].start()
    for f in range(4):
        raw[f, pl.ds(0, R)] = jnp.zeros((R, W), F32)
        raw[f, pl.ds((K + 1) * R, R)] = jnp.zeros((R, W), F32)
    lane = lanes()
    group = lane // G
    packed = []
    for f in range(FIELDS):
        copies[f].wait()
        source = raw.at[f] if f < 4 else raw_wet if f == M else raw_flow.at[f - U]
        edges = jnp.zeros((K, W), F32)
        for r in range(R):
            x = source[pl.ds(R + r if f < 4 else r, K, stride=R), :].astype(F32)
            rows[f, r] = x
            edges = jnp.where(group == r, turn(x, G * r + HALO), edges)
        own[f] = edges
        packed.append(edges)
    west_half = lane % G < HALO
    for p, (f, g) in enumerate(PAIRS):
        a, b = packed[f], packed[g]
        to_east[pl.ds(p * K, K)] = jnp.where(west_half, a, turn(b, HALO))
        to_west[pl.ds(p * K, K)] = jnp.where(west_half, turn(b, -HALO), a)
    part = lane[:8] % G // 2
    for target, column in ((to_east, HALO - 2), (to_west, HALO)):
        block = jnp.zeros((8, W), F32)
        for q in range(K // 8):
            moved = turn(packed[V][8 * q : 8 * q + 8], 2 * q - column)
            block = jnp.where(part == q, moved, block)
        target[pl.ds(len(PAIRS) * K, 8)] = block


def pack_sides(rows, second, first):
    odd = lax.axis_index("ns") % 2
    for out, north in ((second, odd), (first, 1 - odd)):
        for f in range(FIELDS):
            count = 2 if f == U else HALO
            start = (R - count) * north
            for r in range(count):
                out[ROWS_AT[f] + r] = rows[f, start + r]


def pack_corners(own, from_west, from_east, _, left, right, merged, second, first):
    odd = lax.axis_index("ns") % 2
    lane = lanes()
    west_half = lane % G < HALO
    halos = {}
    for p, (f, g) in enumerate(PAIRS):
        a, b = from_west[pl.ds(p * K, K)], from_east[pl.ds(p * K, K)]
        halos[f], halos[g] = (a, b), (turn(a, -HALO), turn(b, HALO))
    a, b = from_west[pl.ds(len(PAIRS) * K, 8)], from_east[pl.ds(len(PAIRS) * K, 8)]
    halos[V] = [
        jnp.concatenate([turn(x, column - 2 * q) for q in range(K // 8)], axis=0)
        for x, column in ((a, HALO - 2), (b, HALO))
    ]
    for f in range(FIELDS):
        a, b = halos[f]
        left[f] = jnp.where(west_half, a, own[f])
        right[f] = jnp.where(west_half, own[f], b)
        merged[f] = jnp.where(west_half, a, b)
    for out, north in ((second, odd), (first, 1 - odd)):
        block = jnp.zeros((K, W), F32)
        for f in range(FIELDS):
            amount = lax.rem(2 * G * f + W - (W - 2 * G) * north, W)
            moved = pltpu.roll(merged[f], amount, 1)
            block = jnp.where(lane // (2 * G) == f, moved, block)
        out[...] = block


def coefficients(speed, mask):
    opened = {d: mask[d] * mask[d + 1] for d in (-2, -1, 0, 1)}
    return face_coefficients({d: scaled(speed[d], opened[d]) for d in opened}, opened)


def scaled(speed, opened):
    return speed * opened * (1.0 / 12.0)


def face_coefficients(s, opened):
    a = {d: jnp.abs(s[d]) for d in s}
    w0 = {d: -(s[d] + a[d]) for d in (-1, 0, 1)}
    w3 = {d: a[d] - s[d] for d in (-2, -1, 0)}
    w1, w2 = {}, {}
    for d in (-1, 0):
        even, odd = 7.0 * s[d], 3.0 * a[d] + horizontal_mix * opened[d]
        w1[d], w2[d] = even + odd, even - odd
    forward = [w0[-1], w1[-1] - w0[0], w3[-1] - w2[0], -w3[0]]
    transposed = [-w3[-2], w3[-2] - w2[-1], w1[0] - w0[1], w0[1]]
    return forward + transposed + [w2[-1] - w1[0]]


def shifted(c, h, d, lane, step=1):
    if d == 0:
        return c
    if d > 0:
        return turn(jnp.where(lane < step * d, h, c), -step * d)
    return turn(jnp.where(lane >= W + step * d, h, c), -step * d)


def x_coefficients(u, uh, m, mh, lane):
    return coefficients(
        {d: shifted(u, uh, d, lane) for d in (-2, -1, 0, 1)},
        {d: shifted(m, mh, d, lane) for d in (-2, -1, 0, 1, 2)},
    )


def level_coefficients(m):
    inner = lax.broadcasted_iota(jnp.int32, (K, W), 0) < K - 1
    after = jnp.where(inner, vertical_mix * m * pltpu.roll(m, K - 1, 0), 0.0)
    before = pltpu.roll(after, 1, 0)
    return after, before, 1.0 - after - before


def chunk(q):
    return pl.ds(8 * q, 8)


def strided(q, j, stride, shift=0):
    return pl.ds((8 * q + 1 + shift) * stride + j, 8, stride=stride)


def pipeline(items, issue, finish, depth=1):
    pending = []
    for item in items:
        pending.append((item, issue(item)))
        if len(pending) > depth:
            finish(*pending.pop(0))
    for late in pending:
        finish(*late)


def step_rows(jobs):
    lane = lanes()[:8]

    def issue(item):
        job, q = item
        if "x" not in job:
            return None
        halo = job["x"][1]
        rolled = []
        for f in range(4):
            c, h = job["load"](f, 0, q), halo(f, q)
            rolled.append([shifted(c, h, d, lane) for d in (-2, -1, 1, 2)])
        return rolled

    def finish(item, rolled):
        job, q = item
        x, y, z = job.get("x"), job.get("y"), job.get("z")
        load, part = job["load"], chunk(q)
        centre = None
        for term in (x and x[0].at[8], y and y.at[8], z and z[0].at[2]):
            if term is not None:
                centre = term[part] if centre is None else centre + term[part]
        if z:
            after, before = z[0].at[0][part], z[0].at[1][part]
        totals = []
        for f in range(4):
            total = centre * load(f, 0, q)
            if "base" in job:
                total += job["base"](f, q)
            if z:
                c_after, c_before = z[1](f, q)
                total += after * c_after + before * c_before
            totals.append(total)
        for coefficients_at, values in (
            (y, lambda f, i: load(f, (-2, -1, 1, 2)[i], q)),
            (x and x[0], lambda f, i: rolled[f][i]),
        ):
            if coefficients_at is None:
                continue
            for i in range(4):
                for direction in (0, 1):
                    coefficient = coefficients_at.at[4 * direction + i][part]
                    for f in (2 * direction, 2 * direction + 1):
                        totals[f] += coefficient * values(f, i)
        for f in range(4):
            job["store"](f, q, totals[f])

    pipeline([(job, q) for job in jobs for q in range(K // 8)], issue, finish)


def halo_columns(merged, j):
    return turn(merged, -HALO - G * j)


def edge_faces(edges):
    opened = edges[M] * turn(edges[M], -1)
    return scaled(edges[U], opened), opened


def edge_columns_and_levels(edges, s, opened):
    m = edges[M]
    xs = face_coefficients(
        {d: turn(s, -d) if d else s for d in (-2, -1, 0, 1)}, {-1: turn(opened, 1), 0: opened}
    )
    after, before, centre = level_coefficients(m)
    results = []
    for f in range(4):
        c = edges[f]
        total = (centre + xs[8]) * c
        total += after * pltpu.roll(c, K - 1, 0) + before * pltpu.roll(c, 1, 0)
        for coefficient, d in zip(xs[4 * (f // 2) :], (-2, -1, 1, 2)):
            total += coefficient * turn(c, -d)
        results.append(total)
    return results


def edge_rows(merged, beyond):
    lane = lanes()
    v, m = merged[V], merged[M]
    vh, mh = beyond(V), beyond(M)
    ys = coefficients(
        {d: shifted(v, vh, d, lane, G) for d in (-2, -1, 0, 1)},
        {d: shifted(m, mh, d, lane, G) for d in (-2, -1, 0, 1, 2)},
    )
    results = []
    for f in range(4):
        c, ch = merged[f], beyond(f)
        total = ys[8] * c
        for coefficient, d in zip(ys[4 * (f // 2) :], (-2, -1, 1, 2)):
            total += coefficient * shifted(c, ch, d, lane, G)
        results.append(total)
    return results


def y_coefficients_at(row, j):
    return coefficients(
        {d: row(V, j + d)[...] for d in (-2, -1, 0, 1)},
        {d: row(M, j + d)[...] for d in (-2, -1, 0, 1, 2)},
    )


def by_fours(start, stop, body):
    def four(i, carry):
        body([start + 4 * i + k for k in range(4)])
        return carry

    lax.fori_loop(0, (stop - start) // 4, four, 0)


def by_fours_packed(start, stop, body, packed, turned, halos):
    for f, source in enumerate(packed):
        turned[f] = turn(source, -G * start)

    def four(i, carry):
        for f in range(len(packed)):
            for k in range(4):
                halos[k, f] = turn(turned[f], -HALO - G * k)
        for f in range(len(packed)):
            turned[f] = turn(turned[f], -4 * G)
        body([start + 4 * i + k for k in range(4)])
        return carry

    lax.fori_loop(0, (stop - start) // 4, four, 0)


def raw_levels(raw, j):
    return lambda f, q: (raw.at[f][strided(q, j, R, 1), :], raw.at[f][strided(q, j, R, -1), :])


TALL = K + 16


def moved_chunk(q, shift=0):
    return pl.ds(8 + 8 * q + shift, 8)


def clear_ends(ref):
    ref[pl.ds(0, 8)] = jnp.zeros((8, W), F32)
    ref[pl.ds(8 + K, 8)] = jnp.zeros((8, W), F32)


def moved_levels(row):
    return lambda f, q: (row(f)[moved_chunk(q, 1)], row(f)[moved_chunk(q, -1)])


def rolled_levels(load, fields):
    after = {f: pltpu.roll(load(f), K - 1, 0) for f in fields}
    before = {f: pltpu.roll(load(f), 1, 0) for f in fields}
    return lambda f, q: (after[f][8 * q : 8 * q + 8], before[f][8 * q : 8 * q + 8])


def prepare(rows, raw, y_out, level_out, base_out):
    def levels(js):
        for j in js:
            for k, value in enumerate(level_coefficients(rows[M, j])):
                level_out[j, k] = value

    by_fours(0, R, levels)

    def across(js):
        for j in js:
            got = y_coefficients_at(lambda f, r: rows.at[f, r], j)
            for k in range(9):
                y_out[j - 2, k] = got[k]

    by_fours(2, R - 2, across)

    def first(js):
        def job(j):
            def store(f, q, value):
                base_out.at[f, j - 2][chunk(q)] = value

            return dict(
                store=store,
                load=lambda f, d, q: rows.at[f, j + d][chunk(q)],
                y=y_out.at[j - 2],
                z=(level_out.at[j], raw_levels(raw, j)),
            )

        step_rows([job(j) for j in js])

    by_fours(2, R - 2, first)


def interior(*refs):
    rows, raw, left, right, merged, y_in, level_in, base_in = refs[:8]
    x_out, c1_out, part1_out, c2_out, part2_out, edge_out, merged1, turned, halos, faces_now = refs[8:]
    lane = lanes()
    west_half = lane % G < HALO
    for f in range(4):
        for r in range(R - 4):
            clear_ends(c1_out.at[f, r])
    faces = [edge_faces(edges) for edges in (left, right)]
    halo_s = jnp.where(west_half, faces[0][0], faces[1][0])
    halo_mixed = jnp.where(west_half, faces[0][1], right[M])

    def x_body(js):
        for k, j in enumerate(js):
            m = rows[M, j]
            opened = m * shifted(m, halos[k, 1], 1, lane)
            faces_now[k, 0] = scaled(rows[U, j], opened)
            faces_now[k, 1] = opened

        def issue(item):
            k, q = item
            s, opened = faces_now.at[k, 0][chunk(q)], faces_now.at[k, 1][chunk(q)]
            hs, hm = halos.at[k, 0][chunk(q)], halos.at[k, 1][chunk(q)]
            return (
                {d: shifted(s, hs, d, lane[:8]) for d in (-2, -1, 0, 1)},
                {-1: shifted(opened, hm, -1, lane[:8]), 0: opened},
            )

        def finish(item, faces_here):
            k, q = item
            for i, value in enumerate(face_coefficients(*faces_here)):
                x_out.at[js[k], i][chunk(q)] = value

        pipeline([(k, q) for k in range(4) for q in range(K // 8)], issue, finish, 2)

    by_fours_packed(0, R, x_body, (halo_s, halo_mixed), turned, halos)

    partial = [edge_columns_and_levels(e, *f) for e, f in zip((left, right), faces)]
    across = edge_rows(merged, lambda f: merged[f])
    for f in range(4):
        edge = jnp.where(west_half, partial[0][f], partial[1][f])
        edge_out[f] = edge
        merged1[f] = edge + across[f]

    def kept(k):
        return lambda f, q: halos.at[k, f][chunk(q)]

    def keep(rows_now, source):
        for f in range(4):
            for k, j in enumerate(rows_now):
                halos[k, f] = halo_columns(source[f], j)

    def first(js):
        def job(k, j):
            def store(f, q, value):
                c1_out.at[f, j - 2][moved_chunk(q)] = value

            return dict(
                store=store,
                load=lambda f, d, q: rows.at[f, j][chunk(q)],
                x=(x_out.at[j], kept(k)),
                base=lambda f, q: base_in.at[f, j - 2][chunk(q)],
            )

        step_rows([job(k, j) for k, j in enumerate(js)])

    by_fours_packed(2, R - 2, first, [merged[f] for f in range(4)], turned, halos)

    def first_part(i, j):
        def store(f, q, value):
            part1_out.at[f, i][chunk(q)] = value

        return dict(
            store=store,
            load=lambda f, d, q: rows.at[f, j][chunk(q)],
            x=(x_out.at[j], kept(i)),
            z=(level_in.at[j], raw_levels(raw, j)),
        )

    ends = (0, 1, R - 2, R - 1)
    keep(ends, merged)
    step_rows([first_part(i, j) for i, j in enumerate(ends)])

    def second(js):
        def job(k, j):
            def store(f, q, value):
                c2_out.at[f, j - 4][chunk(q)] = value

            return dict(
                store=store,
                load=lambda f, d, q: c1_out.at[f, j - 2 + d][moved_chunk(q)],
                x=(x_out.at[j], kept(k)),
                y=y_in.at[j - 2],
                z=(level_in.at[j], moved_levels(lambda f: c1_out.at[f, j - 2])),
            )

        step_rows([job(k, j) for k, j in enumerate(js)])

    by_fours_packed(4, R - 4, second, [merged1[f] for f in range(4)], turned, halos)

    def second_part(i, j):
        def store(f, q, value):
            part2_out.at[f, i][chunk(q)] = value

        return dict(
            store=store,
            load=lambda f, d, q: c1_out.at[f, j - 2][moved_chunk(q)],
            x=(x_out.at[j], kept(i)),
            z=(level_in.at[j], moved_levels(lambda f: c1_out.at[f, j - 2])),
        )

    ends = (2, 3, R - 4, R - 3)
    keep(ends, merged1)
    step_rows([second_part(i, j) for i, j in enumerate(ends)])


def boundary(*refs):
    rows, merged, y_in, level_in, x_in, c1_in, part1_in, c2_in, part2_in, edge_in = refs[:10]
    second, first, second_corners, first_corners = refs[10:14]
    outs = refs[14:18]
    sides, corners, x_new, y_new, level_new, c1_new, merged1, beyond, halos = refs[18:]
    lane = lanes()
    place = lax.axis_index("ns")
    last = lax.axis_size("ns") - 1
    odd = place % 2
    inside = {SOUTH: place > 0, NORTH: place < last}
    near = (-2, -1, 0, 1, R - 2, R - 1, R, R + 1)
    new_at = {j: i for i, j in enumerate(near)}
    def unpack(b, carry):
        for message, side in ((second, odd), (first, 1 - odd)):
            here = jnp.where(side == NORTH, place < last, place > 0)
            sides[side, b] = jnp.where(here, message[b], 0.0)
        return carry

    lax.fori_loop(0, SIDE_BLOCKS, unpack, 0, unroll=2)

    for message, side in ((second_corners, odd), (first_corners, 1 - odd)):
        here = jnp.where(side == NORTH, place < last, place > 0)
        corners[side] = jnp.where(here, message[...], 0.0)

    def row(f, j):
        if j < 0:
            return sides.at[SOUTH, ROWS_AT[f] + j + (2 if f == U else HALO)]
        if j >= R:
            return sides.at[NORTH, ROWS_AT[f] + j - R]
        return rows.at[f, j]

    for f in range(FIELDS):
        south = turn(corners[SOUTH], W - 2 * G - 2 * G * f)
        north = turn(corners[NORTH], -2 * G * f)
        beyond[f] = jnp.where(lane >= W // 2, south, north)
    for f in range(4):
        for i in range(2, 6):
            clear_ends(c1_new.at[f, i])

    for f, across in enumerate(edge_rows(merged, lambda f: beyond[f])):
        merged1[f] = edge_in[f] + across

    def halo_beyond(f, j):
        return halo_columns(beyond[f], j % R)

    for j in near:
        got = y_coefficients_at(row, j)
        for k in range(9):
            y_new[new_at[j], k] = got[k]
        if not 0 <= j < R:
            got = x_coefficients(
                row(U, j)[...], halo_beyond(U, j), row(M, j)[...], halo_beyond(M, j), lane
            )
            for k in range(9):
                x_new[new_at[j], k] = got[k]
            for k, value in enumerate(level_coefficients(row(M, j)[...])):
                level_new[new_at[j], k] = value

    out_rows = [j for j in near if not 0 <= j < R]
    for f in range(4):
        for i, j in enumerate(out_rows):
            halos[i, f] = halo_beyond(f, j)

    def kept(k):
        return lambda f, q: halos.at[k, f][chunk(q)]

    def first_job(j):
        side = SOUTH if j < R // 2 else NORTH

        def store(f, q, value):
            if f >= 2 and not 0 <= j < R:
                value = jnp.where(inside[side], value, 0.0)
            c1_new.at[f, new_at[j]][moved_chunk(q)] = value

        job = dict(
            store=store, load=lambda f, d, q: row(f, j + d)[chunk(q)], y=y_new.at[new_at[j]]
        )
        if 0 <= j < R:
            i = (0, 1, R - 2, R - 1).index(j)
            return job | dict(base=lambda f, q: part1_in.at[f, i][chunk(q)])
        return job | dict(
            x=(x_new.at[new_at[j]], kept(out_rows.index(j))),
            z=(level_new.at[new_at[j]], rolled_levels(lambda f: row(f, j)[...], range(4))),
        )

    step_rows([first_job(j) for j in (-2, 0, -1, 1, R, R - 2, R + 1, R - 1)])

    def load1(f, j, q):
        if j in new_at:
            return c1_new.at[f, new_at[j]][moved_chunk(q)]
        return c1_in.at[f, j - 2][moved_chunk(q)]

    ends = (0, 1, R - 2, R - 1)
    for f in range(4):
        for i, j in enumerate(ends):
            halos[i, f] = halo_columns(merged1[f], j)

    def second_job(j):
        def store(f, q, value):
            outs[f][pl.ds(8 * q * R + j, 8, stride=R), :] = value

        job = dict(store=store, load=lambda f, d, q: load1(f, j + d, q))
        if j in ends:
            return job | dict(
                x=(x_in.at[j], kept(ends.index(j))),
                y=y_new.at[new_at[j]],
                z=(level_in.at[j], moved_levels(lambda f: c1_new.at[f, new_at[j]])),
            )
        i = (2, 3, R - 4, R - 3).index(j)
        return job | dict(y=y_in.at[j - 2], base=lambda f, q: part2_in.at[f, i][chunk(q)])

    step_rows([second_job(j) for j in (0, 2, 1, 3, R - 2, R - 4, R - 1, R - 3)])

    def copy(j, carry):
        for f in range(4):
            outs[f][pl.ds(j, K, stride=R), :] = c2_in[f, j - 4]
        return carry

    lax.fori_loop(4, R - 4, copy, 0, unroll=2)


def vmem():
    return pl.BlockSpec(memory_space=pltpu.VMEM)


def call(kernel, in_specs, out_shapes, scratch=(), limit=16 * MIB, cost=0.1):
    return pl.pallas_call(
        kernel,
        out_shape=[jax.ShapeDtypeStruct(shape, F32) for shape in out_shapes],
        in_specs=in_specs,
        out_specs=[vmem()] * len(out_shapes),
        scratch_shapes=list(scratch),
        compiler_params=pltpu.CompilerParams(vmem_limit_bytes=limit),
        cost_estimate=pl.CostEstimate(flops=int(cost * FLOPS_PER_US), bytes_accessed=MIB, transcendentals=0),
    )


def partners(odd, n_ew, n_ns):
    pairs = []
    for e in range(n_ew):
        for s in range(n_ns):
            step = 1 if (s - odd) % 2 == 0 else -1
            if 0 <= s + step < n_ns:
                to = (e, s + step)
            else:
                to = (e ^ 1 if e ^ 1 < n_ew else e, s)
            pairs.append((e * n_ns + s, to[0] * n_ns + to[1]))
    return pairs


def local(temp, salt, u_east, v_north, wet, cot_temp, cot_salt):
    flat = [a.reshape(K * R, W) for a in (temp, salt, cot_temp, cot_salt, u_east, v_north, wet)]

    row = (K, W)
    padded = ((K + 2) * R, W)
    rows, raw, own, to_east, to_west = call(
        pack_edges,
        [pl.BlockSpec(memory_space=pltpu.HBM)] * FIELDS,
        [(FIELDS, R) + row, (4,) + padded, (FIELDS,) + row, (EDGE_ROWS, W), (EDGE_ROWS, W)],
        [
            pltpu.VMEM((2, K * R, W), F32),
            pltpu.VMEM((K * R, W), jnp.int32),
            pltpu.SemaphoreType.DMA((FIELDS,)),
        ],
        cost=2.2,
    )(*[pltpu.with_memory_space_constraint(a, pltpu.HBM) for a in flat])

    n_ew, n_ns = lax.axis_size("ew"), lax.axis_size("ns")
    from_west = lax.ppermute(to_east, "ew", [(i, (i + 1) % n_ew) for i in range(n_ew)])
    from_east = lax.ppermute(to_west, "ew", [((i + 1) % n_ew, i) for i in range(n_ew)])

    def swap(odd, message):
        return lax.ppermute(message, ("ew", "ns"), partners(odd, n_ew, n_ns))

    second, first = call(pack_sides, [vmem()], [(SIDE_BLOCKS,) + row] * 2, cost=0.1)(rows)
    second = swap(1, second)
    first = swap(0, first)

    y_in, level, base = call(
        prepare,
        [vmem()] * 2,
        [(R - 4, 9) + row, (R, 3) + row, (4, R - 4) + row],
        cost=1.7,
    )(rows, raw)

    left, right, merged, second_corners, first_corners = call(
        pack_corners,
        [vmem()] * 3 + [pl.BlockSpec(memory_space=pl.ANY)],
        [(FIELDS,) + row] * 3 + [row] * 2,
        cost=0.2,
    )(own, from_west, from_east, level)
    second_corners = swap(1, second_corners)
    first_corners = swap(0, first_corners)

    x_in, c1, part1, c2, part2, edge = call(
        interior,
        [vmem()] * 8,
        [(R, 9) + row, (4, R - 4, TALL, W), (4, 4) + row, (4, R - 8) + row, (4, 4) + row, (4,) + row],
        [
            pltpu.VMEM((4,) + row, F32),
            pltpu.VMEM((4,) + row, F32),
            pltpu.VMEM((4, 4) + row, F32),
            pltpu.VMEM((4, 2) + row, F32),
        ],
        cost=4.7,
    )(rows, raw, left, right, merged, y_in, level, base)

    outs = call(
        boundary,
        [vmem()] * 14,
        [(K * R, W)] * 4,
        [
            pltpu.VMEM((2, SIDE_BLOCKS) + row, F32),
            pltpu.VMEM((2,) + row, F32),
            pltpu.VMEM((8, 9) + row, F32),
            pltpu.VMEM((8, 9) + row, F32),
            pltpu.VMEM((8, 3) + row, F32),
            pltpu.VMEM((4, 8, TALL, W), F32),
            pltpu.VMEM((4,) + row, F32),
            pltpu.VMEM((FIELDS,) + row, F32),
            pltpu.VMEM((4, 4) + row, F32),
        ],
        cost=2.9,
    )(
        *(rows, merged, y_in, level, x_in, c1, part1, c2, part2, edge),
        *(second, first, second_corners, first_corners),
    )
    return tuple(a.reshape(K, R, W) for a in outs)


def solution(mesh):
    spec = P(None, "ns", "ew")
    return jax.shard_map(
        local, mesh=mesh, in_specs=(spec,) * 7, out_specs=(spec,) * 4, check_vma=False
    )
```

```python
import jax
import jax.numpy as jnp
from jax import lax
from jax.experimental import pallas as pl
from jax.experimental.pallas import tpu as pltpu
from jax.sharding import PartitionSpec as P

horizontal_mix = 0.05
vertical_mix = 0.2

F32 = jnp.float32
K = 32
R = 16
W = 128
G = W // R
HALO = 4
FIELDS = 7
U, V, M = 4, 5, 6
PAIRS = ((0, 1), (2, 3), (U, M))
EDGE_ROWS = len(PAIRS) * K + 8
SIDE_BLOCKS = 26
ROWS_AT = (0, 4, 8, 12, 24, 16, 20)
SOUTH, NORTH = 0, 1
MIB = 1 << 20
FLOPS_PER_US = 1.15e9


def lanes():
    return lax.broadcasted_iota(jnp.int32, (K, W), 1)


def turn(x, amount):
    return pltpu.roll(x, amount % W, 1)


def pack_edges(*refs):
    sources = refs[:FIELDS]
    rows, raw, own, to_east, to_west, raw_flow, raw_wet, arrived = refs[FIELDS:]
    copies = []
    for f in range(FIELDS):
        target = raw.at[f, pl.ds(R, K * R)] if f < 4 else raw_wet if f == M else raw_flow.at[f - U]
        copies.append(pltpu.make_async_copy(sources[f], target, arrived.at[f]))
        copies[-1].start()
    for f in range(4):
        raw[f, pl.ds(0, R)] = jnp.zeros((R, W), F32)
        raw[f, pl.ds((K + 1) * R, R)] = jnp.zeros((R, W), F32)
    lane = lanes()
    group = lane // G
    packed = []
    for f in range(FIELDS):
        copies[f].wait()
        source = raw.at[f] if f < 4 else raw_wet if f == M else raw_flow.at[f - U]
        edges = jnp.zeros((K, W), F32)
        for r in range(R):
            x = source[pl.ds(R + r if f < 4 else r, K, stride=R), :].astype(F32)
            rows[f, r] = x
            edges = jnp.where(group == r, turn(x, G * r + HALO), edges)
        own[f] = edges
        packed.append(edges)
    west_half = lane % G < HALO
    for p, (f, g) in enumerate(PAIRS):
        a, b = packed[f], packed[g]
        to_east[pl.ds(p * K, K)] = jnp.where(west_half, a, turn(b, HALO))
        to_west[pl.ds(p * K, K)] = jnp.where(west_half, turn(b, -HALO), a)
    part = lane[:8] % G // 2
    for target, column in ((to_east, HALO - 2), (to_west, HALO)):
        block = jnp.zeros((8, W), F32)
        for q in range(K // 8):
            moved = turn(packed[V][8 * q : 8 * q + 8], 2 * q - column)
            block = jnp.where(part == q, moved, block)
        target[pl.ds(len(PAIRS) * K, 8)] = block


def pack_sides(rows, second, first):
    odd = lax.axis_index("ns") % 2
    for out, north in ((second, odd), (first, 1 - odd)):
        for f in range(FIELDS):
            count = 2 if f == U else HALO
            start = (R - count) * north
            for r in range(count):
                out[ROWS_AT[f] + r] = rows[f, start + r]


def pack_corners(own, from_west, from_east, _, left, right, merged, second, first):
    odd = lax.axis_index("ns") % 2
    lane = lanes()
    west_half = lane % G < HALO
    halos = {}
    for p, (f, g) in enumerate(PAIRS):
        a, b = from_west[pl.ds(p * K, K)], from_east[pl.ds(p * K, K)]
        halos[f], halos[g] = (a, b), (turn(a, -HALO), turn(b, HALO))
    a, b = from_west[pl.ds(len(PAIRS) * K, 8)], from_east[pl.ds(len(PAIRS) * K, 8)]
    halos[V] = [
        jnp.concatenate([turn(x, column - 2 * q) for q in range(K // 8)], axis=0)
        for x, column in ((a, HALO - 2), (b, HALO))
    ]
    for f in range(FIELDS):
        a, b = halos[f]
        left[f] = jnp.where(west_half, a, own[f])
        right[f] = jnp.where(west_half, own[f], b)
        merged[f] = jnp.where(west_half, a, b)
    for out, north in ((second, odd), (first, 1 - odd)):
        block = jnp.zeros((K, W), F32)
        for f in range(FIELDS):
            amount = lax.rem(2 * G * f + W - (W - 2 * G) * north, W)
            moved = pltpu.roll(merged[f], amount, 1)
            block = jnp.where(lane // (2 * G) == f, moved, block)
        out[...] = block


def coefficients(speed, mask):
    opened = {d: mask[d] * mask[d + 1] for d in (-2, -1, 0, 1)}
    return face_coefficients({d: scaled(speed[d], opened[d]) for d in opened}, opened)


def scaled(speed, opened):
    return speed * opened * (1.0 / 12.0)


def face_coefficients(s, opened):
    a = {d: jnp.abs(s[d]) for d in s}
    w0 = {d: -(s[d] + a[d]) for d in (-1, 0, 1)}
    w3 = {d: a[d] - s[d] for d in (-2, -1, 0)}
    w1, w2 = {}, {}
    for d in (-1, 0):
        even, odd = 7.0 * s[d], 3.0 * a[d] + horizontal_mix * opened[d]
        w1[d], w2[d] = even + odd, even - odd
    forward = [w0[-1], w1[-1] - w0[0], w3[-1] - w2[0], -w3[0]]
    transposed = [-w3[-2], w3[-2] - w2[-1], w1[0] - w0[1], w0[1]]
    return forward + transposed + [w2[-1] - w1[0]]


def shifted(c, h, d, lane, step=1):
    if d == 0:
        return c
    if d > 0:
        return turn(jnp.where(lane < step * d, h, c), -step * d)
    return turn(jnp.where(lane >= W + step * d, h, c), -step * d)


def x_coefficients(u, uh, m, mh, lane):
    return coefficients(
        {d: shifted(u, uh, d, lane) for d in (-2, -1, 0, 1)},
        {d: shifted(m, mh, d, lane) for d in (-2, -1, 0, 1, 2)},
    )


def level_coefficients(m):
    inner = lax.broadcasted_iota(jnp.int32, (K, W), 0) < K - 1
    after = jnp.where(inner, vertical_mix * m * pltpu.roll(m, K - 1, 0), 0.0)
    before = pltpu.roll(after, 1, 0)
    return after, before, 1.0 - after - before


def chunk(q):
    return pl.ds(8 * q, 8)


def strided(q, j, stride, shift=0):
    return pl.ds((8 * q + 1 + shift) * stride + j, 8, stride=stride)


def pipeline(items, issue, finish, depth=1):
    pending = []
    for item in items:
        pending.append((item, issue(item)))
        if len(pending) > depth:
            finish(*pending.pop(0))
    for late in pending:
        finish(*late)


def step_rows(jobs):
    lane = lanes()[:8]

    def issue(item):
        job, q = item
        if q == 0 and "ahead" in job:
            job["ahead"]()
        if "x" not in job:
            return None
        halo = job["x"][1]
        rolled = []
        for f in range(4):
            c, h = job["load"](f, 0, q), halo(f, q)
            rolled.append([shifted(c, h, d, lane) for d in (-2, -1, 1, 2)])
        return rolled

    def finish(item, rolled):
        job, q = item
        x, y, z = job.get("x"), job.get("y"), job.get("z")
        load, part = job["load"], chunk(q)
        centre = None
        for term in (x and x[0].at[8], y and y.at[8], z and z[0].at[2]):
            if term is not None:
                centre = term[part] if centre is None else centre + term[part]
        if z:
            after, before = z[0].at[0][part], z[0].at[1][part]
        totals = []
        for f in range(4):
            total = centre * load(f, 0, q)
            if "base" in job:
                total += job["base"](f, q)
            if z:
                c_after, c_before = z[1](f, q)
                total += after * c_after + before * c_before
            totals.append(total)
        for coefficients_at, values in (
            (y, lambda f, i: load(f, (-2, -1, 1, 2)[i], q)),
            (x and x[0], lambda f, i: rolled[f][i]),
        ):
            if coefficients_at is None:
                continue
            for i in range(4):
                for direction in (0, 1):
                    coefficient = coefficients_at.at[4 * direction + i][part]
                    for f in (2 * direction, 2 * direction + 1):
                        totals[f] += coefficient * values(f, i)
        for f in range(4):
            job["store"](f, q, totals[f])

    pipeline([(job, q) for job in jobs for q in range(K // 8)], issue, finish)


def halo_columns(merged, j):
    return turn(merged, -HALO - G * j)


def edge_faces(edges):
    opened = edges[M] * turn(edges[M], -1)
    return scaled(edges[U], opened), opened


def edge_columns_and_levels(edges, s, opened):
    m = edges[M]
    xs = face_coefficients(
        {d: turn(s, -d) if d else s for d in (-2, -1, 0, 1)}, {-1: turn(opened, 1), 0: opened}
    )
    after, before, centre = level_coefficients(m)
    results = []
    for f in range(4):
        c = edges[f]
        total = (centre + xs[8]) * c
        total += after * pltpu.roll(c, K - 1, 0) + before * pltpu.roll(c, 1, 0)
        for coefficient, d in zip(xs[4 * (f // 2) :], (-2, -1, 1, 2)):
            total += coefficient * turn(c, -d)
        results.append(total)
    return results


def edge_rows(merged, beyond):
    lane = lanes()
    v, m = merged[V], merged[M]
    vh, mh = beyond(V), beyond(M)
    ys = coefficients(
        {d: shifted(v, vh, d, lane, G) for d in (-2, -1, 0, 1)},
        {d: shifted(m, mh, d, lane, G) for d in (-2, -1, 0, 1, 2)},
    )
    results = []
    for f in range(4):
        c, ch = merged[f], beyond(f)
        total = ys[8] * c
        for coefficient, d in zip(ys[4 * (f // 2) :], (-2, -1, 1, 2)):
            total += coefficient * shifted(c, ch, d, lane, G)
        results.append(total)
    return results


def y_coefficients(low, high, load, emit):
    for q in range(K // 8):
        w = {}
        for j in range(low - 2, high + 2):
            opened = load(M, j, q) * load(M, j + 1, q)
            s = scaled(load(V, j, q), opened)
            a = jnp.abs(s)
            even, odd = 7.0 * s, 3.0 * a + horizontal_mix * opened
            w[j] = (-(s + a), even + odd, even - odd, a - s)
            if j > low:
                at = [w[j - 3], w[j - 2], w[j - 1], w[j]]
                forward = [at[1][0], at[1][1] - at[2][0], at[1][3] - at[2][2], -at[2][3]]
                transposed = [-at[0][3], at[0][3] - at[1][2], at[2][1] - at[3][0], at[3][0]]
                emit(j - 1, q, forward + transposed + [at[1][2] - at[2][1]])


def by_fours(start, stop, body):
    def four(i, carry):
        body([start + 4 * i + k for k in range(4)])
        return carry

    lax.fori_loop(0, (stop - start) // 4, four, 0)


def raw_levels(raw, j):
    return lambda f, q: (raw.at[f][strided(q, j, R, 1), :], raw.at[f][strided(q, j, R, -1), :])


TALL = K + 16


def moved_chunk(q, shift=0):
    return pl.ds(8 + 8 * q + shift, 8)


def clear_ends(ref):
    ref[pl.ds(0, 8)] = jnp.zeros((8, W), F32)
    ref[pl.ds(8 + K, 8)] = jnp.zeros((8, W), F32)


def moved_levels(row):
    return lambda f, q: (row(f)[moved_chunk(q, 1)], row(f)[moved_chunk(q, -1)])


def rolled_levels(load, fields):
    after = {f: pltpu.roll(load(f), K - 1, 0) for f in fields}
    before = {f: pltpu.roll(load(f), 1, 0) for f in fields}
    return lambda f, q: (after[f][8 * q : 8 * q + 8], before[f][8 * q : 8 * q + 8])


def prepare(rows, raw, y_out, level_out, base_out):
    def levels(js):
        for j in js:
            for k, value in enumerate(level_coefficients(rows[M, j])):
                level_out[j, k] = value

    by_fours(0, R, levels)

    def emit(j, q, values):
        for k in range(9):
            y_out.at[j - 2, k][chunk(q)] = values[k]

    y_coefficients(2, R - 3, lambda f, j, q: rows.at[f, j][chunk(q)], emit)

    def first(js):
        def job(j):
            def store(f, q, value):
                base_out.at[f, j - 2][chunk(q)] = value

            return dict(
                store=store,
                load=lambda f, d, q: rows.at[f, j + d][chunk(q)],
                y=y_out.at[j - 2],
                z=(level_out.at[j], raw_levels(raw, j)),
            )

        step_rows([job(j) for j in js])

    by_fours(2, R - 2, first)


def interior(*refs):
    rows, raw, left, right, merged, y_in, level_in, base_in = refs[:8]
    x_out, c1_out, part1_out, c2_out, part2_out, edge_out, merged1, halos, faces_now = refs[8:]
    lane = lanes()
    west_half = lane % G < HALO
    for f in range(4):
        for r in range(R - 4):
            clear_ends(c1_out.at[f, r])
    faces = [edge_faces(edges) for edges in (left, right)]
    halo_s = jnp.where(west_half, faces[0][0], faces[1][0])
    halo_mixed = jnp.where(west_half, faces[0][1], right[M])

    def x_halos(j):
        if j < R:
            halos[j, 0] = halo_columns(halo_s, j)
            halos[j, 1] = halo_columns(halo_mixed, j)

    def x_faces(j):
        if j < R:
            m = rows[M, j]
            opened = m * shifted(m, halos[j, 1], 1, lane)
            faces_now[j, 0] = scaled(rows[U, j], opened)
            faces_now[j, 1] = opened

    for j in range(4):
        x_halos(j)
    for j in range(2):
        x_faces(j)

    def issue(item):
        j, q = item
        if q == 0:
            x_halos(j + 4)
            x_faces(j + 2)
        s, opened = faces_now.at[j, 0][chunk(q)], faces_now.at[j, 1][chunk(q)]
        hs, hm = halos.at[j, 0][chunk(q)], halos.at[j, 1][chunk(q)]
        return (
            {d: shifted(s, hs, d, lane[:8]) for d in (-2, -1, 0, 1)},
            {-1: shifted(opened, hm, -1, lane[:8]), 0: opened},
        )

    def finish(item, faces_here):
        j, q = item
        for i, value in enumerate(face_coefficients(*faces_here)):
            x_out.at[j, i][chunk(q)] = value

    pipeline([(j, q) for j in range(R) for q in range(K // 8)], issue, finish, 2)

    partial = [edge_columns_and_levels(e, *f) for e, f in zip((left, right), faces)]
    across = edge_rows(merged, lambda f: merged[f])
    for f in range(4):
        edge = jnp.where(west_half, partial[0][f], partial[1][f])
        edge_out[f] = edge
        merged1[f] = edge + across[f]

    def kept(j):
        return lambda f, q: halos.at[j, f][chunk(q)]

    def run(jobs, source):
        js = list(jobs)

        def keep(k):
            if k < len(js):
                for f in range(4):
                    halos[js[k], f] = halo_columns(source[f], js[k])

        keep(0)
        keep(1)
        step_rows([job | dict(ahead=lambda k=k: keep(k + 2)) for k, job in enumerate(jobs.values())])

    def first(j):
        def store(f, q, value):
            if j in ends1:
                part1_out.at[f, ends1.index(j)][chunk(q)] = value
            else:
                c1_out.at[f, j - 2][moved_chunk(q)] = value

        job = dict(
            store=store,
            load=lambda f, d, q: rows.at[f, j][chunk(q)],
            x=(x_out.at[j], kept(j)),
        )
        if j in ends1:
            return job | dict(z=(level_in.at[j], raw_levels(raw, j)))
        return job | dict(base=lambda f, q: base_in.at[f, j - 2][chunk(q)])

    ends1 = (0, 1, R - 2, R - 1)
    run({j: first(j) for j in range(R)}, merged)

    def second(j):
        def store(f, q, value):
            if j in ends2:
                part2_out.at[f, ends2.index(j)][chunk(q)] = value
            else:
                c2_out.at[f, j - 4][chunk(q)] = value

        job = dict(
            store=store,
            load=lambda f, d, q: c1_out.at[f, j - 2 + d][moved_chunk(q)],
            x=(x_out.at[j], kept(j)),
            z=(level_in.at[j], moved_levels(lambda f: c1_out.at[f, j - 2])),
        )
        return job if j in ends2 else job | dict(y=y_in.at[j - 2])

    ends2 = (2, 3, R - 4, R - 3)
    run({j: second(j) for j in range(2, R - 2)}, merged1)


def boundary(*refs):
    rows, merged, y_in, level_in, x_in, c1_in, part1_in, c2_in, part2_in, edge_in = refs[:10]
    second, first, second_corners, first_corners = refs[10:14]
    outs = refs[14:18]
    sides, corners, x_new, y_new, level_new, c1_new, merged1, beyond, halos = refs[18:]
    lane = lanes()
    place = lax.axis_index("ns")
    last = lax.axis_size("ns") - 1
    odd = place % 2
    inside = {SOUTH: place > 0, NORTH: place < last}
    near = (-2, -1, 0, 1, R - 2, R - 1, R, R + 1)
    new_at = {j: i for i, j in enumerate(near)}
    def unpack(b, carry):
        for message, side in ((second, odd), (first, 1 - odd)):
            here = jnp.where(side == NORTH, place < last, place > 0)
            sides[side, b] = jnp.where(here, message[b], 0.0)
        return carry

    lax.fori_loop(0, SIDE_BLOCKS, unpack, 0, unroll=2)

    for message, side in ((second_corners, odd), (first_corners, 1 - odd)):
        here = jnp.where(side == NORTH, place < last, place > 0)
        corners[side] = jnp.where(here, message[...], 0.0)

    def row(f, j):
        if j < 0:
            return sides.at[SOUTH, ROWS_AT[f] + j + (2 if f == U else HALO)]
        if j >= R:
            return sides.at[NORTH, ROWS_AT[f] + j - R]
        return rows.at[f, j]

    for f in range(FIELDS):
        south = turn(corners[SOUTH], W - 2 * G - 2 * G * f)
        north = turn(corners[NORTH], -2 * G * f)
        beyond[f] = jnp.where(lane >= W // 2, south, north)
    for f in range(4):
        for i in range(2, 6):
            clear_ends(c1_new.at[f, i])

    for f, across in enumerate(edge_rows(merged, lambda f: beyond[f])):
        merged1[f] = edge_in[f] + across

    def halo_beyond(f, j):
        return halo_columns(beyond[f], j % R)

    def emit(j, q, values):
        for k in range(9):
            y_new.at[new_at[j], k][chunk(q)] = values[k]

    for low in (-2, R - 2):
        y_coefficients(low, low + 3, lambda f, j, q: row(f, j)[chunk(q)], emit)

    for j in near:
        if not 0 <= j < R:
            got = x_coefficients(
                row(U, j)[...], halo_beyond(U, j), row(M, j)[...], halo_beyond(M, j), lane
            )
            for k in range(9):
                x_new[new_at[j], k] = got[k]
            for k, value in enumerate(level_coefficients(row(M, j)[...])):
                level_new[new_at[j], k] = value

    out_rows = [j for j in near if not 0 <= j < R]
    for f in range(4):
        for i, j in enumerate(out_rows):
            halos[i, f] = halo_beyond(f, j)

    def kept(k):
        return lambda f, q: halos.at[k, f][chunk(q)]

    def first_job(j):
        side = SOUTH if j < R // 2 else NORTH

        def store(f, q, value):
            if f >= 2 and not 0 <= j < R:
                value = jnp.where(inside[side], value, 0.0)
            c1_new.at[f, new_at[j]][moved_chunk(q)] = value

        job = dict(
            store=store, load=lambda f, d, q: row(f, j + d)[chunk(q)], y=y_new.at[new_at[j]]
        )
        if 0 <= j < R:
            i = (0, 1, R - 2, R - 1).index(j)
            return job | dict(base=lambda f, q: part1_in.at[f, i][chunk(q)])
        return job | dict(
            x=(x_new.at[new_at[j]], kept(out_rows.index(j))),
            z=(level_new.at[new_at[j]], rolled_levels(lambda f: row(f, j)[...], range(4))),
        )

    step_rows([first_job(j) for j in (-2, 0, -1, 1, R, R - 2, R + 1, R - 1)])

    def load1(f, j, q):
        if j in new_at:
            return c1_new.at[f, new_at[j]][moved_chunk(q)]
        return c1_in.at[f, j - 2][moved_chunk(q)]

    ends = (0, 1, R - 2, R - 1)
    for f in range(4):
        for i, j in enumerate(ends):
            halos[i, f] = halo_columns(merged1[f], j)

    def second_job(j):
        def store(f, q, value):
            outs[f][pl.ds(8 * q * R + j, 8, stride=R), :] = value

        job = dict(store=store, load=lambda f, d, q: load1(f, j + d, q))
        if j in ends:
            return job | dict(
                x=(x_in.at[j], kept(ends.index(j))),
                y=y_new.at[new_at[j]],
                z=(level_in.at[j], moved_levels(lambda f: c1_new.at[f, new_at[j]])),
            )
        i = (2, 3, R - 4, R - 3).index(j)
        return job | dict(y=y_in.at[j - 2], base=lambda f, q: part2_in.at[f, i][chunk(q)])

    step_rows([second_job(j) for j in (0, 2, 1, 3, R - 2, R - 4, R - 1, R - 3)])

    def copy(j, carry):
        for f in range(4):
            outs[f][pl.ds(j, K, stride=R), :] = c2_in[f, j - 4]
        return carry

    lax.fori_loop(4, R - 4, copy, 0, unroll=2)


def vmem():
    return pl.BlockSpec(memory_space=pltpu.VMEM)


def call(kernel, in_specs, out_shapes, scratch=(), limit=16 * MIB, cost=0.1):
    return pl.pallas_call(
        kernel,
        out_shape=[jax.ShapeDtypeStruct(shape, F32) for shape in out_shapes],
        in_specs=in_specs,
        out_specs=[vmem()] * len(out_shapes),
        scratch_shapes=list(scratch),
        compiler_params=pltpu.CompilerParams(vmem_limit_bytes=limit),
        cost_estimate=pl.CostEstimate(flops=int(cost * FLOPS_PER_US), bytes_accessed=MIB, transcendentals=0),
    )


def partners(odd, n_ew, n_ns):
    pairs = []
    for e in range(n_ew):
        for s in range(n_ns):
            step = 1 if (s - odd) % 2 == 0 else -1
            if 0 <= s + step < n_ns:
                to = (e, s + step)
            else:
                to = (e ^ 1 if e ^ 1 < n_ew else e, s)
            pairs.append((e * n_ns + s, to[0] * n_ns + to[1]))
    return pairs


def local(temp, salt, u_east, v_north, wet, cot_temp, cot_salt):
    flat = [a.reshape(K * R, W) for a in (temp, salt, cot_temp, cot_salt, u_east, v_north, wet)]

    row = (K, W)
    padded = ((K + 2) * R, W)
    rows, raw, own, to_east, to_west = call(
        pack_edges,
        [pl.BlockSpec(memory_space=pltpu.HBM)] * FIELDS,
        [(FIELDS, R) + row, (4,) + padded, (FIELDS,) + row, (EDGE_ROWS, W), (EDGE_ROWS, W)],
        [
            pltpu.VMEM((2, K * R, W), F32),
            pltpu.VMEM((K * R, W), jnp.int32),
            pltpu.SemaphoreType.DMA((FIELDS,)),
        ],
        cost=2.2,
    )(*[pltpu.with_memory_space_constraint(a, pltpu.HBM) for a in flat])

    n_ew, n_ns = lax.axis_size("ew"), lax.axis_size("ns")
    from_west = lax.ppermute(to_east, "ew", [(i, (i + 1) % n_ew) for i in range(n_ew)])
    from_east = lax.ppermute(to_west, "ew", [((i + 1) % n_ew, i) for i in range(n_ew)])

    def swap(odd, message):
        return lax.ppermute(message, ("ew", "ns"), partners(odd, n_ew, n_ns))

    second, first = call(pack_sides, [vmem()], [(SIDE_BLOCKS,) + row] * 2, cost=0.1)(rows)
    second = swap(1, second)
    first = swap(0, first)

    y_in, level, base = call(
        prepare,
        [vmem()] * 2,
        [(R - 4, 9) + row, (R, 3) + row, (4, R - 4) + row],
        cost=1.7,
    )(rows, raw)

    left, right, merged, second_corners, first_corners = call(
        pack_corners,
        [vmem()] * 3 + [pl.BlockSpec(memory_space=pl.ANY)],
        [(FIELDS,) + row] * 3 + [row] * 2,
        cost=0.2,
    )(own, from_west, from_east, level)
    second_corners = swap(1, second_corners)
    first_corners = swap(0, first_corners)

    x_in, c1, part1, c2, part2, edge = call(
        interior,
        [vmem()] * 8,
        [(R, 9) + row, (4, R - 4, TALL, W), (4, 4) + row, (4, R - 8) + row, (4, 4) + row, (4,) + row],
        [
            pltpu.VMEM((4,) + row, F32),
            pltpu.VMEM((R, 4) + row, F32),
            pltpu.VMEM((R, 2) + row, F32),
        ],
        cost=4.7,
    )(rows, raw, left, right, merged, y_in, level, base)

    outs = call(
        boundary,
        [vmem()] * 14,
        [(K * R, W)] * 4,
        [
            pltpu.VMEM((2, SIDE_BLOCKS) + row, F32),
            pltpu.VMEM((2,) + row, F32),
            pltpu.VMEM((8, 9) + row, F32),
            pltpu.VMEM((8, 9) + row, F32),
            pltpu.VMEM((8, 3) + row, F32),
            pltpu.VMEM((4, 8, TALL, W), F32),
            pltpu.VMEM((4,) + row, F32),
            pltpu.VMEM((FIELDS,) + row, F32),
            pltpu.VMEM((4, 4) + row, F32),
        ],
        cost=2.9,
    )(
        *(rows, merged, y_in, level, x_in, c1, part1, c2, part2, edge),
        *(second, first, second_corners, first_corners),
    )
    return tuple(a.reshape(K, R, W) for a in outs)


def solution(mesh):
    spec = P(None, "ns", "ew")
    return jax.shard_map(
        local, mesh=mesh, in_specs=(spec,) * 7, out_specs=(spec,) * 4, check_vma=False
    )
```

```python
import jax
import jax.numpy as jnp
from jax import lax
from jax.experimental import pallas as pl
from jax.experimental.pallas import tpu as pltpu
from jax.sharding import PartitionSpec as P

horizontal_mix = 0.05
vertical_mix = 0.2

F32 = jnp.float32
K = 32
R = 16
W = 128
G = W // R
HALO = 4
FIELDS = 7
U, V, M = 4, 5, 6
PAIRS = ((0, 1), (2, 3), (U, M))
EDGE_ROWS = len(PAIRS) * K + 8
SIDE_BLOCKS = 26
ROWS_AT = (0, 4, 8, 12, 24, 16, 20)
SOUTH, NORTH = 0, 1
MIB = 1 << 20
FLOPS_PER_US = 1.15e9


def lanes():
    return lax.broadcasted_iota(jnp.int32, (K, W), 1)


def turn(x, amount):
    return pltpu.roll(x, amount % W, 1)


def pack_edges(*refs):
    sources = refs[:FIELDS]
    rows, raw, own, to_east, to_west, raw_flow, raw_wet, arrived = refs[FIELDS:]
    copies = []
    for f in range(FIELDS):
        target = raw.at[f, pl.ds(R, K * R)] if f < 4 else raw_wet if f == M else raw_flow.at[f - U]
        copies.append(pltpu.make_async_copy(sources[f], target, arrived.at[f]))
        copies[-1].start()
    for f in range(4):
        raw[f, pl.ds(0, R)] = jnp.zeros((R, W), F32)
        raw[f, pl.ds((K + 1) * R, R)] = jnp.zeros((R, W), F32)
    lane = lanes()
    group = lane // G
    packed = []
    for f in range(FIELDS):
        copies[f].wait()
        source = raw.at[f] if f < 4 else raw_wet if f == M else raw_flow.at[f - U]
        edges = jnp.zeros((K, W), F32)
        for r in range(R):
            x = source[pl.ds(R + r if f < 4 else r, K, stride=R), :].astype(F32)
            rows[f, r] = x
            edges = jnp.where(group == r, turn(x, G * r + HALO), edges)
        own[f] = edges
        packed.append(edges)
    west_half = lane % G < HALO
    for p, (f, g) in enumerate(PAIRS):
        a, b = packed[f], packed[g]
        to_east[pl.ds(p * K, K)] = jnp.where(west_half, a, turn(b, HALO))
        to_west[pl.ds(p * K, K)] = jnp.where(west_half, turn(b, -HALO), a)
    part = lane[:8] % G // 2
    for target, column in ((to_east, HALO - 2), (to_west, HALO)):
        block = jnp.zeros((8, W), F32)
        for q in range(K // 8):
            moved = turn(packed[V][8 * q : 8 * q + 8], 2 * q - column)
            block = jnp.where(part == q, moved, block)
        target[pl.ds(len(PAIRS) * K, 8)] = block


def pack_sides(rows, second, first):
    odd = lax.axis_index("ns") % 2
    for out, north in ((second, odd), (first, 1 - odd)):
        for f in range(FIELDS):
            count = 2 if f == U else HALO
            start = (R - count) * north
            for r in range(count):
                out[ROWS_AT[f] + r] = rows[f, start + r]


def pack_corners(own, from_west, from_east, _, left, right, merged, second, first):
    odd = lax.axis_index("ns") % 2
    lane = lanes()
    west_half = lane % G < HALO
    halos = {}
    for p, (f, g) in enumerate(PAIRS):
        a, b = from_west[pl.ds(p * K, K)], from_east[pl.ds(p * K, K)]
        halos[f], halos[g] = (a, b), (turn(a, -HALO), turn(b, HALO))
    a, b = from_west[pl.ds(len(PAIRS) * K, 8)], from_east[pl.ds(len(PAIRS) * K, 8)]
    halos[V] = [
        jnp.concatenate([turn(x, column - 2 * q) for q in range(K // 8)], axis=0)
        for x, column in ((a, HALO - 2), (b, HALO))
    ]
    for f in range(FIELDS):
        a, b = halos[f]
        left[f] = jnp.where(west_half, a, own[f])
        right[f] = jnp.where(west_half, own[f], b)
        merged[f] = jnp.where(west_half, a, b)
    for out, north in ((second, odd), (first, 1 - odd)):
        block = jnp.zeros((K, W), F32)
        for f in range(FIELDS):
            amount = lax.rem(2 * G * f + W - (W - 2 * G) * north, W)
            moved = pltpu.roll(merged[f], amount, 1)
            block = jnp.where(lane // (2 * G) == f, moved, block)
        out[...] = block


def coefficients(speed, mask):
    opened = {d: mask[d] * mask[d + 1] for d in (-2, -1, 0, 1)}
    return face_coefficients({d: scaled(speed[d], opened[d]) for d in opened}, opened)


def scaled(speed, opened):
    return speed * opened * (1.0 / 12.0)


def face_coefficients(s, opened):
    a = {d: jnp.abs(s[d]) for d in s}
    w0 = {d: -(s[d] + a[d]) for d in (-1, 0, 1)}
    w3 = {d: a[d] - s[d] for d in (-2, -1, 0)}
    w1, w2 = {}, {}
    for d in (-1, 0):
        even, odd = 7.0 * s[d], 3.0 * a[d] + horizontal_mix * opened[d]
        w1[d], w2[d] = even + odd, even - odd
    forward = [w0[-1], w1[-1] - w0[0], w3[-1] - w2[0], -w3[0]]
    transposed = [-w3[-2], w3[-2] - w2[-1], w1[0] - w0[1], w0[1]]
    return forward + transposed + [w2[-1] - w1[0]]


def shifted(c, h, d, lane, step=1):
    if d == 0:
        return c
    if d > 0:
        return turn(jnp.where(lane < step * d, h, c), -step * d)
    return turn(jnp.where(lane >= W + step * d, h, c), -step * d)


def x_coefficients(u, uh, m, mh, lane):
    return coefficients(
        {d: shifted(u, uh, d, lane) for d in (-2, -1, 0, 1)},
        {d: shifted(m, mh, d, lane) for d in (-2, -1, 0, 1, 2)},
    )


def level_coefficients(m):
    inner = lax.broadcasted_iota(jnp.int32, (K, W), 0) < K - 1
    after = jnp.where(inner, vertical_mix * m * pltpu.roll(m, K - 1, 0), 0.0)
    before = pltpu.roll(after, 1, 0)
    return after, before, 1.0 - after - before


def levels_of(masks):
    inner = lax.broadcasted_iota(jnp.int32, (K, W), 0) < K - 1
    for i in range(0, len(masks), 4):
        some = masks[i : i + 4]
        nexts = [pltpu.roll(m, K - 1, 0) for m in some]
        after = [jnp.where(inner, vertical_mix * m * n, 0.0) for m, n in zip(some, nexts)]
        before = [pltpu.roll(a, 1, 0) for a in after]
        for a, b in zip(after, before):
            yield a, b, 1.0 - a - b


def chunk(q):
    return pl.ds(8 * q, 8)


def strided(q, j, stride, shift=0):
    return pl.ds((8 * q + 1 + shift) * stride + j, 8, stride=stride)


def pipeline(items, issue, finish, depth=1):
    pending = []
    for item in items:
        pending.append((item, issue(item)))
        if len(pending) > depth:
            finish(*pending.pop(0))
    for late in pending:
        finish(*late)


def step_rows(jobs):
    lane = lanes()[:8]

    def issue(item):
        job, q = item
        if q == 0 and "ahead" in job:
            job["ahead"]()
        if "x" not in job:
            return None
        halo = job["x"][1]
        rolled = []
        for f in range(4):
            c, h = job["load"](f, 0, q), halo(f, q)
            rolled.append([shifted(c, h, d, lane) for d in (-2, -1, 1, 2)])
        return rolled

    def finish(item, rolled):
        job, q = item
        x, y, z = job.get("x"), job.get("y"), job.get("z")
        load, part = job["load"], chunk(q)
        centre = None
        for term in (x and x[0].at[8], y and y.at[8], z and z[0].at[2]):
            if term is not None:
                centre = term[part] if centre is None else centre + term[part]
        if z:
            after, before = z[0].at[0][part], z[0].at[1][part]
        totals = []
        for f in range(4):
            total = centre * load(f, 0, q)
            if "base" in job:
                total += job["base"](f, q)
            if z:
                c_after, c_before = z[1](f, q)
                total += after * c_after + before * c_before
            totals.append(total)
        for coefficients_at, values in (
            (y, lambda f, i: load(f, (-2, -1, 1, 2)[i], q)),
            (x and x[0], lambda f, i: rolled[f][i]),
        ):
            if coefficients_at is None:
                continue
            for i in range(4):
                for direction in (0, 1):
                    coefficient = coefficients_at.at[4 * direction + i][part]
                    for f in (2 * direction, 2 * direction + 1):
                        totals[f] += coefficient * values(f, i)
        for f in range(4):
            job["store"](f, q, totals[f])

    pipeline([(job, q) for job in jobs for q in range(K // 8)], issue, finish)


def halo_columns(merged, j):
    return turn(merged, -HALO - G * j)


def edge_faces(edges):
    opened = edges[M] * turn(edges[M], -1)
    return scaled(edges[U], opened), opened


def edge_columns_and_levels(edges, s, opened):
    m = edges[M]
    xs = face_coefficients(
        {d: turn(s, -d) if d else s for d in (-2, -1, 0, 1)}, {-1: turn(opened, 1), 0: opened}
    )
    after, before, centre = level_coefficients(m)
    results = []
    for f in range(4):
        c = edges[f]
        total = (centre + xs[8]) * c
        total += after * pltpu.roll(c, K - 1, 0) + before * pltpu.roll(c, 1, 0)
        for coefficient, d in zip(xs[4 * (f // 2) :], (-2, -1, 1, 2)):
            total += coefficient * turn(c, -d)
        results.append(total)
    return results


def edge_rows(merged, beyond):
    lane = lanes()
    v, m = merged[V], merged[M]
    vh, mh = beyond(V), beyond(M)
    ys = coefficients(
        {d: shifted(v, vh, d, lane, G) for d in (-2, -1, 0, 1)},
        {d: shifted(m, mh, d, lane, G) for d in (-2, -1, 0, 1, 2)},
    )
    results = []
    for f in range(4):
        c, ch = merged[f], beyond(f)
        total = ys[8] * c
        for coefficient, d in zip(ys[4 * (f // 2) :], (-2, -1, 1, 2)):
            total += coefficient * shifted(c, ch, d, lane, G)
        results.append(total)
    return results


def y_coefficients(low, high, load, emit):
    for q in range(K // 8):
        w = {}
        for j in range(low - 2, high + 2):
            opened = load(M, j, q) * load(M, j + 1, q)
            s = scaled(load(V, j, q), opened)
            a = jnp.abs(s)
            even, odd = 7.0 * s, 3.0 * a + horizontal_mix * opened
            w[j] = (-(s + a), even + odd, even - odd, a - s)
            if j > low:
                at = [w[j - 3], w[j - 2], w[j - 1], w[j]]
                forward = [at[1][0], at[1][1] - at[2][0], at[1][3] - at[2][2], -at[2][3]]
                transposed = [-at[0][3], at[0][3] - at[1][2], at[2][1] - at[3][0], at[3][0]]
                emit(j - 1, q, forward + transposed + [at[1][2] - at[2][1]])


def raw_levels(raw, j):
    return lambda f, q: (raw.at[f][strided(q, j, R, 1), :], raw.at[f][strided(q, j, R, -1), :])


TALL = K + 16


def moved_chunk(q, shift=0):
    return pl.ds(8 + 8 * q + shift, 8)


def clear_ends(ref):
    ref[pl.ds(0, 8)] = jnp.zeros((8, W), F32)
    ref[pl.ds(8 + K, 8)] = jnp.zeros((8, W), F32)


def moved_levels(row):
    return lambda f, q: (row(f)[moved_chunk(q, 1)], row(f)[moved_chunk(q, -1)])


def rolled_levels(load, fields):
    after = {f: pltpu.roll(load(f), K - 1, 0) for f in fields}
    before = {f: pltpu.roll(load(f), 1, 0) for f in fields}
    return lambda f, q: (after[f][8 * q : 8 * q + 8], before[f][8 * q : 8 * q + 8])


def prepare(rows, raw, y_out, level_out, base_out):
    for j, got in enumerate(levels_of([rows[M, j] for j in range(R)])):
        for k in range(3):
            level_out[j, k] = got[k]

    def emit(j, q, values):
        for k in range(9):
            y_out.at[j - 2, k][chunk(q)] = values[k]

    y_coefficients(2, R - 3, lambda f, j, q: rows.at[f, j][chunk(q)], emit)

    def job(j):
        def store(f, q, value):
            base_out.at[f, j - 2][chunk(q)] = value

        return dict(
            store=store,
            load=lambda f, d, q: rows.at[f, j + d][chunk(q)],
            y=y_out.at[j - 2],
            z=(level_out.at[j], raw_levels(raw, j)),
        )

    step_rows([job(j) for j in range(2, R - 2)])


def interior(*refs):
    rows, raw, left, right, merged, y_in, level_in, base_in = refs[:8]
    x_out, c1_out, part1_out, c2_out, part2_out, edge_out, merged1, halos, faces_now = refs[8:]
    lane = lanes()
    west_half = lane % G < HALO
    for f in range(4):
        for r in range(R - 4):
            clear_ends(c1_out.at[f, r])
    faces = [edge_faces(edges) for edges in (left, right)]
    halo_s = jnp.where(west_half, faces[0][0], faces[1][0])
    halo_mixed = jnp.where(west_half, faces[0][1], right[M])

    def x_halos(j):
        if j < R:
            halos[j, 0] = halo_columns(halo_s, j)
            halos[j, 1] = halo_columns(halo_mixed, j)

    def x_faces(j):
        if j < R:
            m = rows[M, j]
            opened = m * shifted(m, halos[j, 1], 1, lane)
            faces_now[j, 0] = scaled(rows[U, j], opened)
            faces_now[j, 1] = opened

    for j in range(4):
        x_halos(j)
    for j in range(2):
        x_faces(j)

    def issue(item):
        j, q = item
        if q == 0:
            x_halos(j + 4)
            x_faces(j + 2)
        s, opened = faces_now.at[j, 0][chunk(q)], faces_now.at[j, 1][chunk(q)]
        hs, hm = halos.at[j, 0][chunk(q)], halos.at[j, 1][chunk(q)]
        return (
            {d: shifted(s, hs, d, lane[:8]) for d in (-2, -1, 0, 1)},
            {-1: shifted(opened, hm, -1, lane[:8]), 0: opened},
        )

    def finish(item, faces_here):
        j, q = item
        for i, value in enumerate(face_coefficients(*faces_here)):
            x_out.at[j, i][chunk(q)] = value

    pipeline([(j, q) for j in range(R) for q in range(K // 8)], issue, finish, 2)

    partial = [edge_columns_and_levels(e, *f) for e, f in zip((left, right), faces)]
    across = edge_rows(merged, lambda f: merged[f])
    for f in range(4):
        edge = jnp.where(west_half, partial[0][f], partial[1][f])
        edge_out[f] = edge
        merged1[f] = edge + across[f]

    def kept(j):
        return lambda f, q: halos.at[j, f][chunk(q)]

    def run(jobs, source):
        js = list(jobs)

        def keep(k):
            if k < len(js):
                for f in range(4):
                    halos[js[k], f] = halo_columns(source[f], js[k])

        keep(0)
        keep(1)
        step_rows([job | dict(ahead=lambda k=k: keep(k + 2)) for k, job in enumerate(jobs.values())])

    def first(j):
        def store(f, q, value):
            if j in ends1:
                part1_out.at[f, ends1.index(j)][chunk(q)] = value
            else:
                c1_out.at[f, j - 2][moved_chunk(q)] = value

        job = dict(
            store=store,
            load=lambda f, d, q: rows.at[f, j][chunk(q)],
            x=(x_out.at[j], kept(j)),
        )
        if j in ends1:
            return job | dict(z=(level_in.at[j], raw_levels(raw, j)))
        return job | dict(base=lambda f, q: base_in.at[f, j - 2][chunk(q)])

    ends1 = (0, 1, R - 2, R - 1)
    run({j: first(j) for j in range(R)}, merged)

    def second(j):
        def store(f, q, value):
            if j in ends2:
                part2_out.at[f, ends2.index(j)][chunk(q)] = value
            else:
                c2_out.at[f, j - 4][chunk(q)] = value

        job = dict(
            store=store,
            load=lambda f, d, q: c1_out.at[f, j - 2 + d][moved_chunk(q)],
            x=(x_out.at[j], kept(j)),
            z=(level_in.at[j], moved_levels(lambda f: c1_out.at[f, j - 2])),
        )
        return job if j in ends2 else job | dict(y=y_in.at[j - 2])

    ends2 = (2, 3, R - 4, R - 3)
    run({j: second(j) for j in range(2, R - 2)}, merged1)


def boundary(*refs):
    rows, merged, y_in, level_in, x_in, c1_in, part1_in, c2_in, part2_in, edge_in = refs[:10]
    second, first, second_corners, first_corners = refs[10:14]
    outs = refs[14:18]
    sides, corners, x_new, y_new, level_new, c1_new, merged1, beyond, halos, halos_x = refs[18:]
    lane = lanes()
    place = lax.axis_index("ns")
    last = lax.axis_size("ns") - 1
    odd = place % 2
    inside = {SOUTH: place > 0, NORTH: place < last}
    near = (-2, -1, 0, 1, R - 2, R - 1, R, R + 1)
    new_at = {j: i for i, j in enumerate(near)}
    for message, side in ((second, odd), (first, 1 - odd)):
        here = jnp.where(side == NORTH, place < last, place > 0)
        for b in range(SIDE_BLOCKS):
            sides[side, b] = jnp.where(here, message[b], 0.0)
    for message, side in ((second_corners, odd), (first_corners, 1 - odd)):
        here = jnp.where(side == NORTH, place < last, place > 0)
        corners[side] = jnp.where(here, message[...], 0.0)

    def row(f, j):
        if j < 0:
            return sides.at[SOUTH, ROWS_AT[f] + j + (2 if f == U else HALO)]
        if j >= R:
            return sides.at[NORTH, ROWS_AT[f] + j - R]
        return rows.at[f, j]

    for f in range(FIELDS):
        south = turn(corners[SOUTH], W - 2 * G - 2 * G * f)
        north = turn(corners[NORTH], -2 * G * f)
        beyond[f] = jnp.where(lane >= W // 2, south, north)
    for f in range(4):
        for i in range(2, 6):
            clear_ends(c1_new.at[f, i])

    for f, across in enumerate(edge_rows(merged, lambda f: beyond[f])):
        merged1[f] = edge_in[f] + across

    def halo_beyond(f, j):
        return halo_columns(beyond[f], j % R)

    def emit(j, q, values):
        for k in range(9):
            y_new.at[new_at[j], k][chunk(q)] = values[k]

    for low in (-2, R - 2):
        y_coefficients(low, low + 3, lambda f, j, q: row(f, j)[chunk(q)], emit)

    out_rows = [j for j in near if not 0 <= j < R]
    for i, j in enumerate(out_rows):
        for k, f in enumerate((U, M)):
            halos_x[i, k] = halo_beyond(f, j)
    for f in range(4):
        for i, j in enumerate(out_rows):
            halos[i, f] = halo_beyond(f, j)

    def issue(item):
        i, q = item
        u, m = (row(f, out_rows[i])[chunk(q)] for f in (U, M))
        uh, mh = (halos_x.at[i, k][chunk(q)] for k in range(2))
        return (
            {d: shifted(u, uh, d, lane[:8]) for d in (-2, -1, 0, 1)},
            {d: shifted(m, mh, d, lane[:8]) for d in (-2, -1, 0, 1, 2)},
        )

    def finish(item, got):
        i, q = item
        for k, value in enumerate(coefficients(*got)):
            x_new.at[new_at[out_rows[i]], k][chunk(q)] = value

    pipeline([(i, q) for i in range(4) for q in range(K // 8)], issue, finish)
    for j, got in zip(out_rows, levels_of([row(M, j)[...] for j in out_rows])):
        for k in range(3):
            level_new[new_at[j], k] = got[k]

    def kept(k):
        return lambda f, q: halos.at[k, f][chunk(q)]

    def first_job(j):
        side = SOUTH if j < R // 2 else NORTH

        def store(f, q, value):
            if f >= 2 and not 0 <= j < R:
                value = jnp.where(inside[side], value, 0.0)
            c1_new.at[f, new_at[j]][moved_chunk(q)] = value

        job = dict(
            store=store, load=lambda f, d, q: row(f, j + d)[chunk(q)], y=y_new.at[new_at[j]]
        )
        if 0 <= j < R:
            i = (0, 1, R - 2, R - 1).index(j)
            return job | dict(base=lambda f, q: part1_in.at[f, i][chunk(q)])
        return job | dict(
            x=(x_new.at[new_at[j]], kept(out_rows.index(j))),
            z=(level_new.at[new_at[j]], rolled_levels(lambda f: row(f, j)[...], range(4))),
        )

    step_rows([first_job(j) for j in (-2, 0, -1, 1, R, R - 2, R + 1, R - 1)])

    def load1(f, j, q):
        if j in new_at:
            return c1_new.at[f, new_at[j]][moved_chunk(q)]
        return c1_in.at[f, j - 2][moved_chunk(q)]

    ends = (0, 1, R - 2, R - 1)
    for f in range(4):
        for i, j in enumerate(ends):
            halos[i, f] = halo_columns(merged1[f], j)

    def second_job(j):
        def store(f, q, value):
            outs[f][pl.ds(8 * q * R + j, 8, stride=R), :] = value

        job = dict(store=store, load=lambda f, d, q: load1(f, j + d, q))
        if j in ends:
            return job | dict(
                x=(x_in.at[j], kept(ends.index(j))),
                y=y_new.at[new_at[j]],
                z=(level_in.at[j], moved_levels(lambda f: c1_new.at[f, new_at[j]])),
            )
        i = (2, 3, R - 4, R - 3).index(j)
        return job | dict(y=y_in.at[j - 2], base=lambda f, q: part2_in.at[f, i][chunk(q)])

    step_rows([second_job(j) for j in (0, 2, 1, 3, R - 2, R - 4, R - 1, R - 3)])

    for j in range(4, R - 4):
        for f in range(4):
            outs[f][pl.ds(j, K, stride=R), :] = c2_in[f, j - 4]


def vmem():
    return pl.BlockSpec(memory_space=pltpu.VMEM)


def call(kernel, in_specs, out_shapes, scratch=(), limit=16 * MIB, cost=0.1):
    return pl.pallas_call(
        kernel,
        out_shape=[jax.ShapeDtypeStruct(shape, F32) for shape in out_shapes],
        in_specs=in_specs,
        out_specs=[vmem()] * len(out_shapes),
        scratch_shapes=list(scratch),
        compiler_params=pltpu.CompilerParams(vmem_limit_bytes=limit),
        cost_estimate=pl.CostEstimate(flops=int(cost * FLOPS_PER_US), bytes_accessed=MIB, transcendentals=0),
    )


def partners(odd, n_ew, n_ns):
    pairs = []
    for e in range(n_ew):
        for s in range(n_ns):
            step = 1 if (s - odd) % 2 == 0 else -1
            if 0 <= s + step < n_ns:
                to = (e, s + step)
            else:
                to = (e ^ 1 if e ^ 1 < n_ew else e, s)
            pairs.append((e * n_ns + s, to[0] * n_ns + to[1]))
    return pairs


def local(temp, salt, u_east, v_north, wet, cot_temp, cot_salt):
    flat = [a.reshape(K * R, W) for a in (temp, salt, cot_temp, cot_salt, u_east, v_north, wet)]

    row = (K, W)
    padded = ((K + 2) * R, W)
    rows, raw, own, to_east, to_west = call(
        pack_edges,
        [pl.BlockSpec(memory_space=pltpu.HBM)] * FIELDS,
        [(FIELDS, R) + row, (4,) + padded, (FIELDS,) + row, (EDGE_ROWS, W), (EDGE_ROWS, W)],
        [
            pltpu.VMEM((2, K * R, W), F32),
            pltpu.VMEM((K * R, W), jnp.int32),
            pltpu.SemaphoreType.DMA((FIELDS,)),
        ],
        cost=2.2,
    )(*[pltpu.with_memory_space_constraint(a, pltpu.HBM) for a in flat])

    n_ew, n_ns = lax.axis_size("ew"), lax.axis_size("ns")
    from_west = lax.ppermute(to_east, "ew", [(i, (i + 1) % n_ew) for i in range(n_ew)])
    from_east = lax.ppermute(to_west, "ew", [((i + 1) % n_ew, i) for i in range(n_ew)])

    def swap(odd, message):
        return lax.ppermute(message, ("ew", "ns"), partners(odd, n_ew, n_ns))

    second, first = call(pack_sides, [vmem()], [(SIDE_BLOCKS,) + row] * 2, cost=0.1)(rows)
    second = swap(1, second)
    first = swap(0, first)

    y_in, level, base = call(
        prepare,
        [vmem()] * 2,
        [(R - 4, 9) + row, (R, 3) + row, (4, R - 4) + row],
        cost=1.7,
    )(rows, raw)

    left, right, merged, second_corners, first_corners = call(
        pack_corners,
        [vmem()] * 3 + [pl.BlockSpec(memory_space=pl.ANY)],
        [(FIELDS,) + row] * 3 + [row] * 2,
        cost=0.2,
    )(own, from_west, from_east, level)
    second_corners = swap(1, second_corners)
    first_corners = swap(0, first_corners)

    x_in, c1, part1, c2, part2, edge = call(
        interior,
        [vmem()] * 8,
        [(R, 9) + row, (4, R - 4, TALL, W), (4, 4) + row, (4, R - 8) + row, (4, 4) + row, (4,) + row],
        [
            pltpu.VMEM((4,) + row, F32),
            pltpu.VMEM((R, 4) + row, F32),
            pltpu.VMEM((R, 2) + row, F32),
        ],
        cost=4.7,
    )(rows, raw, left, right, merged, y_in, level, base)

    outs = call(
        boundary,
        [vmem()] * 14,
        [(K * R, W)] * 4,
        [
            pltpu.VMEM((2, SIDE_BLOCKS) + row, F32),
            pltpu.VMEM((2,) + row, F32),
            pltpu.VMEM((8, 9) + row, F32),
            pltpu.VMEM((8, 9) + row, F32),
            pltpu.VMEM((8, 3) + row, F32),
            pltpu.VMEM((4, 8, TALL, W), F32),
            pltpu.VMEM((4,) + row, F32),
            pltpu.VMEM((FIELDS,) + row, F32),
            pltpu.VMEM((4, 4) + row, F32),
            pltpu.VMEM((4, 2) + row, F32),
        ],
        cost=2.9,
    )(
        *(rows, merged, y_in, level, x_in, c1, part1, c2, part2, edge),
        *(second, first, second_corners, first_corners),
    )
    return tuple(a.reshape(K, R, W) for a in outs)


def solution(mesh):
    spec = P(None, "ns", "ew")
    return jax.shard_map(
        local, mesh=mesh, in_specs=(spec,) * 7, out_specs=(spec,) * 4, check_vma=False
    )
```
